512 devices in a mesh: grp: 2 (over y_lo), slab: 64 (over y_hi, z, core), col: 4 (over x).
Axes of the slice: x: 4, y: 8 (y_hi: 4, y_lo: 2; y = y_hi * 2 + y_lo), z: 8, core: 2. Of those that a mesh axis runs over, the one named last changes fastest.
Arguments:
- heat_field: float32 [2, 32, 1024, 512], P('grp', None, 'slab', 'col'), may hold values from -6 to 6
- coeff: float32 [2, 32, 1024, 512], P('grp', None, 'slab', 'col'), may hold values from 0.2 to 1
- order: float32 [2, 2, 32, 1024, 512], P('grp', None, None, 'slab', 'col'), may hold values from 0.5 to 1
- block_owner: int32 [4, 64, 64, 1], P('col'), may hold values from 0 to 63; in each aligned block of 64 rows (0 to 63, 64 to 127, ..., all dimensions but the last counted through in order) at most 2 rows name the same one
- block_source: int32 [4, 64, 64], P('col'), may hold values from 0 to 255
- laser_cells: int32 [64, 4, 32], P('slab', 'col'), may hold values from 0 to 2047
Outputs:
- ending_warmth_pair: float32 [2, 32, 1024, 512], P('grp', None, 'slab', 'col')
- joined_solver_outputs: float32 [2, 2, 32, 1024, 512], P('grp', None, None, 'slab', 'col')
The draws below stay inside these ranges and needn't reach their ends.
Inputs may be any that keep to these rules, and one draw needn't show every extreme that they name: `block_owner`: within the 64 units of one window device no owner slab is named more than 2 times; some window device names one owner exactly 2 times in every draw. `block_source`: several window units may read the same plate unit. `laser_cells`: A cell may repeat; each entry adds its heat.
All inputs are finite; a program needn't handle non-finite values.
Results may differ from the reference program's by a relative error of at most 0.0003.
Values sent between devices are 32-bit elements; how exact they have to be, the bound alone decides.
No kernel may reach another device: no remote copies, remote signals or barrier semaphores. Data moves between devices by JAX's collectives and lax.ppermute only.
A program may use at most 64 MiB of HBM per device.

```python
import math
import jax
import jax.numpy as jnp
import numpy as np
from jax import lax

PZ = 32
ZQ = 4
CX = 16
CY = 128
LASER = 32
WU = 64
PU = 256
CAP = 2
NX = 1024
NY = 512
N_SLAB = 64
N_COL = 4


def touch_ends(values, key, smallest, high):
    longest = values.shape.index(max(values.shape))
    spots = []
    for shift in (0, 1):
        where = [jax.random.randint(jax.random.fold_in(key, axis), (), 0, length) for axis, length in enumerate(values.shape)]
        where[longest] = (where[longest] + shift) % values.shape[longest]
        spots.append(tuple(where))
    return values.at[spots[0]].set(smallest).at[spots[1]].set(high)


def levels(own_key, extent, cuts, low, top_value):
    def one(axis_at, parts):
        draws = jax.random.uniform(jax.random.fold_in(jax.random.fold_in(own_key, 6), axis_at), (parts,), jnp.float32, low / len(cuts), top_value / len(cuts))
        return jnp.repeat(jnp.exp(draws), extent[axis_at] // parts).reshape((-1,) + (1,) * (len(extent) - axis_at - 1))

    gain = one(*cuts[0])
    for cut in cuts[1:]:
        gain = gain * one(*cut)
    return gain


def deal_out(rng, own, number, rows, amount, top, reach, skew):
    ranking = jax.random.permutation(rng, amount)
    heavy_load, common = shares(amount, rows * top, reach, skew, True), shares(amount, rows * top, reach, skew, False)
    places = jnp.arange(amount)

    def named(lengths, rotation):
        used = int((lengths > 0).sum())
        fixed = max(1, used // 4)
        shifted = fixed + (places - fixed + rotation * (used - fixed)) % max(1, amount - fixed)
        return jnp.zeros((amount,), jnp.int32).at[ranking[jnp.where(places < fixed, places, shifted)]].set(jnp.asarray(lengths, jnp.int32))

    lengths = jnp.where(number % 4 == 0, named(heavy_load, number // 4), named(common, number - number // 4 - 1))
    mixed = jax.random.permutation(jax.random.fold_in(own, 3), amount)
    source_of, taker = mixed[0:amount // 2 * 2:2], mixed[1:amount // 2 * 2:2]
    margin = jnp.minimum(lengths[source_of] - 1, reach - lengths[taker]) // 2
    margin = jnp.where((source_of == ranking[0]) | (taker == ranking[0]) | (lengths[taker] == 0), 0, jnp.maximum(margin, 0))
    shifted = jax.random.randint(jax.random.fold_in(own, 4), (amount // 2,), 0, 1 << 20) % (margin + 1)
    lengths = lengths.at[source_of].add(-shifted).at[taker].add(shifted)
    members = jnp.searchsorted(jnp.cumsum(lengths), jnp.arange(rows * top), side="right").astype(jnp.int32)
    table = members.reshape(top, rows).T
    table = table[jax.random.permutation(jax.random.fold_in(own, 1), rows)]
    rotation = jax.random.randint(jax.random.fold_in(own, 2), (rows, 1), 0, top)
    return jnp.take_along_axis(table, (jnp.arange(top)[None, :] + rotation) % top, axis=1)


def shares(count, total, bound, lean, full):
    loads = [(1 << 20) // math.isqrt(standing ** lean) + 1 for standing in range(1, count + 1)]
    largest = bound if full else min(bound, max(-(-total // count), total * loads[0] // sum(loads)))
    least = 1 if total - largest >= count - 1 else 0
    holding, spare = [largest] + [least] * (count - 1), total - largest - least * (count - 1)
    while spare > 0:
        movable = [i for i in range(1, count) if holding[i] < largest] or [i for i in range(1, count) if holding[i] < bound]
        whole, left = sum([loads[i] for i in movable]), spare
        for i in movable:
            extra = min(bound - holding[i], max(1, left * loads[i] // whole), spare)
            holding[i] = holding[i] + extra
            spare = spare - extra
    return np.array(holding)


def gaussian(key, shape, scale, limit, cuts=(), kind=jnp.bfloat16):
    array = scale * jax.random.normal(key, shape, jnp.float32)
    if cuts:
        array = array * levels(key, shape, cuts, -0.22, 0.18)
    return jnp.clip(array, -limit, limit).astype(kind)


def setup_inputs(seed: int = 0) -> dict:
    arg_keys = jax.random.split(jax.random.key(seed), 7)
    heat_field = gaussian(arg_keys[0], (2, PZ, NX, NY), 1.0, 6.0, ((0, 2), (2, 64), (3, 4)), jnp.float32)
    coeff = jnp.clip(jnp.exp(math.log(1.0) - 1.609438 * jax.random.uniform(arg_keys[1], (2, PZ, NX, NY), jnp.float32) ** levels(arg_keys[1], (2, PZ, NX, NY), ((0, 2), (2, 64), (3, 4)), -0.2, 0.2)), 0.2, 1.0)
    order = jnp.clip(0.5 + 0.5 * jax.random.uniform(arg_keys[2], (2, 2, PZ, NX, NY), jnp.float32) ** levels(arg_keys[2], (2, 2, PZ, NX, NY), ((0, 2), (3, 64), (4, 4)), -0.2, 0.2), 0.5, 1.0)
    block_owner_keys = jax.random.split(jax.random.fold_in(arg_keys[3], 1), N_COL * N_SLAB * WU // WU)
    block_owner_turns = jax.random.permutation(jax.random.fold_in(arg_keys[3], 3), N_COL * N_SLAB * WU // WU)
    block_owner = jax.vmap(lambda own, number: deal_out(jax.random.fold_in(arg_keys[3], 2), own, number, WU, N_SLAB, 1, CAP, 2))(block_owner_keys, block_owner_turns).reshape((N_COL, N_SLAB, WU, 1))
    block_source = touch_ends(jax.random.randint(arg_keys[4], (N_COL, N_SLAB, WU), 0, PU), jax.random.fold_in(arg_keys[4], 1), 0, PU - 1).astype(jnp.int32)
    laser_cells = touch_ends(jax.random.randint(arg_keys[5], (N_SLAB, N_COL, LASER), 0, CX * CY), jax.random.fold_in(arg_keys[5], 1), 0, (CX * CY) - 1).astype(jnp.int32)
    return {"heat_field": heat_field, "coeff": coeff, "order": order, "block_owner": block_owner, "block_source": block_source, "laser_cells": laser_cells}


heat_dt = 0.07
phase_dt = 0.1
laser_power = 3.0
liquefying_threshold = 0.3
freezing_line_gradient = 0.5
solute_reject = 0.5
STENCIL_SHIFTS = ((0, 1, 1), (2, 1, 1), (1, 0, 1), (1, 2, 1), (1, 1, 0), (1, 1, 2))
PHASE_WEIGHTS = (1.0, 1.0, 1.3, 1.3, 0.7, 0.7)
SOLUTE_WEIGHTS = (0.8, 0.8, 0.8, 0.8, 0.8, 0.8)


def harmonic(center, beside):
    return 2.0 * center * beside / (center + beside)


def conduction(temp_pad, cond_pad):
    vertical_cell_count = temp_pad.shape[0] - 2
    row_count = temp_pad.shape[1] - 2
    col_count = temp_pad.shape[2] - 2
    center = temp_pad[1:-1, 1:-1, 1:-1]
    cond_mid = cond_pad[1:-1, 1:-1, 1:-1]
    summed = jnp.zeros_like(center)
    for along_z, along_x, along_y in STENCIL_SHIFTS:
        neighbour = temp_pad[along_z:along_z + vertical_cell_count, along_x:along_x + row_count, along_y:along_y + col_count]
        cond_next = cond_pad[along_z:along_z + vertical_cell_count, along_x:along_x + row_count, along_y:along_y + col_count]
        summed = summed + harmonic(cond_mid, cond_next) * (neighbour - center)
    return summed


def anisotropic(field_pad, weights):
    vertical_cell_count = field_pad.shape[0] - 2
    row_count = field_pad.shape[1] - 2
    col_count = field_pad.shape[2] - 2
    center = field_pad[1:-1, 1:-1, 1:-1]
    summed = jnp.zeros_like(center)
    for (along_z, along_x, along_y), weight in zip(STENCIL_SHIFTS, weights):
        neighbour = field_pad[along_z:along_z + vertical_cell_count, along_x:along_x + row_count, along_y:along_y + col_count]
        summed = summed + weight * (neighbour - center)
    return summed


def heat_step(temp_pad, cond_pad, temp, source, thermal_heat_capacity, loss):
    return temp + heat_dt * ((conduction(temp_pad, cond_pad) + source) / thermal_heat_capacity - loss * temp)


def order_variable_update(bordered_order_variable, bordered_concentration, patch_warmth, response_measure):
    order_variable = bordered_order_variable[1:-1, 1:-1, 1:-1]
    dissolved_concentration = bordered_concentration[1:-1, 1:-1, 1:-1]
    forcing_term = 0.45 * jnp.tanh(response_measure * (liquefying_threshold - patch_warmth - freezing_line_gradient * dissolved_concentration))
    updated_order_variable = order_variable + phase_dt * (anisotropic(bordered_order_variable, PHASE_WEIGHTS) + 4.0 * order_variable * (1.0 - order_variable) * (order_variable - 0.5 + forcing_term))
    updated_concentration = dissolved_concentration + phase_dt * anisotropic(bordered_concentration, SOLUTE_WEIGHTS) - solute_reject * (updated_order_variable - order_variable) * dissolved_concentration
    return updated_order_variable, updated_concentration


def refine_table(half_cols):
    source = jnp.arange(half_cols)[:, None]
    target = jnp.arange(2 * half_cols)[None, :]
    parent = target // 2
    parity = target % 2
    beside = jnp.clip(parent - 1 + 2 * parity, 0, half_cols - 1)
    return 0.75 * (source == parent).astype(jnp.float32) + 0.25 * (source == beside).astype(jnp.float32)


def upsample_finer(coarse):
    table = refine_table(coarse.shape[-1])
    finer = jnp.dot(coarse, table, precision=lax.Precision.HIGHEST, preferred_element_type=jnp.float32)
    return jnp.broadcast_to(finer[..., None, :], finer.shape[:-1] + (2, finer.shape[-1]))


def coarsen(fine):
    split = fine.reshape(fine.shape[:-1] + (fine.shape[-1] // 2, 2))
    return 0.25 * jnp.sum(split, axis=(-3, -1))


def plate_cut(block):
    return block.reshape(PZ // ZQ, ZQ, CX, 2, CY // 2).transpose(0, 2, 3, 1, 4).reshape((PZ // ZQ) * CX * 2, ZQ, CY // 2)


def plate_join(units):
    return units.reshape(PZ // ZQ, CX, 2, ZQ, CY // 2).transpose(0, 3, 1, 2, 4).reshape(PZ, CX, CY)


def window_cut(block):
    return block.reshape(PZ // ZQ, ZQ, CX // 2, 2, CY).transpose(0, 2, 1, 3, 4).reshape((PZ // ZQ) * (CX // 2), ZQ, 2, CY)


def patch_assembly(units):
    return units.reshape(PZ // ZQ, CX // 2, ZQ, 2, CY).transpose(0, 2, 1, 3, 4).reshape(PZ, CX, CY)


def blocks(field):
    return field.reshape(PZ, N_SLAB, CX, N_COL, CY).transpose(3, 1, 0, 2, 4)


def releases_waiting(pieces):
    return pieces.transpose(2, 1, 3, 0, 4).reshape(PZ, NX, NY)


def reference(heat_field, coeff, order, block_owner, block_source, laser_cells):
    plate = heat_field[0]
    latent_prev = heat_field[1]
    conduct = coeff[0]
    response_measure = coeff[1]
    thermal_heat_capacity = order[0, 0]
    loss = order[0, 1]
    order_variable = order[1, 0]
    dissolved_concentration = order[1, 1]
    owners = block_owner[..., 0]
    col_index = jnp.arange(N_COL)[:, None, None]
    plate_units = jax.vmap(jax.vmap(plate_cut))(blocks(plate))
    averaged_down_input = plate_units[col_index, owners, block_source]
    patch_warmth = releases_waiting(jax.vmap(jax.vmap(patch_assembly))(upsample_finer(averaged_down_input)))
    latent_units = coarsen(jax.vmap(jax.vmap(window_cut))(blocks(latent_prev)))
    received = jnp.zeros(plate_units.shape, jnp.float32).at[col_index, owners, block_source].add(latent_units)
    latent_heat = releases_waiting(jax.vmap(jax.vmap(plate_join))(received))
    current_slab_index = jnp.arange(N_SLAB)[:, None, None]
    col_inner = jnp.arange(N_COL)[None, :, None]
    deposit = jnp.zeros((N_SLAB, N_COL, CX * CY), jnp.float32).at[current_slab_index, col_inner, laser_cells].add(laser_power)
    top_layer = deposit.reshape(N_SLAB, N_COL, CX, CY).transpose(0, 2, 1, 3).reshape(NX, NY)
    laser_field = jnp.concatenate([top_layer[None], jnp.zeros((PZ - 1, NX, NY), jnp.float32)], 0)
    source = laser_field + latent_heat
    cond_pad = jnp.pad(conduct, 1)
    first = heat_step(jnp.pad(plate, 1), cond_pad, plate, source, thermal_heat_capacity, loss)
    second_partial_update = heat_step(jnp.pad(first, 1), cond_pad, first, source, thermal_heat_capacity, loss)
    updated_order_variable, updated_concentration = order_variable_update(jnp.pad(order_variable, 1), jnp.pad(dissolved_concentration, 1), patch_warmth, response_measure)
    ending_warmth_pair = jnp.stack([second_partial_update, patch_warmth])
    joined_solver_outputs = jnp.stack([jnp.stack([latent_heat, first]), jnp.stack([updated_order_variable, updated_concentration])])
    return ending_warmth_pair, joined_solver_outputs
```

```python
import functools

import jax
import jax.numpy as jnp
from jax import lax
from jax.experimental import pallas as pl
from jax.experimental.pallas import tpu as pltpu
from jax.sharding import PartitionSpec as P

PZ = 32
ZQ = 4
CX = 16
CY = 128
HALF = CY // 2

heat_dt = 0.07
phase_dt = 0.1
laser_power = 3.0
liquefying_threshold = 0.3
freezing_line_gradient = 0.5
solute_reject = 0.5
PHASE_WEIGHTS = (1.0, 1.3, 0.7)
SOLUTE_WEIGHTS = (0.8, 0.8, 0.8)

F32 = jnp.float32
BF16 = jnp.bfloat16
BIG = 1 << 20


def iota(shape, dim):
    return lax.broadcasted_iota(jnp.int32, shape, dim)


def ones_where(mask):
    return jnp.where(mask, 1.0, 0.0).astype(BF16)


def two_parts(x):
    high = x.astype(BF16)
    return high, (x - high.astype(F32)).astype(BF16)


def dot(a, b, dims=((1,), (0,))):
    return lax.dot_general(a, b, (dims, ((), ())), preferred_element_type=F32)


def pick_left(table, x, dims=((1,), (0,))):
    width = x.shape[1]
    both = dot(table, jnp.concatenate(two_parts(x), axis=1), dims)
    return both[:, :width] + both[:, width:]


def pick_right(x, table, dims=((1,), (0,))):
    high, low = two_parts(x)
    return dot(high, table, dims) + dot(low, table, dims)


def plate_table(owners, sources, slab):
    count = owners.shape[0] // 2
    rows = []
    for parity in (0, 1):
        own = owners[pl.ds(parity, count, stride=2), :]
        src = sources[pl.ds(parity, count, stride=2), :]
        key = iota(own.shape, 1) * 256 + src
        mine = own == slab
        first = jnp.min(jnp.where(mine, key, BIG).astype(F32), axis=1, keepdims=True)
        last = jnp.max(jnp.where(mine, key, -1).astype(F32), axis=1, keepdims=True)
        first, last = first.astype(jnp.int32), last.astype(jnp.int32)
        for value, valid in ((first, first < BIG), (last, last > first)):
            unit = value & 255
            place = jnp.where(valid, (unit & 1) * 128 + (unit >> 1), -1)
            rows.append(ones_where(iota((count, 256), 1) == place))
    return jnp.concatenate(rows, axis=0)


def window_table(owners, slab):
    count = owners.shape[0] // 2
    own = owners[pl.ds(slab, 1), :]
    units = own.shape[1]
    unit = iota((count, units), 1)
    rows = []
    for parity in (0, 1):
        mine = jnp.broadcast_to(own, (count, units)) == iota((count, units), 0) * 2 + parity
        first = jnp.min(jnp.where(mine, unit, BIG).astype(F32), axis=1, keepdims=True)
        last = jnp.max(jnp.where(mine, unit, -1).astype(F32), axis=1, keepdims=True)
        first, last = first.astype(jnp.int32), last.astype(jnp.int32)
        rows.append(ones_where(unit == first))
        rows.append(ones_where((unit == last) & (last > first)))
    spread = ones_where((iota((units, 2 * units), 1) >> 1) == iota((units, 2 * units), 0))
    return dot(jnp.concatenate(rows, axis=0), spread).astype(BF16)


def pack_kernel(ids, owners, sources, heat, out):
    grp, slab = ids[0], ids[1]
    count = owners.shape[0] // 2
    lane = iota((CY, CY), 1)

    def store(result, pair):
        for block in range(4):
            out[:, block * 2 + pair, :] = result[block * count : (block + 1) * count]

    @pl.when(grp == 0)
    def _():
        table = plate_table(owners, sources, slab)
        for pair in (0, 1):
            even = heat[:, 2 * pair].reshape(CY, CY)
            odd = heat[:, 2 * pair + 1].reshape(CY, CY)
            left = jnp.where(lane < HALF, even, pltpu.roll(odd, HALF, 1))
            right = jnp.where(lane < HALF, pltpu.roll(even, HALF, 1), odd)
            store(pick_left(table, jnp.concatenate([left, right], axis=0)), pair)

    @pl.when(grp == 1)
    def _():
        table = window_table(owners, slab)
        row = iota((2 * CY, CY), 0)
        col = iota((2 * CY, CY), 1)
        mean = jnp.where((row >> 1) == col, 0.25, 0.0).astype(BF16)
        for pair in (0, 1):
            even = heat[:, 2 * pair].reshape(CY, CY)
            odd = heat[:, 2 * pair + 1].reshape(CY, CY)
            means = pick_right(jnp.concatenate([even, odd], axis=1), mean)
            store(pick_left(table, means), pair)


def edge_columns(x, first_row):
    row, lane = iota((8, CY), 0), iota((8, CY), 1)
    pick = ((row == first_row) & (lane == 0)) | ((row == first_row + 1) & (lane == CY - 1))
    high, low = two_parts(x)
    dims = ((1,), (1,))
    return dot(ones_where(pick), high, dims) + dot(ones_where(pick), low, dims)


def send_edges(x, parity, near, far, part):
    top, bottom = x[:, 0, :], x[:, CX - 1, :]
    near[part] = jnp.where(parity == 0, bottom, top)
    far[part] = jnp.where(parity == 0, top, bottom)


def edges_kernel(ids, heat, coeff, order, near, far, sides):
    grp, parity = ids[0], ids[1] & 1

    def send(fields):
        total = jnp.zeros((8, PZ * CX), F32)
        for part, field in enumerate(fields):
            send_edges(field, parity, near, far, part)
            total = total + edge_columns(field[...].reshape(PZ * CX, CY), 2 * part)
        sides[...] = total

    @pl.when(grp == 0)
    def _():
        send((heat, coeff))

    @pl.when(grp == 1)
    def _():
        send((order.at[0], order.at[1]))


def receive_sides(ids, sides, part):
    col, cols = ids[2], sides.shape[0]
    left = sides[pl.ds(jnp.maximum(col - 1, 0), 1), 2 * part + 1, :]
    right = sides[pl.ds(jnp.minimum(col + 1, cols - 1), 1), 2 * part, :]
    left = jnp.where(col > 0, left, 0.0)
    right = jnp.where(col < cols - 1, right, 0.0)
    size = left.shape[1]
    row = iota((8, size), 0)
    left = jnp.broadcast_to(left, (8, size))
    right = jnp.broadcast_to(right, (8, size))
    both = jnp.where(row == 0, left, jnp.where(row == 1, right, 0.0))
    row, lane = iota((8, CY), 0), iota((8, CY), 1)
    place = ones_where(((row == 0) & (lane == 0)) | ((row == 1) & (lane == CY - 1)))
    return pick_right(both, place, ((0,), (0,)))


def receive_rows(ids, near, far, part, above, below, slabs):
    slab = ids[1]
    parity = slab & 1
    near_row = jnp.where(parity == 0, near[1, part], near[0, part])
    far_row = jnp.where(parity == 0, far[0, part], far[1, part])
    above[...] = jnp.where(slab == 0, 0.0, jnp.where(parity == 0, far_row, near_row))
    below[...] = jnp.where(slab == slabs - 1, 0.0, jnp.where(parity == 0, near_row, far_row))


def beside(v, above, below, sides):
    row, lane = iota((CX, CY), 0), iota((CX, CY), 1)
    up = jnp.where(row == 0, jnp.broadcast_to(above, (CX, CY)), pltpu.roll(v, 1, 0))
    down = jnp.where(row == CX - 1, jnp.broadcast_to(below, (CX, CY)), pltpu.roll(v, CX - 1, 0))
    left = jnp.where(lane == 0, sides, pltpu.roll(v, 1, 1))
    right = jnp.where(lane == CY - 1, sides, pltpu.roll(v, CY - 1, 1))
    return up, down, left, right


def harmonic(center, beside_it):
    return 2.0 * center * beside_it / (center + beside_it)


def heat_planes(temp, cond, order, source, result, temp_halo, cond_halo):
    temp_above, temp_below, temp_sides = temp_halo
    cond_above, cond_below, cond_sides = cond_halo

    def plane(z, from_above):
        v, k = temp[z], cond[z]
        one = pl.ds(z, 1)
        vs = beside(v, temp_above[one, :], temp_below[one, :], temp_sides[z])
        ks = beside(k, cond_above[one, :], cond_below[one, :], cond_sides[z])
        later = jnp.minimum(z + 1, PZ - 1)
        to_below = harmonic(k, cond[later]) * (temp[later] - v)
        total = to_below - from_above
        for v_next, k_next in zip(vs, ks):
            total = total + harmonic(k, k_next) * (v_next - v)
        result[z] = v + heat_dt * ((total + source(z)) / order[0, z] - order[1, z] * v)
        return to_below

    lax.fori_loop(0, PZ, plane, jnp.zeros((CX, CY), F32), unroll=4)


def phase_planes(phi, sol, response, warmth, new_phi, new_sol, phi_halo, sol_halo):
    phi_above, phi_below, phi_sides = phi_halo
    sol_above, sol_below, sol_sides = sol_halo

    def spread(field, z, halo, weights):
        above, below, sides = halo
        f = field[z]
        one = pl.ds(z, 1)
        up, down, left, right = beside(f, above[one, :], below[one, :], sides[z])
        before = jnp.where(z > 0, field[jnp.maximum(z - 1, 0)], 0.0)
        after = jnp.where(z < PZ - 1, field[jnp.minimum(z + 1, PZ - 1)], 0.0)
        wz, wx, wy = weights
        total = (wz * ((before - f) + (after - f)) + wx * ((up - f) + (down - f))) + wy * (
            (left - f) + (right - f)
        )
        return f, total

    def plane(z, carry):
        p, spread_p = spread(phi, z, phi_halo, PHASE_WEIGHTS)
        s, spread_s = spread(sol, z, sol_halo, SOLUTE_WEIGHTS)
        drive = 0.45 * jnp.tanh(
            response[z] * (liquefying_threshold - warmth[z] - freezing_line_gradient * s)
        )
        p_new = p + phase_dt * (spread_p + 4.0 * p * (1.0 - p) * (p - 0.5 + drive))
        new_phi[z] = p_new
        new_sol[z] = s + phase_dt * spread_s - solute_reject * (p_new - p) * s
        return carry

    lax.fori_loop(0, PZ, plane, 0, unroll=4)


def first_kernel(
    slabs,
    ids,
    laser,
    owners,
    sources,
    inbox,
    near,
    far,
    sides,
    heat,
    coeff,
    order,
    warmth,
    joined,
    near_out,
    far_out,
    sides_out,
    above_a,
    below_a,
    sides_a,
    above_b,
    below_b,
    sides_b,
    deposit,
):
    grp, slab = ids[0], ids[1]
    parity = slab & 1
    count = owners.shape[0] // 2
    for part, (above, below, side) in enumerate(
        ((above_a, below_a, sides_a), (above_b, below_b, sides_b))
    ):
        receive_rows(ids, near, far, part, above, below, slabs)
        side[...] = receive_sides(ids, sides, part).reshape(PZ, CX, CY)
    halo_a = (above_a, below_a, sides_a)
    halo_b = (above_b, below_b, sides_b)

    def arrived(pair):
        rows = []
        for core in (0, 1):
            for slot in (0, 1):
                at = 2 * slot + pair
                rows.append(
                    jnp.where(parity == 0, inbox[core, :, at, :], inbox[core, :, 4 + at, :])
                )
        return jnp.concatenate(rows, axis=0)

    lane = iota((CY, CY), 1)

    @pl.when(grp == 0)
    def _():
        table = plate_table(owners, sources, slab)
        for pair in (0, 1):
            units = pick_left(table, arrived(pair), ((0,), (0,)))
            left, right = units[:CY], units[CY:]
            even = jnp.where(lane < HALF, left, pltpu.roll(right, HALF, 1))
            odd = jnp.where(lane < HALF, pltpu.roll(left, HALF, 1), right)
            for i, layer in ((2 * pair, even), (2 * pair + 1, odd)):
                layer = layer.reshape(PZ // ZQ, CX, CY)
                for q in range(PZ // ZQ):
                    joined[0, 0, ZQ * q + i] = layer[q]
        cell = iota((CX, CY), 0) * CY + iota((CX, CY), 1)

        def add(n, total):
            return total + jnp.where(cell == laser[n], laser_power, 0.0)

        deposit[...] = lax.fori_loop(
            0, laser.shape[0], add, jnp.zeros((CX, CY), F32), unroll=True
        )

        def source(z):
            return joined[0, 0, z] + jnp.where(z == 0, deposit[...], 0.0)

        first = joined.at[0, 1]
        heat_planes(heat, coeff, order, source, first, halo_a, halo_b)
        send_edges(first, parity, near_out, far_out, 0)
        sides_out[...] = edge_columns(first[...].reshape(PZ * CX, CY), 0)

    @pl.when(grp == 1)
    def _():
        table = window_table(owners, slab)
        row = iota((CY, 2 * CY), 0)
        col = iota((CY, 2 * CY), 1)
        target = col & (CY - 1)
        parent = target >> 1
        next_to = jnp.clip(parent - 1 + 2 * (target & 1), 0, HALF - 1)
        at = row - (col >> 7) * HALF
        fine = (jnp.where(at == parent, 0.75, 0.0) + jnp.where(at == next_to, 0.25, 0.0)).astype(
            BF16
        )
        for pair in (0, 1):
            refined = pick_right(arrived(pair), fine)
            placed = pick_left(table, refined, ((0,), (0,)))
            for i in (0, 1):
                layer = placed[:, i * CY : (i + 1) * CY].reshape(PZ // ZQ, CX, CY)
                for q in range(PZ // ZQ):
                    warmth[0, ZQ * q + 2 * pair + i] = layer[q]
        phase_planes(
            order.at[0],
            order.at[1],
            coeff,
            warmth.at[0],
            joined.at[0, 0],
            joined.at[0, 1],
            halo_a,
            halo_b,
        )


def second_kernel(
    slabs,
    ids,
    laser,
    near_k,
    far_k,
    sides_k,
    near,
    far,
    sides,
    coeff,
    order,
    warmth,
    joined,
    result,
    above_a,
    below_a,
    sides_a,
    above_b,
    below_b,
    sides_b,
    deposit,
):
    grp = ids[0]

    @pl.when(grp == 0)
    def _():
        receive_rows(ids, near, far, 0, above_a, below_a, slabs)
        sides_a[...] = receive_sides(ids, sides, 0).reshape(PZ, CX, CY)
        receive_rows(ids, near_k, far_k, 1, above_b, below_b, slabs)
        sides_b[...] = receive_sides(ids, sides_k, 1).reshape(PZ, CX, CY)
        cell = iota((CX, CY), 0) * CY + iota((CX, CY), 1)

        def add(n, total):
            return total + jnp.where(cell == laser[n], laser_power, 0.0)

        deposit[...] = lax.fori_loop(
            0, laser.shape[0], add, jnp.zeros((CX, CY), F32), unroll=True
        )

        def source(z):
            return joined[0, 0, z] + jnp.where(z == 0, deposit[...], 0.0)

        heat_planes(
            joined.at[0, 1],
            coeff,
            order,
            source,
            result.at[0],
            (above_a, below_a, sides_a),
            (above_b, below_b, sides_b),
        )

    @pl.when(grp == 1)
    def _():
        result[...] = warmth[...]


SMEM = pl.BlockSpec(memory_space=pltpu.SMEM)
VMEM = pl.BlockSpec(memory_space=pltpu.VMEM)
PARAMS = pltpu.CompilerParams(vmem_limit_bytes=24 << 20)


def call(kernel, specs, outs, scratch=()):
    shapes = [jax.ShapeDtypeStruct(shape, F32) for shape in outs]
    single = len(shapes) == 1
    return pl.pallas_call(
        kernel,
        out_shape=shapes[0] if single else shapes,
        in_specs=list(specs),
        out_specs=VMEM if single else [VMEM] * len(shapes),
        scratch_shapes=list(scratch),
        compiler_params=PARAMS,
    )


def halo_scratch():
    one = [
        pltpu.VMEM((PZ, CY), F32),
        pltpu.VMEM((PZ, CY), F32),
        pltpu.VMEM((PZ, CX, CY), F32),
    ]
    return one + one + [pltpu.VMEM((CX, CY), F32)]


def per_device(heat_field, coeff, order, block_owner, block_source, laser_cells):
    slabs = lax.axis_size("slab")
    chips = slabs // 2
    grp = lax.axis_index("grp")
    ids = jnp.stack([grp, lax.axis_index("slab"), lax.axis_index("col")]).astype(jnp.int32)
    near_pairs = [[2 * i, 2 * i + 1] for i in range(chips)]
    far_pairs = [[2 * i + 1, (2 * i + 2) % slabs] for i in range(chips)]
    same_core = [[2 * i + k for i in range(chips)] for k in range(2)]
    heat, conduct, orders = heat_field[0], coeff[0], order[0]
    owners, sources, laser = block_owner[0, :, :, 0], block_source[0], laser_cells[0, 0]

    outbox = call(pack_kernel, [SMEM, VMEM, VMEM, VMEM], [(chips, 8, CY)])(
        ids, owners, sources, heat.reshape(PZ // ZQ, ZQ, CX, CY)
    )
    crossed = lax.all_gather(outbox, "grp")
    crossed = lax.dynamic_index_in_dim(crossed, 1 - grp, 0, keepdims=False)
    moved = lax.all_to_all(
        crossed, "slab", split_axis=0, concat_axis=0, tiled=True, axis_index_groups=same_core
    )
    inbox = lax.all_gather(moved, "slab", axis_index_groups=near_pairs)

    rows, columns = (2, PZ, CY), (8, PZ * CX)
    near, far, sides = call(edges_kernel, [SMEM, VMEM, VMEM, VMEM], [rows, rows, columns])(
        ids, heat, conduct, orders
    )

    def exchanged(near, far, sides):
        def pairs(x, groups):
            return lax.all_gather(x, "slab", axis_index_groups=groups)

        return pairs(near, near_pairs), pairs(far, far_pairs), lax.all_gather(sides, "col")

    near, far, sides = exchanged(near, far, sides)
    row, field = (1, PZ, CY), (PZ, CX, CY)
    warmth, joined, near_1, far_1, sides_1 = call(
        functools.partial(first_kernel, slabs),
        [SMEM, SMEM] + [VMEM] * 9,
        [(1,) + field, (1, 2) + field, row, row, columns],
        halo_scratch(),
    )(ids, laser, owners, sources, inbox, near, far, sides, heat, conduct, orders)
    near_1, far_1, sides_1 = exchanged(near_1, far_1, sides_1)
    warmth = call(
        functools.partial(second_kernel, slabs),
        [SMEM, SMEM] + [VMEM] * 10,
        [(1,) + field],
        halo_scratch(),
    )(ids, laser, near, far, sides, near_1, far_1, sides_1, conduct, orders, warmth, joined)
    return warmth, joined


def solution(mesh):
    placed = (
        P("grp", None, "slab", "col"),
        P("grp", None, "slab", "col"),
        P("grp", None, None, "slab", "col"),
        P("col", None, None, None),
        P("col", None, None),
        P("slab", "col", None),
    )
    return jax.shard_map(
        per_device,
        mesh=mesh,
        in_specs=placed,
        out_specs=(P("grp", None, "slab", "col"), P("grp", None, None, "slab", "col")),
        check_vma=False,
    )
```

```python
import jax
import jax.numpy as jnp
from jax import lax
from jax.experimental import pallas as pl
from jax.experimental.pallas import tpu as pltpu
from jax.sharding import PartitionSpec as P

PZ = 32
ZQ = 4
CX = 16
CY = 128
HALF = CY // 2

heat_dt = 0.07
phase_dt = 0.1
laser_power = 3.0
liquefying_threshold = 0.3
freezing_line_gradient = 0.5
solute_reject = 0.5
PHASE_WEIGHTS = (1.0, 1.3, 0.7)
SOLUTE_WEIGHTS = (0.8, 0.8, 0.8)

F32 = jnp.float32
BF16 = jnp.bfloat16
BIG = 1 << 20


def iota(shape, dim):
    return lax.broadcasted_iota(jnp.int32, shape, dim)


def ones_where(mask):
    return jnp.where(mask, 1.0, 0.0).astype(BF16)


def two_parts(x):
    high = x.astype(BF16)
    return high, (x - high.astype(F32)).astype(BF16)


def dot(a, b, dims=((1,), (0,))):
    return lax.dot_general(a, b, (dims, ((), ())), preferred_element_type=F32)


def pick_left(table, x, dims=((1,), (0,))):
    width = x.shape[1]
    both = dot(table, jnp.concatenate(two_parts(x), axis=1), dims)
    return both[:, :width] + both[:, width:]


def pick_right(x, table, dims=((1,), (0,))):
    high, low = two_parts(x)
    return dot(high, table, dims) + dot(low, table, dims)


def plate_table(owners, sources, slab):
    count = owners.shape[0] // 2
    rows = []
    for parity in (0, 1):
        own = owners[pl.ds(parity, count, stride=2), :]
        src = sources[pl.ds(parity, count, stride=2), :]
        key = iota(own.shape, 1) * 256 + src
        mine = own == slab
        first = jnp.min(jnp.where(mine, key, BIG).astype(F32), axis=1, keepdims=True)
        last = jnp.max(jnp.where(mine, key, -1).astype(F32), axis=1, keepdims=True)
        first, last = first.astype(jnp.int32), last.astype(jnp.int32)
        for value, valid in ((first, first < BIG), (last, last > first)):
            unit = value & 255
            place = jnp.where(valid, (unit & 1) * 128 + (unit >> 1), -1)
            rows.append(ones_where(iota((count, 256), 1) == place))
    return jnp.concatenate(rows, axis=0)


def window_table(owners, slab):
    count = owners.shape[0] // 2
    own = owners[pl.ds(slab, 1), :]
    units = own.shape[1]
    unit = iota((count, units), 1)
    rows = []
    for parity in (0, 1):
        mine = jnp.broadcast_to(own, (count, units)) == iota((count, units), 0) * 2 + parity
        first = jnp.min(jnp.where(mine, unit, BIG).astype(F32), axis=1, keepdims=True)
        last = jnp.max(jnp.where(mine, unit, -1).astype(F32), axis=1, keepdims=True)
        first, last = first.astype(jnp.int32), last.astype(jnp.int32)
        rows.append(ones_where(unit == first))
        rows.append(ones_where((unit == last) & (last > first)))
    spread = ones_where((iota((units, 2 * units), 1) >> 1) == iota((units, 2 * units), 0))
    return dot(jnp.concatenate(rows, axis=0), spread).astype(BF16)


def pack_kernel(ids, owners, sources, heats, out):
    grp, slab = ids[0], ids[1]
    heat = heats.at[1 - grp]
    count = owners.shape[0] // 2
    lane = iota((CY, CY), 1)

    def store(result, pair):
        for block in range(4):
            out[:, block * 2 + pair, :] = result[block * count : (block + 1) * count]

    @pl.when(grp == 1)
    def _():
        table = plate_table(owners, sources, slab)
        for pair in (0, 1):
            even = heat[:, 2 * pair].reshape(CY, CY)
            odd = heat[:, 2 * pair + 1].reshape(CY, CY)
            left = jnp.where(lane < HALF, even, pltpu.roll(odd, HALF, 1))
            right = jnp.where(lane < HALF, pltpu.roll(even, HALF, 1), odd)
            store(pick_left(table, jnp.concatenate([left, right], axis=0)), pair)

    @pl.when(grp == 0)
    def _():
        table = window_table(owners, slab)
        row = iota((2 * CY, CY), 0)
        col = iota((2 * CY, CY), 1)
        mean = jnp.where((row >> 1) == col, 0.25, 0.0).astype(BF16)
        for pair in (0, 1):
            even = heat[:, 2 * pair].reshape(CY, CY)
            odd = heat[:, 2 * pair + 1].reshape(CY, CY)
            means = pick_right(jnp.concatenate([even, odd], axis=1), mean)
            store(pick_left(table, means), pair)


def edge_columns(x, right):
    pick = ones_where(iota((8, CY), 1) == jnp.where(right, CY - 1, 0))
    high, low = two_parts(x)
    dims = ((1,), (1,))
    return (dot(pick, high, dims) + dot(pick, low, dims))[:1]


def send_edges(ids, fields, near, far, side_a, side_b):
    even_slab, even_col = ids[1] & 1 == 0, ids[2] & 1 == 0
    for part, x in enumerate(fields):
        top, bottom = x[:, 0, :], x[:, CX - 1, :]
        near[part] = jnp.where(even_slab, bottom, top)
        far[part] = jnp.where(even_slab, top, bottom)
        flat = x[...].reshape(PZ * CX, CY)
        side_a[part : part + 1] = edge_columns(flat, even_col)
        side_b[part : part + 1] = edge_columns(flat, jnp.logical_not(even_col))


def edges_kernel(ids, heat, coeff, order, near, far, side_a, side_b):
    grp = ids[0]

    @pl.when(grp == 0)
    def _():
        send_edges(ids, (heat, coeff), near, far, side_a, side_b)

    @pl.when(grp == 1)
    def _():
        send_edges(ids, (order.at[0], order.at[1]), near, far, side_a, side_b)


def receive_sides(ids, side_a, side_b, part):
    even = ids[2] & 1 == 0
    in_a, in_b = side_a[part : part + 1], side_b[part : part + 1]
    left, right = jnp.where(even, in_b, in_a), jnp.where(even, in_a, in_b)
    size = left.shape[1]
    row = iota((8, size), 0)
    left = jnp.broadcast_to(left, (8, size))
    right = jnp.broadcast_to(right, (8, size))
    both = jnp.where(row == 0, left, jnp.where(row == 1, right, 0.0))
    row, lane = iota((8, CY), 0), iota((8, CY), 1)
    place = ones_where(((row == 0) & (lane == 0)) | ((row == 1) & (lane == CY - 1)))
    return pick_right(both, place, ((0,), (0,)))


def receive_rows(ids, near, far, part, above, below):
    even = ids[1] & 1 == 0
    near_row = jnp.where(even, near[1, part], near[0, part])
    far_row = far[part]
    above[...] = jnp.where(even, far_row, near_row)
    below[...] = jnp.where(even, near_row, far_row)


def beside(v, above, below, sides):
    row, lane = iota((CX, CY), 0), iota((CX, CY), 1)
    up = jnp.where(row == 0, jnp.broadcast_to(above, (CX, CY)), pltpu.roll(v, 1, 0))
    down = jnp.where(row == CX - 1, jnp.broadcast_to(below, (CX, CY)), pltpu.roll(v, CX - 1, 0))
    left = jnp.where(lane == 0, sides, pltpu.roll(v, 1, 1))
    right = jnp.where(lane == CY - 1, sides, pltpu.roll(v, CY - 1, 1))
    return up, down, left, right


def harmonic(center, beside_it):
    return 2.0 * center * beside_it / (center + beside_it)


def heat_planes(temp, cond, order, source, result, temp_halo, cond_halo):
    temp_above, temp_below, temp_sides = temp_halo
    cond_above, cond_below, cond_sides = cond_halo

    def plane(z, from_above):
        v, k = temp[z], cond[z]
        one = pl.ds(z, 1)
        vs = beside(v, temp_above[one, :], temp_below[one, :], temp_sides[z])
        ks = beside(k, cond_above[one, :], cond_below[one, :], cond_sides[z])
        later = jnp.minimum(z + 1, PZ - 1)
        to_below = harmonic(k, cond[later]) * (temp[later] - v)
        total = to_below - from_above
        for v_next, k_next in zip(vs, ks):
            total = total + harmonic(k, k_next) * (v_next - v)
        result[z] = v + heat_dt * ((total + source(z)) / order[0, z] - order[1, z] * v)
        return to_below

    lax.fori_loop(0, PZ, plane, jnp.zeros((CX, CY), F32), unroll=4)


def phase_planes(phi, sol, response, warmth, new_phi, new_sol, phi_halo, sol_halo):
    phi_above, phi_below, phi_sides = phi_halo
    sol_above, sol_below, sol_sides = sol_halo

    def spread(field, z, halo, weights):
        above, below, sides = halo
        f = field[z]
        one = pl.ds(z, 1)
        up, down, left, right = beside(f, above[one, :], below[one, :], sides[z])
        before = jnp.where(z > 0, field[jnp.maximum(z - 1, 0)], 0.0)
        after = jnp.where(z < PZ - 1, field[jnp.minimum(z + 1, PZ - 1)], 0.0)
        wz, wx, wy = weights
        total = (wz * ((before - f) + (after - f)) + wx * ((up - f) + (down - f))) + wy * (
            (left - f) + (right - f)
        )
        return f, total

    def plane(z, carry):
        p, spread_p = spread(phi, z, phi_halo, PHASE_WEIGHTS)
        s, spread_s = spread(sol, z, sol_halo, SOLUTE_WEIGHTS)
        drive = 0.45 * jnp.tanh(
            response[z] * (liquefying_threshold - warmth[z] - freezing_line_gradient * s)
        )
        p_new = p + phase_dt * (spread_p + 4.0 * p * (1.0 - p) * (p - 0.5 + drive))
        new_phi[z] = p_new
        new_sol[z] = s + phase_dt * spread_s - solute_reject * (p_new - p) * s
        return carry

    lax.fori_loop(0, PZ, plane, 0, unroll=4)


def first_kernel(
    ids,
    laser,
    owners,
    sources,
    inbox,
    near,
    far,
    side_a,
    side_b,
    heat,
    coeff,
    order,
    warmth,
    joined,
    near_out,
    far_out,
    side_a_out,
    side_b_out,
    above_a,
    below_a,
    sides_a,
    above_b,
    below_b,
    sides_b,
    deposit,
):
    grp, slab = ids[0], ids[1]
    parity = slab & 1
    count = owners.shape[0] // 2
    for part, (above, below, side) in enumerate(
        ((above_a, below_a, sides_a), (above_b, below_b, sides_b))
    ):
        receive_rows(ids, near, far, part, above, below)
        side[...] = receive_sides(ids, side_a, side_b, part).reshape(PZ, CX, CY)
    halo_a = (above_a, below_a, sides_a)
    halo_b = (above_b, below_b, sides_b)

    def arrived(pair):
        rows = []
        for core in (0, 1):
            for slot in (0, 1):
                at = 2 * slot + pair
                rows.append(
                    jnp.where(parity == 0, inbox[core, :, at, :], inbox[core, :, 4 + at, :])
                )
        return jnp.concatenate(rows, axis=0)

    lane = iota((CY, CY), 1)

    @pl.when(grp == 0)
    def _():
        table = plate_table(owners, sources, slab)
        for pair in (0, 1):
            units = pick_left(table, arrived(pair), ((0,), (0,)))
            left, right = units[:CY], units[CY:]
            even = jnp.where(lane < HALF, left, pltpu.roll(right, HALF, 1))
            odd = jnp.where(lane < HALF, pltpu.roll(left, HALF, 1), right)
            for i, layer in ((2 * pair, even), (2 * pair + 1, odd)):
                layer = layer.reshape(PZ // ZQ, CX, CY)
                for q in range(PZ // ZQ):
                    joined[0, 0, ZQ * q + i] = layer[q]
        cell = iota((CX, CY), 0) * CY + iota((CX, CY), 1)

        def add(n, total):
            return total + jnp.where(cell == laser[n], laser_power, 0.0)

        deposit[...] = lax.fori_loop(
            0, laser.shape[0], add, jnp.zeros((CX, CY), F32), unroll=True
        )

        def source(z):
            return joined[0, 0, z] + jnp.where(z == 0, deposit[...], 0.0)

        first = joined.at[0, 1]
        heat_planes(heat, coeff, order, source, first, halo_a, halo_b)
        send_edges(ids, (first,), near_out, far_out, side_a_out, side_b_out)

    @pl.when(grp == 1)
    def _():
        table = window_table(owners, slab)
        row = iota((CY, 2 * CY), 0)
        col = iota((CY, 2 * CY), 1)
        target = col & (CY - 1)
        parent = target >> 1
        next_to = jnp.clip(parent - 1 + 2 * (target & 1), 0, HALF - 1)
        at = row - (col >> 7) * HALF
        fine = (jnp.where(at == parent, 0.75, 0.0) + jnp.where(at == next_to, 0.25, 0.0)).astype(
            BF16
        )
        for pair in (0, 1):
            refined = pick_right(arrived(pair), fine)
            placed = pick_left(table, refined, ((0,), (0,)))
            for i in (0, 1):
                layer = placed[:, i * CY : (i + 1) * CY].reshape(PZ // ZQ, CX, CY)
                for q in range(PZ // ZQ):
                    warmth[0, ZQ * q + 2 * pair + i] = layer[q]
        phase_planes(
            order.at[0],
            order.at[1],
            coeff,
            warmth.at[0],
            joined.at[0, 0],
            joined.at[0, 1],
            halo_a,
            halo_b,
        )


def second_kernel(
    ids,
    laser,
    near_k,
    far_k,
    side_a_k,
    side_b_k,
    near,
    far,
    side_a,
    side_b,
    coeff,
    order,
    warmth,
    joined,
    result,
    above_a,
    below_a,
    sides_a,
    above_b,
    below_b,
    sides_b,
    deposit,
):
    grp = ids[0]

    @pl.when(grp == 0)
    def _():
        receive_rows(ids, near, far, 0, above_a, below_a)
        sides_a[...] = receive_sides(ids, side_a, side_b, 0).reshape(PZ, CX, CY)
        receive_rows(ids, near_k, far_k, 1, above_b, below_b)
        sides_b[...] = receive_sides(ids, side_a_k, side_b_k, 1).reshape(PZ, CX, CY)
        cell = iota((CX, CY), 0) * CY + iota((CX, CY), 1)

        def add(n, total):
            return total + jnp.where(cell == laser[n], laser_power, 0.0)

        deposit[...] = lax.fori_loop(
            0, laser.shape[0], add, jnp.zeros((CX, CY), F32), unroll=True
        )

        def source(z):
            return joined[0, 0, z] + jnp.where(z == 0, deposit[...], 0.0)

        heat_planes(
            joined.at[0, 1],
            coeff,
            order,
            source,
            result.at[0],
            (above_a, below_a, sides_a),
            (above_b, below_b, sides_b),
        )

    @pl.when(grp == 1)
    def _():
        result[...] = warmth[...]


SMEM = pl.BlockSpec(memory_space=pltpu.SMEM)
VMEM = pl.BlockSpec(memory_space=pltpu.VMEM)
PARAMS = pltpu.CompilerParams(vmem_limit_bytes=24 << 20)


def call(kernel, specs, outs, scratch=()):
    shapes = [jax.ShapeDtypeStruct(shape, F32) for shape in outs]
    single = len(shapes) == 1
    return pl.pallas_call(
        kernel,
        out_shape=shapes[0] if single else shapes,
        in_specs=list(specs),
        out_specs=VMEM if single else [VMEM] * len(shapes),
        scratch_shapes=list(scratch),
        compiler_params=PARAMS,
    )


def halo_scratch():
    one = [
        pltpu.VMEM((PZ, CY), F32),
        pltpu.VMEM((PZ, CY), F32),
        pltpu.VMEM((PZ, CX, CY), F32),
    ]
    return one + one + [pltpu.VMEM((CX, CY), F32)]


def swaps(starts):
    return [pair for i in starts for pair in ((i, i + 1), (i + 1, i))]


def per_device(heat_field, coeff, order, block_owner, block_source, laser_cells):
    slabs, cols = lax.axis_size("slab"), lax.axis_size("col")
    chips = slabs // 2
    grp = lax.axis_index("grp")
    ids = jnp.stack([grp, lax.axis_index("slab"), lax.axis_index("col")]).astype(jnp.int32)
    near_pairs = [[2 * i, 2 * i + 1] for i in range(chips)]
    same_core = [[2 * i + k for i in range(chips)] for k in range(2)]
    far_swap = swaps(range(1, slabs - 1, 2))
    side_a_swap, side_b_swap = swaps(range(0, cols - 1, 2)), swaps(range(1, cols - 1, 2))
    heat, conduct, orders = heat_field[0], coeff[0], order[0]
    owners, sources, laser = block_owner[0, :, :, 0], block_source[0], laser_cells[0, 0]

    heats = lax.all_gather(heat.reshape(PZ // ZQ, ZQ, CX, CY), "grp")
    outbox = call(pack_kernel, [SMEM, VMEM, VMEM, VMEM], [(chips, 8, CY)])(
        ids, owners, sources, heats
    )
    moved = lax.all_to_all(
        outbox, "slab", split_axis=0, concat_axis=0, tiled=True, axis_index_groups=same_core
    )
    inbox = lax.all_gather(moved, "slab", axis_index_groups=near_pairs)

    def exchanged(near, far, side_a, side_b):
        far = lax.ppermute(far, "slab", far_swap)
        side_a = lax.ppermute(side_a, "col", side_a_swap)
        side_b = lax.ppermute(side_b, "col", side_b_swap)
        near = lax.all_gather(near, "slab", axis_index_groups=near_pairs)
        return near, far, side_a, side_b

    rows, column = (2, PZ, CY), (2, PZ * CX)
    edges = call(edges_kernel, [SMEM, VMEM, VMEM, VMEM], [rows, rows, column, column])(
        ids, heat, conduct, orders
    )
    edges = exchanged(*edges)
    row, column, field = (1, PZ, CY), (1, PZ * CX), (PZ, CX, CY)
    warmth, joined, *edges_1 = call(
        first_kernel,
        [SMEM, SMEM] + [VMEM] * 10,
        [(1,) + field, (1, 2) + field, row, row, column, column],
        halo_scratch(),
    )(ids, laser, owners, sources, inbox, *edges, heat, conduct, orders)
    edges_1 = exchanged(*edges_1)
    warmth = call(
        second_kernel,
        [SMEM, SMEM] + [VMEM] * 12,
        [(1,) + field],
        halo_scratch(),
    )(ids, laser, *edges, *edges_1, conduct, orders, warmth, joined)
    return warmth, joined


def solution(mesh):
    placed = (
        P("grp", None, "slab", "col"),
        P("grp", None, "slab", "col"),
        P("grp", None, None, "slab", "col"),
        P("col", None, None, None),
        P("col", None, None),
        P("slab", "col", None),
    )
    return jax.shard_map(
        per_device,
        mesh=mesh,
        in_specs=placed,
        out_specs=(P("grp", None, "slab", "col"), P("grp", None, None, "slab", "col")),
        check_vma=False,
    )
```

```python
import jax
import jax.numpy as jnp
from jax import lax
from jax.experimental import pallas as pl
from jax.experimental.pallas import tpu as pltpu
from jax.sharding import PartitionSpec as P

PZ = 32
ZQ = 4
CX = 16
CY = 128
HALF = CY // 2

heat_dt = 0.07
phase_dt = 0.1
laser_power = 3.0
liquefying_threshold = 0.3
freezing_line_gradient = 0.5
solute_reject = 0.5
PHASE_WEIGHTS = (1.0, 1.3, 0.7)
SOLUTE_WEIGHTS = (0.8, 0.8, 0.8)

F32 = jnp.float32
BF16 = jnp.bfloat16
BIG = 1 << 20


def iota(shape, dim):
    return lax.broadcasted_iota(jnp.int32, shape, dim)


def ones_where(mask):
    return jnp.where(mask, 1.0, 0.0).astype(BF16)


def two_parts(x):
    high = x.astype(BF16)
    return high, (x - high.astype(F32)).astype(BF16)


def dot(a, b, dims=((1,), (0,))):
    return lax.dot_general(a, b, (dims, ((), ())), preferred_element_type=F32)


def pick_left(table, x, dims=((1,), (0,))):
    width = x.shape[1]
    both = dot(table, jnp.concatenate(two_parts(x), axis=1), dims)
    return both[:, :width] + both[:, width:]


def pick_right(x, table, dims=((1,), (0,))):
    high, low = two_parts(x)
    return dot(high, table, dims) + dot(low, table, dims)


def plate_table(owners, sources, slab):
    count = owners.shape[0] // 2
    rows = []
    for parity in (0, 1):
        own = owners[pl.ds(parity, count, stride=2), :]
        src = sources[pl.ds(parity, count, stride=2), :]
        key = iota(own.shape, 1) * 256 + src
        mine = own == slab
        first = jnp.min(jnp.where(mine, key, BIG).astype(F32), axis=1, keepdims=True)
        last = jnp.max(jnp.where(mine, key, -1).astype(F32), axis=1, keepdims=True)
        first, last = first.astype(jnp.int32), last.astype(jnp.int32)
        for value, valid in ((first, first < BIG), (last, last > first)):
            unit = value & 255
            place = jnp.where(valid, (unit & 1) * 128 + (unit >> 1), -1)
            rows.append(ones_where(iota((count, 256), 1) == place))
    return jnp.concatenate(rows, axis=0)


def window_table(owners, slab):
    count = owners.shape[0] // 2
    own = owners[pl.ds(slab, 1), :]
    units = own.shape[1]
    unit = iota((count, units), 1)
    rows = []
    for parity in (0, 1):
        mine = jnp.broadcast_to(own, (count, units)) == iota((count, units), 0) * 2 + parity
        first = jnp.min(jnp.where(mine, unit, BIG).astype(F32), axis=1, keepdims=True)
        last = jnp.max(jnp.where(mine, unit, -1).astype(F32), axis=1, keepdims=True)
        first, last = first.astype(jnp.int32), last.astype(jnp.int32)
        rows.append(ones_where(unit == first))
        rows.append(ones_where((unit == last) & (last > first)))
    spread = ones_where((iota((units, 2 * units), 1) >> 1) == iota((units, 2 * units), 0))
    return dot(jnp.concatenate(rows, axis=0), spread).astype(BF16)


def laser_heat(cells):
    count = cells.shape[1]
    rows = ones_where(iota((CX, count), 0) == jnp.broadcast_to(cells >> 7, (CX, count)))
    lanes = ones_where(iota((CY, count), 0) == jnp.broadcast_to(cells & 127, (CY, count)))
    return laser_power * dot(rows, lanes, ((1,), (1,)))


def pack_kernel(
    ids,
    owners_in,
    sources_in,
    heat_in,
    laser_in,
    out,
    deposit,
    owners,
    sources,
    heat,
    laser,
    sems,
):
    copies = [
        pltpu.make_async_copy(source, target, sems.at[n])
        for n, (source, target) in enumerate(
            (
                (owners_in, owners),
                (sources_in, sources),
                (heat_in, heat),
                (laser_in, laser),
            )
        )
    ]
    for copy in copies:
        copy.start()
    grp, slab = ids[0], ids[1]
    count = owners.shape[0] // 2
    lane = iota((CY, CY), 1)

    def store(result, pair):
        for block in range(4):
            out[:, block * 2 + pair, :] = result[block * count : (block + 1) * count]

    for n in (0, 1, 3):
        copies[n].wait()

    @pl.when(grp == 0)
    def _():
        table = plate_table(owners, sources, slab)
        deposit[...] = laser_heat(laser[...])
        copies[2].wait()
        for pair in (0, 1):
            even = heat[:, 2 * pair].reshape(CY, CY)
            odd = heat[:, 2 * pair + 1].reshape(CY, CY)
            left = jnp.where(lane < HALF, even, pltpu.roll(odd, HALF, 1))
            right = jnp.where(lane < HALF, pltpu.roll(even, HALF, 1), odd)
            store(pick_left(table, jnp.concatenate([left, right], axis=0)), pair)

    @pl.when(grp == 1)
    def _():
        table = window_table(owners, slab)
        copies[2].wait()
        row = iota((2 * CY, CY), 0)
        col = iota((2 * CY, CY), 1)
        mean = jnp.where((row >> 1) == col, 0.25, 0.0).astype(BF16)
        for pair in (0, 1):
            even = heat[:, 2 * pair].reshape(CY, CY)
            odd = heat[:, 2 * pair + 1].reshape(CY, CY)
            means = pick_right(jnp.concatenate([even, odd], axis=1), mean)
            store(pick_left(table, means), pair)


def edge_columns(x, right):
    pick = ones_where(iota((8, CY), 1) == jnp.where(right, CY - 1, 0))
    high, low = two_parts(x)
    dims = ((1,), (1,))
    return (dot(pick, high, dims) + dot(pick, low, dims))[:1]


def send_edges(ids, fields, near, far, side_a, side_b):
    even_slab, even_col = ids[1] & 1 == 0, ids[2] & 1 == 0
    for part, x in enumerate(fields):
        top, bottom = x[:, 0, :], x[:, CX - 1, :]
        near[part] = jnp.where(even_slab, bottom, top)
        far[part] = jnp.where(even_slab, top, bottom)
        flat = x[...].reshape(PZ * CX, CY)
        side_a[part : part + 1] = edge_columns(flat, even_col)
        side_b[part : part + 1] = edge_columns(flat, jnp.logical_not(even_col))


def edges_kernel(ids, heat, coeff, order, near, far, side_a, side_b):
    grp = ids[0]

    @pl.when(grp == 0)
    def _():
        send_edges(ids, (heat, coeff), near, far, side_a, side_b)

    @pl.when(grp == 1)
    def _():
        send_edges(ids, (order.at[0], order.at[1]), near, far, side_a, side_b)


def receive_sides(ids, side_a, side_b, part):
    even = ids[2] & 1 == 0
    in_a, in_b = side_a[part : part + 1], side_b[part : part + 1]
    left, right = jnp.where(even, in_b, in_a), jnp.where(even, in_a, in_b)
    size = left.shape[1]
    row = iota((8, size), 0)
    left = jnp.broadcast_to(left, (8, size))
    right = jnp.broadcast_to(right, (8, size))
    both = jnp.where(row == 0, left, jnp.where(row == 1, right, 0.0))
    row, lane = iota((8, CY), 0), iota((8, CY), 1)
    place = ones_where(((row == 0) & (lane == 0)) | ((row == 1) & (lane == CY - 1)))
    return pick_right(both, place, ((0,), (0,)))


def near_rows(inbox, chips, part):
    start = chips + part * PZ // 8
    return [inbox[core, start : start + PZ // 8].reshape(PZ, CY) for core in (0, 1)]


def receive_rows(ids, near, far, part, above, below):
    even = ids[1] & 1 == 0
    near_row = jnp.where(even, near[1], near[0])
    far_row = far[part]
    above[...] = jnp.where(even, far_row, near_row)
    below[...] = jnp.where(even, near_row, far_row)


def beside(v, above, below, sides):
    row, lane = iota((CX, CY), 0), iota((CX, CY), 1)
    up = jnp.where(row == 0, jnp.broadcast_to(above, (CX, CY)), pltpu.roll(v, 1, 0))
    down = jnp.where(row == CX - 1, jnp.broadcast_to(below, (CX, CY)), pltpu.roll(v, CX - 1, 0))
    left = jnp.where(lane == 0, sides, pltpu.roll(v, 1, 1))
    right = jnp.where(lane == CY - 1, sides, pltpu.roll(v, CY - 1, 1))
    return up, down, left, right


def harmonic(center, beside_it):
    return 2.0 * center * beside_it / (center + beside_it)


def heat_planes(
    temp, cond, order, source, result, temp_halo, cond_halo, begin=0, end=PZ
):
    temp_above, temp_below, temp_sides = temp_halo
    cond_above, cond_below, cond_sides = cond_halo

    def plane(z, from_above):
        v, k = temp[z], cond[z]
        one = pl.ds(z, 1)
        vs = beside(v, temp_above[one, :], temp_below[one, :], temp_sides[z])
        ks = beside(k, cond_above[one, :], cond_below[one, :], cond_sides[z])
        later = jnp.minimum(z + 1, PZ - 1)
        to_below = harmonic(k, cond[later]) * (temp[later] - v)
        total = to_below - from_above
        for v_next, k_next in zip(vs, ks):
            total = total + harmonic(k, k_next) * (v_next - v)
        result[z] = v + heat_dt * ((total + source(z)) / order[0, z] - order[1, z] * v)
        return to_below

    if begin == 0:
        carry = jnp.zeros((CX, CY), F32)
    else:
        before = begin - 1
        carry = harmonic(cond[before], cond[begin]) * (temp[begin] - temp[before])
    lax.fori_loop(begin, end, plane, carry, unroll=4)


def phase_planes(phi, sol, response, warmth, new_phi, new_sol, phi_halo, sol_halo):
    phi_above, phi_below, phi_sides = phi_halo
    sol_above, sol_below, sol_sides = sol_halo

    def spread(field, z, halo, weights):
        above, below, sides = halo
        f = field[z]
        one = pl.ds(z, 1)
        up, down, left, right = beside(f, above[one, :], below[one, :], sides[z])
        before = jnp.where(z > 0, field[jnp.maximum(z - 1, 0)], 0.0)
        after = jnp.where(z < PZ - 1, field[jnp.minimum(z + 1, PZ - 1)], 0.0)
        wz, wx, wy = weights
        total = (wz * ((before - f) + (after - f)) + wx * ((up - f) + (down - f))) + wy * (
            (left - f) + (right - f)
        )
        return f, total

    def plane(z, carry):
        p, spread_p = spread(phi, z, phi_halo, PHASE_WEIGHTS)
        s, spread_s = spread(sol, z, sol_halo, SOLUTE_WEIGHTS)
        drive = 0.45 * jnp.tanh(
            response[z] * (liquefying_threshold - warmth[z] - freezing_line_gradient * s)
        )
        p_new = p + phase_dt * (spread_p + 4.0 * p * (1.0 - p) * (p - 0.5 + drive))
        new_phi[z] = p_new
        new_sol[z] = s + phase_dt * spread_s - solute_reject * (p_new - p) * s
        return carry

    lax.fori_loop(0, PZ, plane, 0, unroll=4)


def first_kernel(
    ids,
    deposit,
    owners,
    sources,
    inbox,
    far,
    side_a,
    side_b,
    heat,
    coeff,
    order,
    joined,
    warmth,
    near_out,
    far_out,
    side_a_out,
    side_b_out,
    above_a,
    below_a,
    sides_a,
    above_b,
    below_b,
    sides_b,
):
    grp, slab = ids[0], ids[1]
    parity = slab & 1
    chips = owners.shape[0] // 2
    for part, (above, below, side) in enumerate(
        ((above_a, below_a, sides_a), (above_b, below_b, sides_b))
    ):
        receive_rows(ids, near_rows(inbox, chips, part), far, part, above, below)
        side[...] = receive_sides(ids, side_a, side_b, part).reshape(PZ, CX, CY)
    halo_a = (above_a, below_a, sides_a)
    halo_b = (above_b, below_b, sides_b)

    def arrived(pair):
        rows = []
        for core in (0, 1):
            for slot in (0, 1):
                at = 2 * slot + pair
                rows.append(
                    jnp.where(
                        parity == 0, inbox[core, :chips, at, :], inbox[core, :chips, 4 + at, :]
                    )
                )
        return jnp.concatenate(rows, axis=0)

    lane = iota((CY, CY), 1)

    @pl.when(grp == 0)
    def _():
        table = plate_table(owners, sources, slab)
        for pair in (0, 1):
            units = pick_left(table, arrived(pair), ((0,), (0,)))
            left, right = units[:CY], units[CY:]
            even = jnp.where(lane < HALF, left, pltpu.roll(right, HALF, 1))
            odd = jnp.where(lane < HALF, pltpu.roll(left, HALF, 1), right)
            for i, layer in ((2 * pair, even), (2 * pair + 1, odd)):
                layer = layer.reshape(PZ // ZQ, CX, CY)
                for q in range(PZ // ZQ):
                    joined[0, ZQ * q + i] = layer[q]

        def source(z):
            return joined[0, z] + jnp.where(z == 0, deposit[...], 0.0)

        first = joined.at[1]
        heat_planes(heat, coeff, order, source, first, halo_a, halo_b)
        send_edges(ids, (first,), near_out, far_out, side_a_out, side_b_out)

    @pl.when(grp == 1)
    def _():
        table = window_table(owners, slab)
        row = iota((CY, 2 * CY), 0)
        col = iota((CY, 2 * CY), 1)
        target = col & (CY - 1)
        parent = target >> 1
        next_to = jnp.clip(parent - 1 + 2 * (target & 1), 0, HALF - 1)
        at = row - (col >> 7) * HALF
        fine = (jnp.where(at == parent, 0.75, 0.0) + jnp.where(at == next_to, 0.25, 0.0)).astype(
            BF16
        )
        for pair in (0, 1):
            refined = pick_right(arrived(pair), fine)
            placed = pick_left(table, refined, ((0,), (0,)))
            for i in (0, 1):
                layer = placed[:, i * CY : (i + 1) * CY].reshape(PZ // ZQ, CX, CY)
                for q in range(PZ // ZQ):
                    warmth[ZQ * q + 2 * pair + i] = layer[q]
        phase_planes(
            order.at[0],
            order.at[1],
            coeff,
            warmth,
            joined.at[0],
            joined.at[1],
            halo_a,
            halo_b,
        )


def second_kernel(
    ids,
    deposit,
    inbox,
    far_k,
    side_a_k,
    side_b_k,
    near,
    far,
    side_a,
    side_b,
    coeff,
    order,
    joined,
    warmth,
    result_out,
    joined_out,
    above_a,
    below_a,
    sides_a,
    above_b,
    below_b,
    sides_b,
    result,
    sems,
):
    grp = ids[0]
    joined_copy = pltpu.make_async_copy(joined, joined_out.at[0], sems.at[0])
    joined_copy.start()
    parts = RESULT_PARTS
    size = PZ // parts

    @pl.when(grp == 0)
    def _():
        receive_rows(ids, [near[0, 0], near[1, 0]], far, 0, above_a, below_a)
        sides_a[...] = receive_sides(ids, side_a, side_b, 0).reshape(PZ, CX, CY)
        chips = inbox.shape[1] - 2 * PZ // 8
        receive_rows(ids, near_rows(inbox, chips, 1), far_k, 1, above_b, below_b)
        sides_b[...] = receive_sides(ids, side_a_k, side_b_k, 1).reshape(PZ, CX, CY)

        def source(z):
            return joined[0, z] + jnp.where(z == 0, deposit[...], 0.0)

        copies = []
        for n in range(parts):
            heat_planes(
                joined.at[1],
                coeff,
                order,
                source,
                result,
                (above_a, below_a, sides_a),
                (above_b, below_b, sides_b),
                n * size,
                (n + 1) * size,
            )
            planes = pl.ds(n * size, size)
            copy = pltpu.make_async_copy(
                result.at[planes], result_out.at[0, planes], sems.at[1 + n]
            )
            copy.start()
            copies.append(copy)
        for copy in copies:
            copy.wait()

    @pl.when(grp == 1)
    def _():
        copy = pltpu.make_async_copy(warmth, result_out.at[0], sems.at[1])
        copy.start()
        copy.wait()

    joined_copy.wait()


RESULT_PARTS = 4
HBM = pl.BlockSpec(memory_space=pltpu.HBM)
SMEM = pl.BlockSpec(memory_space=pltpu.SMEM)
VMEM = pl.BlockSpec(memory_space=pltpu.VMEM)


def call(kernel, specs, outs, scratch=(), out_space=VMEM, limit=24 << 20):
    shapes = [jax.ShapeDtypeStruct(shape, F32) for shape in outs]
    single = len(shapes) == 1
    return pl.pallas_call(
        kernel,
        out_shape=shapes[0] if single else shapes,
        in_specs=list(specs),
        out_specs=out_space if single else [out_space] * len(shapes),
        scratch_shapes=list(scratch),
        compiler_params=pltpu.CompilerParams(vmem_limit_bytes=limit),
    )


def halo_scratch():
    one = [
        pltpu.VMEM((PZ, CY), F32),
        pltpu.VMEM((PZ, CY), F32),
        pltpu.VMEM((PZ, CX, CY), F32),
    ]
    return one + one


def swaps(starts):
    return [pair for i in starts for pair in ((i, i + 1), (i + 1, i))]


def per_device(heat_field, coeff, order, block_owner, block_source, laser_cells):
    slabs, cols = lax.axis_size("slab"), lax.axis_size("col")
    chips = slabs // 2
    grp = lax.axis_index("grp")
    ids = jnp.stack([grp, lax.axis_index("slab"), lax.axis_index("col")]).astype(jnp.int32)
    near_pairs = [[2 * i, 2 * i + 1] for i in range(chips)]
    same_core = [[2 * i + k for i in range(chips)] for k in range(2)]
    far_swap = swaps(range(1, slabs - 1, 2))
    side_a_swap, side_b_swap = swaps(range(0, cols - 1, 2)), swaps(range(1, cols - 1, 2))
    heat, conduct, orders = heat_field[0], coeff[0], order[0]
    owners, sources, laser = block_owner[0, :, :, 0], block_source[0], laser_cells[0]

    slab_table = pltpu.VMEM(owners.shape, jnp.int32)
    outbox, deposit = call(
        pack_kernel,
        [SMEM] + [HBM] * 4,
        [(chips, 8, CY), (CX, CY)],
        [
            slab_table,
            slab_table,
            pltpu.VMEM((PZ // ZQ, ZQ, CX, CY), F32),
            pltpu.VMEM(laser.shape, jnp.int32),
            pltpu.SemaphoreType.DMA((4,)),
        ],
        limit=60 << 20,
    )(ids, owners, sources, heat.reshape(PZ // ZQ, ZQ, CX, CY), laser)
    crossed = lax.all_gather(outbox, "grp")
    crossed = lax.dynamic_index_in_dim(crossed, 1 - grp, 0, keepdims=False)
    moved = lax.all_to_all(
        crossed, "slab", split_axis=0, concat_axis=0, tiled=True, axis_index_groups=same_core
    )

    def exchanged(far, side_a, side_b):
        far = lax.ppermute(far, "slab", far_swap)
        side_a = lax.ppermute(side_a, "col", side_a_swap)
        side_b = lax.ppermute(side_b, "col", side_b_swap)
        return far, side_a, side_b

    rows, column = (2, PZ, CY), (12, PZ * CX)
    near, *edges = call(
        edges_kernel, [SMEM] + [VMEM] * 3, [rows, rows, column, column]
    )(ids, heat, conduct, orders)
    edges = exchanged(*edges)
    inbox = lax.all_gather(
        jnp.concatenate([moved, near.reshape(-1, 8, CY)]), "slab", axis_index_groups=near_pairs
    )
    row, column, field = (1, PZ, CY), (1, PZ * CX), (PZ, CX, CY)
    joined, warmth, near_1, *edges_1 = call(
        first_kernel,
        [SMEM] + [VMEM] * 10,
        [(2,) + field, field, row, row, column, column],
        halo_scratch(),
    )(ids, deposit, owners, sources, inbox, *edges, heat, conduct, orders)
    edges_1 = exchanged(*edges_1)
    near_1 = lax.all_gather(near_1, "slab", axis_index_groups=near_pairs)
    return call(
        second_kernel,
        [SMEM] + [VMEM] * 13,
        [(1,) + field, (1, 2) + field],
        halo_scratch() + [pltpu.VMEM(field, F32), pltpu.SemaphoreType.DMA((1 + RESULT_PARTS,))],
        HBM,
    )(ids, deposit, inbox, *edges, near_1, *edges_1, conduct, orders, joined, warmth)


def solution(mesh):
    placed = (
        P("grp", None, "slab", "col"),
        P("grp", None, "slab", "col"),
        P("grp", None, None, "slab", "col"),
        P("col", None, None, None),
        P("col", None, None),
        P("slab", "col", None),
    )
    return jax.shard_map(
        per_device,
        mesh=mesh,
        in_specs=placed,
        out_specs=(P("grp", None, "slab", "col"), P("grp", None, None, "slab", "col")),
        check_vma=False,
    )
```

```python
import jax
import jax.numpy as jnp
from jax import lax
from jax.experimental import pallas as pl
from jax.experimental.pallas import tpu as pltpu
from jax.sharding import PartitionSpec as P

PZ = 32
ZQ = 4
CX = 16
CY = 128
HALF = CY // 2

heat_dt = 0.07
phase_dt = 0.1
laser_power = 3.0
liquefying_threshold = 0.3
freezing_line_gradient = 0.5
solute_reject = 0.5
PHASE_WEIGHTS = (1.0, 1.3, 0.7)
SOLUTE_WEIGHTS = (0.8, 0.8, 0.8)

F32 = jnp.float32
BF16 = jnp.bfloat16
BIG = 1 << 20


def iota(shape, dim):
    return lax.broadcasted_iota(jnp.int32, shape, dim)


def ones_where(mask):
    return jnp.where(mask, 1.0, 0.0).astype(BF16)


def two_parts(x):
    high = x.astype(BF16)
    return high, (x - high.astype(F32)).astype(BF16)


def dot(a, b, dims=((1,), (0,))):
    return lax.dot_general(a, b, (dims, ((), ())), preferred_element_type=F32)


def pick_left(table, x, dims=((1,), (0,))):
    width = x.shape[1]
    both = dot(table, jnp.concatenate(two_parts(x), axis=1), dims)
    return both[:, :width] + both[:, width:]


def pick_right(x, table, dims=((1,), (0,))):
    high, low = two_parts(x)
    return dot(high, table, dims) + dot(low, table, dims)


def plate_table(owners, sources, slab):
    count = owners.shape[0] // 2
    rows = []
    for parity in (0, 1):
        own = owners[pl.ds(parity, count, stride=2), :]
        src = sources[pl.ds(parity, count, stride=2), :]
        key = iota(own.shape, 1) * 256 + src
        mine = own == slab
        first = jnp.min(jnp.where(mine, key, BIG).astype(F32), axis=1, keepdims=True)
        last = jnp.max(jnp.where(mine, key, -1).astype(F32), axis=1, keepdims=True)
        first, last = first.astype(jnp.int32), last.astype(jnp.int32)
        for value, valid in ((first, first < BIG), (last, last > first)):
            unit = value & 255
            place = jnp.where(valid, (unit & 1) * 128 + (unit >> 1), -1)
            rows.append(ones_where(iota((count, 256), 1) == place))
    return jnp.concatenate(rows, axis=0)


def window_table(owners, slab):
    count = owners.shape[0] // 2
    own = owners[pl.ds(slab, 1), :]
    units = own.shape[1]
    unit = iota((count, units), 1)
    rows = []
    for parity in (0, 1):
        mine = jnp.broadcast_to(own, (count, units)) == iota((count, units), 0) * 2 + parity
        first = jnp.min(jnp.where(mine, unit, BIG).astype(F32), axis=1, keepdims=True)
        last = jnp.max(jnp.where(mine, unit, -1).astype(F32), axis=1, keepdims=True)
        first, last = first.astype(jnp.int32), last.astype(jnp.int32)
        rows.append(ones_where(unit == first))
        rows.append(ones_where((unit == last) & (last > first)))
    spread = ones_where((iota((units, 2 * units), 1) >> 1) == iota((units, 2 * units), 0))
    return dot(jnp.concatenate(rows, axis=0), spread).astype(BF16)


def laser_heat(cells):
    count = cells.shape[1]
    rows = ones_where(iota((CX, count), 0) == jnp.broadcast_to(cells >> 7, (CX, count)))
    lanes = ones_where(iota((CY, count), 0) == jnp.broadcast_to(cells & 127, (CY, count)))
    return laser_power * dot(rows, lanes, ((1,), (1,)))


def pack_kernel(
    ids,
    owners_in,
    sources_in,
    heat_in,
    laser_in,
    out,
    deposit,
    owners,
    sources,
    heat,
    laser,
    sems,
):
    copies = [
        pltpu.make_async_copy(source, target, sems.at[n])
        for n, (source, target) in enumerate(
            (
                (owners_in, owners),
                (sources_in, sources),
                (heat_in, heat),
                (laser_in, laser),
            )
        )
    ]
    for copy in copies:
        copy.start()
    grp, slab = ids[0], ids[1]
    count = owners.shape[0] // 2
    lane = iota((CY, CY), 1)

    def store(result, pair):
        for block in range(4):
            out[:, block * 2 + pair, :] = result[block * count : (block + 1) * count]

    for n in (0, 1, 3):
        copies[n].wait()

    @pl.when(grp == 0)
    def _():
        table = plate_table(owners, sources, slab)
        deposit[...] = laser_heat(laser[...])
        copies[2].wait()
        for pair in (0, 1):
            even = heat[:, 2 * pair].reshape(CY, CY)
            odd = heat[:, 2 * pair + 1].reshape(CY, CY)
            left = jnp.where(lane < HALF, even, pltpu.roll(odd, HALF, 1))
            right = jnp.where(lane < HALF, pltpu.roll(even, HALF, 1), odd)
            store(pick_left(table, jnp.concatenate([left, right], axis=0)), pair)

    @pl.when(grp == 1)
    def _():
        table = window_table(owners, slab)
        copies[2].wait()
        row = iota((2 * CY, CY), 0)
        col = iota((2 * CY, CY), 1)
        mean = jnp.where((row >> 1) == col, 0.25, 0.0).astype(BF16)
        for pair in (0, 1):
            even = heat[:, 2 * pair].reshape(CY, CY)
            odd = heat[:, 2 * pair + 1].reshape(CY, CY)
            means = pick_right(jnp.concatenate([even, odd], axis=1), mean)
            store(pick_left(table, means), pair)


def edge_columns(x, right):
    side = jnp.where(right, iota((8, CY), 0), 1 - iota((8, CY), 0))
    lane = iota((8, CY), 1)
    pick = ones_where(((side == 0) & (lane == CY - 1)) | ((side == 1) & (lane == 0)))
    high, low = two_parts(x)
    dims = ((1,), (1,))
    return (dot(pick, high, dims) + dot(pick, low, dims))[:2]


def send_columns(ids, x, side_a, side_b, part):
    columns = edge_columns(x, ids[2] & 1 == 0)
    side_a[part : part + 1, : x.shape[0]] = columns[:1]
    side_b[part : part + 1, : x.shape[0]] = columns[1:]


def edge_row(x, top):
    return jnp.where(top, x[:, 0, :], x[:, CX - 1, :])


def edges_kernel(ids, heat, coeff, order, near, side_a, side_b):
    grp, top = ids[0], ids[1] & 1 == 1

    def send(fields):
        for part, x in enumerate(fields):
            near[part] = edge_row(x, top)
            send_columns(ids, x[...].reshape(PZ * CX, CY), side_a, side_b, part)

    @pl.when(grp == 0)
    def _():
        send((heat, coeff))

    @pl.when(grp == 1)
    def _():
        send((order.at[0], order.at[1]))


def lines_of(ids, side_a, side_b, part):
    even = ids[2] & 1 == 0
    in_a, in_b = side_a[part : part + 1], side_b[part : part + 1]
    return jnp.where(even, in_b, in_a), jnp.where(even, in_a, in_b)


def down(line, start=0, step=1):
    shape = (PZ, line.shape[1])
    at = iota(shape, 1) == iota(shape, 0) * step + start
    return jnp.sum(jnp.where(at, jnp.broadcast_to(line, shape), 0.0), axis=1, keepdims=True)


def receive_sides(ids, side_a, side_b, part):
    left, right = lines_of(ids, side_a, side_b, part)
    size = left.shape[1]
    row = iota((8, size), 0)
    left = jnp.broadcast_to(left, (8, size))
    right = jnp.broadcast_to(right, (8, size))
    both = jnp.where(row == 0, left, jnp.where(row == 1, right, 0.0))
    row, lane = iota((8, CY), 0), iota((8, CY), 1)
    place = ones_where(((row == 0) & (lane == 0)) | ((row == 1) & (lane == CY - 1)))
    return pick_right(both, place, ((0,), (0,)))


def near_row(inbox, chips, parity, part):
    start = chips + part * PZ // 8
    return inbox[1 - parity, pl.ds(start, PZ // 8)].reshape(PZ, CY)


def beside(v, above, below, sides):
    row, lane = iota((CX, CY), 0), iota((CX, CY), 1)
    up = jnp.where(row == 0, jnp.broadcast_to(above, (CX, CY)), pltpu.roll(v, 1, 0))
    down = jnp.where(row == CX - 1, jnp.broadcast_to(below, (CX, CY)), pltpu.roll(v, CX - 1, 0))
    left = jnp.where(lane == 0, sides, pltpu.roll(v, 1, 1))
    right = jnp.where(lane == CY - 1, sides, pltpu.roll(v, CY - 1, 1))
    return up, down, left, right


def harmonic(center, beside_it):
    return 2.0 * center * beside_it / (center + beside_it)


def heat_planes(
    temp, cond, order, source, result, temp_halo, cond_halo, begin=0, end=PZ
):
    temp_above, temp_below, temp_sides = temp_halo
    cond_above, cond_below, cond_sides = cond_halo

    def plane(z, from_above):
        v, k = temp[z], cond[z]
        one = pl.ds(z, 1)
        vs = beside(v, temp_above[one, :], temp_below[one, :], temp_sides[z])
        ks = beside(k, cond_above[one, :], cond_below[one, :], cond_sides[z])
        later = jnp.minimum(z + 1, PZ - 1)
        to_below = harmonic(k, cond[later]) * (temp[later] - v)
        total = to_below - from_above
        for v_next, k_next in zip(vs, ks):
            total = total + harmonic(k, k_next) * (v_next - v)
        result[z] = v + heat_dt * ((total + source(z)) / order[0, z] - order[1, z] * v)
        return to_below

    if begin == 0:
        carry = jnp.zeros((CX, CY), F32)
    else:
        before = begin - 1
        carry = harmonic(cond[before], cond[begin]) * (temp[begin] - temp[before])
    lax.fori_loop(begin, end, plane, carry, unroll=4)


def phase_planes(
    phi, sol, response, warmth, new_phi, new_sol, phi_halo, sol_halo, begin, end
):
    phi_above, phi_below, phi_sides = phi_halo
    sol_above, sol_below, sol_sides = sol_halo

    def spread(field, z, halo, weights):
        above, below, sides = halo
        f = field[z]
        one = pl.ds(z, 1)
        up, down, left, right = beside(f, above[one, :], below[one, :], sides[z])
        before = jnp.where(z > 0, field[jnp.maximum(z - 1, 0)], 0.0)
        after = jnp.where(z < PZ - 1, field[jnp.minimum(z + 1, PZ - 1)], 0.0)
        wz, wx, wy = weights
        total = (wz * ((before - f) + (after - f)) + wx * ((up - f) + (down - f))) + wy * (
            (left - f) + (right - f)
        )
        return f, total

    def plane(z, carry):
        p, spread_p = spread(phi, z, phi_halo, PHASE_WEIGHTS)
        s, spread_s = spread(sol, z, sol_halo, SOLUTE_WEIGHTS)
        drive = 0.45 * jnp.tanh(
            response[z] * (liquefying_threshold - warmth[z] - freezing_line_gradient * s)
        )
        p_new = p + phase_dt * (spread_p + 4.0 * p * (1.0 - p) * (p - 0.5 + drive))
        new_phi[z] = p_new
        new_sol[z] = s + phase_dt * spread_s - solute_reject * (p_new - p) * s
        return carry

    lax.fori_loop(begin, end, plane, 0, unroll=4)


def first_kernel(
    ids,
    deposit,
    owners,
    sources,
    inbox,
    side_a,
    side_b,
    heat,
    coeff,
    order,
    joined,
    warmth,
    near_out,
    far_out,
    side_a_out,
    side_b_out,
    above_a,
    below_a,
    sides_a,
    above_b,
    below_b,
    sides_b,
):
    grp, slab = ids[0], ids[1]
    parity = slab & 1
    far_top = parity == 0
    chips = owners.shape[0] // 2

    def arrived(pair):
        rows = []
        for core in (0, 1):
            for slot in (0, 1):
                at = 2 * slot + pair
                rows.append(
                    jnp.where(
                        parity == 0, inbox[core, :chips, at, :], inbox[core, :chips, 4 + at, :]
                    )
                )
        return jnp.concatenate(rows, axis=0)

    lane = iota((CY, CY), 1)

    @pl.when(grp == 0)
    def _():
        table = plate_table(owners, sources, slab)
        for pair in (0, 1):
            units = pick_left(table, arrived(pair), ((0,), (0,)))
            left, right = units[:CY], units[CY:]
            even = jnp.where(lane < HALF, left, pltpu.roll(right, HALF, 1))
            odd = jnp.where(lane < HALF, pltpu.roll(left, HALF, 1), right)
            for i, layer in ((2 * pair, even), (2 * pair + 1, odd)):
                layer = layer.reshape(PZ // ZQ, CX, CY)
                for q in range(PZ // ZQ):
                    joined[0, ZQ * q + i] = layer[q]

        def source(z):
            return joined[0, z] + jnp.where(z == 0, deposit[...], 0.0)

        near_above = parity == 1
        for part, (above, below, side) in enumerate(
            ((above_a, below_a, sides_a), (above_b, below_b, sides_b))
        ):
            row = near_row(inbox, chips, parity, part)
            above[...] = jnp.where(near_above, row, 0.0)
            below[...] = jnp.where(near_above, 0.0, row)
            side[...] = receive_sides(ids, side_a, side_b, part).reshape(PZ, CX, CY)
        halo_a = (above_a, below_a, sides_a)
        halo_b = (above_b, below_b, sides_b)
        first = joined.at[1]
        heat_planes(heat, coeff, order, source, first, halo_a, halo_b)
        near_out[0] = edge_row(first, near_above)
        scale = heat_dt / edge_row(order.at[0], far_top)
        for part, x in enumerate((heat, coeff, first)):
            far_out[part * PZ : (part + 1) * PZ] = edge_row(x, far_top)
        far_out[3 * PZ : 4 * PZ] = scale
        at = iota((PZ * CX, CY), 0) == iota((PZ * CX, CY), 1) * CX + jnp.where(far_top, 0, CX - 1)
        lines = lines_of(ids, side_a, side_b, 0) + lines_of(ids, side_a, side_b, 1)
        rows = iota((8, PZ * CX), 0)
        corners = jnp.zeros((8, PZ * CX), F32)
        for n, line in enumerate(lines):
            corners = jnp.where(rows == n, jnp.broadcast_to(line, corners.shape), corners)
        far_out[4 * PZ :] = pick_right(corners, ones_where(at))
        send_columns(ids, first[...].reshape(PZ * CX, CY), side_a_out, side_b_out, 0)
        send_columns(ids, scale, side_a_out, side_b_out, 1)

    @pl.when(grp == 1)
    def _():
        table = window_table(owners, slab)
        row = iota((CY, 2 * CY), 0)
        col = iota((CY, 2 * CY), 1)
        target = col & (CY - 1)
        parent = target >> 1
        next_to = jnp.clip(parent - 1 + 2 * (target & 1), 0, HALF - 1)
        at = row - (col >> 7) * HALF
        fine = (jnp.where(at == parent, 0.75, 0.0) + jnp.where(at == next_to, 0.25, 0.0)).astype(
            BF16
        )
        for pair in (0, 1):
            refined = pick_right(arrived(pair), fine)
            placed = pick_left(table, refined, ((0,), (0,)))
            for i in (0, 1):
                layer = placed[:, i * CY : (i + 1) * CY].reshape(PZ // ZQ, CX, CY)
                for q in range(PZ // ZQ):
                    warmth[ZQ * q + 2 * pair + i] = layer[q]
        for part in (0, 1):
            far_out[part * PZ : (part + 1) * PZ] = edge_row(order.at[part], far_top)


def second_kernel(
    ids,
    deposit,
    inbox,
    side_a_k,
    side_b_k,
    near,
    far,
    side_a,
    side_b,
    heat,
    coeff,
    order,
    joined,
    warmth,
    result_out,
    joined_out,
    above_a,
    below_a,
    sides_a,
    above_b,
    below_b,
    sides_b,
    result,
    both,
    sems,
):
    grp, parity = ids[0], ids[1] & 1
    even = parity == 0
    chips = inbox.shape[1] - 2 * PZ // 8
    parts = RESULT_PARTS
    size = PZ // parts
    halo_a = (above_a, below_a, sides_a)
    halo_b = (above_b, below_b, sides_b)

    def place(above, below, near_values, far_values):
        above[...] = jnp.where(even, far_values, near_values)
        below[...] = jnp.where(even, near_values, far_values)

    def write(source, target, n):
        copy = pltpu.make_async_copy(source, target, sems.at[n])
        copy.start()
        return copy

    @pl.when(grp == 0)
    def _():
        copies = [write(joined.at[0], joined_out.at[0, 0], 0)]
        t_far, k_far, partial, scale_far = [far[n * PZ : (n + 1) * PZ] for n in range(4)]
        t_here, k_here = edge_row(heat, even), edge_row(coeff, even)
        scale = heat_dt / edge_row(order.at[0], even)
        crossing = harmonic(k_here, k_far) * (t_far - t_here)
        first = both.at[0]
        first[...] = joined[1]
        for top, row in ((True, 0), (False, CX - 1)):
            add = jnp.where(even == top, scale * crossing, 0.0)
            first[:, row, :] = first[:, row, :] + add
        copies.append(write(first, joined_out.at[0, 1], 1))
        place(above_a, below_a, near[1 - parity, 0], partial - scale_far * crossing)
        place(above_b, below_b, near_row(inbox, chips, parity, 1), k_far)
        sides_a[...] = receive_sides(ids, side_a, side_b, 0).reshape(PZ, CX, CY)
        sides_b[...] = receive_sides(ids, side_a_k, side_b_k, 1).reshape(PZ, CX, CY)
        row = jnp.where(even, 0, CX - 1)
        lane = iota((PZ, CY), 1)
        add = jnp.zeros((PZ, CY), F32)
        temps, conds = lines_of(ids, side_a_k, side_b_k, 0), lines_of(ids, side_a_k, side_b_k, 1)
        scales = lines_of(ids, side_a, side_b, 1)
        for n, end in enumerate((0, CY - 1)):
            t, k = down(temps[n], row, CX), down(conds[n], row, CX)
            corner = 4 * PZ + n
            t_next, k_next = down(far[corner : corner + 1]), down(far[corner + 2 : corner + 3])
            shared = 2.0 * k * k_next / jnp.maximum(k + k_next, 1e-6)
            change = down(scales[n][:, :CY]) * shared * (t_next - t)
            add = add + jnp.where(lane == end, change, 0.0)
        for top, row in ((True, 0), (False, CX - 1)):
            sides_a[:, row, :] = sides_a[:, row, :] + jnp.where(even == top, add, 0.0)

        def source(z):
            return joined[0, z] + jnp.where(z == 0, deposit[...], 0.0)

        for n in range(parts):
            begin, end = n * size, (n + 1) * size
            heat_planes(first, coeff, order, source, result, halo_a, halo_b, begin, end)
            planes = pl.ds(begin, size)
            copies.append(write(result.at[planes], result_out.at[0, planes], 2 + n))
        for copy in copies:
            copy.wait()

    @pl.when(grp == 1)
    def _():
        copies = [write(warmth, result_out.at[0], 0)]
        for part, (above, below, side) in enumerate((halo_a, halo_b)):
            far_values = far[part * PZ : (part + 1) * PZ]
            place(above, below, near_row(inbox, chips, parity, part), far_values)
            side[...] = receive_sides(ids, side_a_k, side_b_k, part).reshape(PZ, CX, CY)
        for n in range(parts):
            begin, end = n * size, (n + 1) * size
            phase_planes(
                order.at[0],
                order.at[1],
                coeff,
                warmth,
                both.at[0],
                both.at[1],
                halo_a,
                halo_b,
                begin,
                end,
            )
            planes = pl.ds(begin, size)
            copies.append(write(both.at[:, planes], joined_out.at[0, :, planes], 2 + n))
        for copy in copies:
            copy.wait()


RESULT_PARTS = 4
HBM = pl.BlockSpec(memory_space=pltpu.HBM)
SMEM = pl.BlockSpec(memory_space=pltpu.SMEM)
VMEM = pl.BlockSpec(memory_space=pltpu.VMEM)


def located(kernel, slabs, cols):
    def body(number, *refs):
        n = number[0]
        ids = lax.div(n, slabs * cols), lax.rem(lax.div(n, cols), slabs), lax.rem(n, cols)
        kernel(ids, *refs)

    return body


def call(kernel, specs, outs, scratch=(), out_space=VMEM, limit=24 << 20):
    shapes = [jax.ShapeDtypeStruct(shape, F32) for shape in outs]
    single = len(shapes) == 1
    return pl.pallas_call(
        kernel,
        out_shape=shapes[0] if single else shapes,
        in_specs=list(specs),
        out_specs=out_space if single else [out_space] * len(shapes),
        scratch_shapes=list(scratch),
        compiler_params=pltpu.CompilerParams(vmem_limit_bytes=limit),
    )


def halo_scratch():
    one = [
        pltpu.VMEM((PZ, CY), F32),
        pltpu.VMEM((PZ, CY), F32),
        pltpu.VMEM((PZ, CX, CY), F32),
    ]
    return one + one


def swaps(starts):
    return [pair for i in starts for pair in ((i, i + 1), (i + 1, i))]


def per_device(heat_field, coeff, order, block_owner, block_source, laser_cells):
    slabs, cols = lax.axis_size("slab"), lax.axis_size("col")
    chips = slabs // 2
    grp = lax.axis_index("grp")
    number = lax.axis_index(("grp", "slab", "col")).reshape(1)

    def place(kernel, *specs, **options):
        return call(located(kernel, slabs, cols), *specs, **options)

    near_pairs = [[2 * i, 2 * i + 1] for i in range(chips)]
    same_core = [[2 * i + k for i in range(chips)] for k in range(2)]
    far_swap = swaps(range(1, slabs - 1, 2))
    side_a_swap, side_b_swap = swaps(range(0, cols - 1, 2)), swaps(range(1, cols - 1, 2))
    heat, conduct, orders = heat_field[0], coeff[0], order[0]
    owners, sources, laser = block_owner[0, :, :, 0], block_source[0], laser_cells[0]

    slab_table = pltpu.VMEM(owners.shape, jnp.int32)
    outbox, deposit = place(
        pack_kernel,
        [SMEM] + [HBM] * 4,
        [(chips, 8, CY), (CX, CY)],
        [
            slab_table,
            slab_table,
            pltpu.VMEM((PZ // ZQ, ZQ, CX, CY), F32),
            pltpu.VMEM(laser.shape, jnp.int32),
            pltpu.SemaphoreType.DMA((4,)),
        ],
        limit=60 << 20,
    )(number, owners, sources, heat.reshape(PZ // ZQ, ZQ, CX, CY), laser)
    moved = lax.all_to_all(
        outbox, "slab", split_axis=0, concat_axis=0, tiled=True, axis_index_groups=same_core
    )
    crossed = lax.all_gather(moved, "grp")
    crossed = lax.dynamic_index_in_dim(crossed, 1 - grp, 0, keepdims=False)

    rows, column, field = (2, PZ, CY), (2, PZ * CX), (PZ, CX, CY)
    near, side_a, side_b = place(edges_kernel, [SMEM] + [VMEM] * 3, [rows, column, column])(
        number, heat, conduct, orders
    )
    side_a = lax.ppermute(side_a, "col", side_a_swap)
    side_b = lax.ppermute(side_b, "col", side_b_swap)
    inbox = lax.all_gather(
        jnp.concatenate([crossed, near.reshape(-1, 8, CY)]), "slab", axis_index_groups=near_pairs
    )
    joined, warmth, near_1, far_1, side_a_1, side_b_1 = place(
        first_kernel,
        [SMEM] + [VMEM] * 9,
        [(2,) + field, field, (1, PZ, CY), (4 * PZ + 8, CY), column, column],
        halo_scratch(),
    )(number, deposit, owners, sources, inbox, side_a, side_b, heat, conduct, orders)
    far_1 = lax.ppermute(far_1, "slab", far_swap)
    side_a_1 = lax.ppermute(side_a_1, "col", side_a_swap)
    side_b_1 = lax.ppermute(side_b_1, "col", side_b_swap)
    near_1 = lax.all_gather(near_1, "slab", axis_index_groups=near_pairs)
    return place(
        second_kernel,
        [SMEM] + [VMEM] * 13,
        [(1,) + field, (1, 2) + field],
        halo_scratch()
        + [
            pltpu.VMEM(field, F32),
            pltpu.VMEM((2,) + field, F32),
            pltpu.SemaphoreType.DMA((2 + RESULT_PARTS,)),
        ],
        HBM,
    )(
        number,
        deposit,
        inbox,
        side_a,
        side_b,
        near_1,
        far_1,
        side_a_1,
        side_b_1,
        heat,
        conduct,
        orders,
        joined,
        warmth,
    )


def solution(mesh):
    placed = (
        P("grp", None, "slab", "col"),
        P("grp", None, "slab", "col"),
        P("grp", None, None, "slab", "col"),
        P("col", None, None, None),
        P("col", None, None),
        P("slab", "col", None),
    )
    return jax.shard_map(
        per_device,
        mesh=mesh,
        in_specs=placed,
        out_specs=(P("grp", None, "slab", "col"), P("grp", None, None, "slab", "col")),
        check_vma=False,
    )
```

```python
import jax
import jax.numpy as jnp
from jax import lax
from jax.experimental import pallas as pl
from jax.experimental.pallas import tpu as pltpu
from jax.sharding import PartitionSpec as P

PZ = 32
ZQ = 4
CX = 16
CY = 128
HALF = CY // 2

heat_dt = 0.07
phase_dt = 0.1
laser_power = 3.0
liquefying_threshold = 0.3
freezing_line_gradient = 0.5
solute_reject = 0.5
PHASE_WEIGHTS = (1.0, 1.3, 0.7)
SOLUTE_WEIGHTS = (0.8, 0.8, 0.8)

F32 = jnp.float32
BF16 = jnp.bfloat16
BIG = 1 << 20


def iota(shape, dim):
    return lax.broadcasted_iota(jnp.int32, shape, dim)


def ones_where(mask):
    return jnp.where(mask, 1.0, 0.0).astype(BF16)


def two_parts(x):
    high = x.astype(BF16)
    return high, (x - high.astype(F32)).astype(BF16)


def dot(a, b, dims=((1,), (0,))):
    return lax.dot_general(a, b, (dims, ((), ())), preferred_element_type=F32)


def pick_left(table, x, dims=((1,), (0,))):
    width = x.shape[1]
    both = dot(table, jnp.concatenate(two_parts(x), axis=1), dims)
    return both[:, :width] + both[:, width:]


def pick_right(x, table, dims=((1,), (0,))):
    high, low = two_parts(x)
    return dot(high, table, dims) + dot(low, table, dims)


def plate_table(owners, sources, slab):
    count = owners.shape[0] // 2
    rows = []
    for parity in (0, 1):
        own = owners[pl.ds(parity, count, stride=2), :]
        src = sources[pl.ds(parity, count, stride=2), :]
        key = iota(own.shape, 1) * 256 + src
        mine = own == slab
        first = jnp.min(jnp.where(mine, key, BIG).astype(F32), axis=1, keepdims=True)
        last = jnp.max(jnp.where(mine, key, -1).astype(F32), axis=1, keepdims=True)
        first, last = first.astype(jnp.int32), last.astype(jnp.int32)
        for value, valid in ((first, first < BIG), (last, last > first)):
            unit = value & 255
            place = jnp.where(valid, (unit & 1) * 128 + (unit >> 1), -1)
            rows.append(ones_where(iota((count, 256), 1) == place))
    return jnp.concatenate(rows, axis=0)


def window_table(owners, slab):
    count = owners.shape[0] // 2
    own = owners[pl.ds(slab, 1), :]
    units = own.shape[1]
    unit = iota((count, units), 1)
    rows = []
    for parity in (0, 1):
        mine = jnp.broadcast_to(own, (count, units)) == iota((count, units), 0) * 2 + parity
        first = jnp.min(jnp.where(mine, unit, BIG).astype(F32), axis=1, keepdims=True)
        last = jnp.max(jnp.where(mine, unit, -1).astype(F32), axis=1, keepdims=True)
        first, last = first.astype(jnp.int32), last.astype(jnp.int32)
        rows.append(ones_where(unit == first))
        rows.append(ones_where((unit == last) & (last > first)))
    spread = ones_where((iota((units, 2 * units), 1) >> 1) == iota((units, 2 * units), 0))
    return dot(jnp.concatenate(rows, axis=0), spread).astype(BF16)


def laser_heat(cells):
    count = cells.shape[1]
    rows = ones_where(iota((CX, count), 0) == jnp.broadcast_to(cells >> 7, (CX, count)))
    lanes = ones_where(iota((CY, count), 0) == jnp.broadcast_to(cells & 127, (CY, count)))
    return laser_power * dot(rows, lanes, ((1,), (1,)))


def pack_kernel(
    ids,
    owners_in,
    sources_in,
    heat_in,
    laser_in,
    out,
    deposit,
    owners,
    sources,
    heat,
    laser,
    sems,
):
    copies = [
        pltpu.make_async_copy(source, target, sems.at[n])
        for n, (source, target) in enumerate(
            (
                (owners_in, owners),
                (sources_in, sources),
                (heat_in, heat),
                (laser_in, laser),
            )
        )
    ]
    for copy in copies:
        copy.start()
    grp, slab = ids[0], ids[1]
    count = owners.shape[0] // 2
    lane = iota((CY, CY), 1)

    def store(result, pair):
        for block in range(4):
            at = (block & 1) * 2 + pair
            out[1 - grp, :, block >> 1, at, :] = result[block * count : (block + 1) * count]

    for n in (0, 1, 3):
        copies[n].wait()

    @pl.when(grp == 0)
    def _():
        table = plate_table(owners, sources, slab)
        deposit[...] = laser_heat(laser[...])
        copies[2].wait()
        for pair in (0, 1):
            even = heat[:, 2 * pair].reshape(CY, CY)
            odd = heat[:, 2 * pair + 1].reshape(CY, CY)
            left = jnp.where(lane < HALF, even, pltpu.roll(odd, HALF, 1))
            right = jnp.where(lane < HALF, pltpu.roll(even, HALF, 1), odd)
            store(pick_left(table, jnp.concatenate([left, right], axis=0)), pair)

    @pl.when(grp == 1)
    def _():
        table = window_table(owners, slab)
        copies[2].wait()
        row = iota((2 * CY, CY), 0)
        col = iota((2 * CY, CY), 1)
        mean = jnp.where((row >> 1) == col, 0.25, 0.0).astype(BF16)
        for pair in (0, 1):
            even = heat[:, 2 * pair].reshape(CY, CY)
            odd = heat[:, 2 * pair + 1].reshape(CY, CY)
            means = pick_right(jnp.concatenate([even, odd], axis=1), mean)
            store(pick_left(table, means), pair)


def edge_columns(x, right):
    side = jnp.where(right, iota((8, CY), 0), 1 - iota((8, CY), 0))
    lane = iota((8, CY), 1)
    pick = ones_where(((side == 0) & (lane == CY - 1)) | ((side == 1) & (lane == 0)))
    high, low = two_parts(x)
    dims = ((1,), (1,))
    return (dot(pick, high, dims) + dot(pick, low, dims))[:2]


def send_columns(ids, x, side_a, side_b, part):
    columns = edge_columns(x, ids[2] & 1 == 0)
    side_a[part : part + 1, : x.shape[0]] = columns[:1]
    side_b[part : part + 1, : x.shape[0]] = columns[1:]


def edge_row(x, top):
    return jnp.where(top, x[:, 0, :], x[:, CX - 1, :])


def edges_kernel(ids, heat, coeff, order, near, side_a, side_b):
    grp, top = ids[0], ids[1] & 1 == 1

    def send(fields):
        for part, x in enumerate(fields):
            near[part] = edge_row(x, top)
            send_columns(ids, x[...].reshape(PZ * CX, CY), side_a, side_b, part)

    @pl.when(grp == 0)
    def _():
        send((heat, coeff))

    @pl.when(grp == 1)
    def _():
        send((order.at[0], order.at[1]))


def lines_of(ids, side_a, side_b, part):
    even = ids[2] & 1 == 0
    in_a, in_b = side_a[part : part + 1], side_b[part : part + 1]
    return jnp.where(even, in_b, in_a), jnp.where(even, in_a, in_b)


def down(line, start=0, step=1):
    shape = (PZ, line.shape[1])
    at = iota(shape, 1) == iota(shape, 0) * step + start
    return jnp.sum(jnp.where(at, jnp.broadcast_to(line, shape), 0.0), axis=1, keepdims=True)


def receive_sides(ids, side_a, side_b, part):
    left, right = lines_of(ids, side_a, side_b, part)
    size = left.shape[1]
    row = iota((8, size), 0)
    left = jnp.broadcast_to(left, (8, size))
    right = jnp.broadcast_to(right, (8, size))
    both = jnp.where(row == 0, left, jnp.where(row == 1, right, 0.0))
    row, lane = iota((8, CY), 0), iota((8, CY), 1)
    place = ones_where(((row == 0) & (lane == 0)) | ((row == 1) & (lane == CY - 1)))
    return pick_right(both, place, ((0,), (0,)))


def beside(v, above, below, sides):
    row, lane = iota((CX, CY), 0), iota((CX, CY), 1)
    up = jnp.where(row == 0, jnp.broadcast_to(above, (CX, CY)), pltpu.roll(v, 1, 0))
    down = jnp.where(row == CX - 1, jnp.broadcast_to(below, (CX, CY)), pltpu.roll(v, CX - 1, 0))
    left = jnp.where(lane == 0, sides, pltpu.roll(v, 1, 1))
    right = jnp.where(lane == CY - 1, sides, pltpu.roll(v, CY - 1, 1))
    return up, down, left, right


def harmonic(center, beside_it):
    return 2.0 * center * beside_it / (center + beside_it)


def heat_planes(
    temp, cond, order, source, result, temp_halo, cond_halo, begin=0, end=PZ
):
    temp_above, temp_below, temp_sides = temp_halo
    cond_above, cond_below, cond_sides = cond_halo

    def plane(z, from_above):
        v, k = temp[z], cond[z]
        one = pl.ds(z, 1)
        vs = beside(v, temp_above[one, :], temp_below[one, :], temp_sides[z])
        ks = beside(k, cond_above[one, :], cond_below[one, :], cond_sides[z])
        later = jnp.minimum(z + 1, PZ - 1)
        to_below = harmonic(k, cond[later]) * (temp[later] - v)
        total = to_below - from_above
        for v_next, k_next in zip(vs, ks):
            total = total + harmonic(k, k_next) * (v_next - v)
        result[z] = v + heat_dt * ((total + source(z)) / order[0, z] - order[1, z] * v)
        return to_below

    if begin == 0:
        carry = jnp.zeros((CX, CY), F32)
    else:
        before = begin - 1
        carry = harmonic(cond[before], cond[begin]) * (temp[begin] - temp[before])
    lax.fori_loop(begin, end, plane, carry, unroll=4)


def phase_planes(
    phi, sol, response, warmth, new_phi, new_sol, phi_halo, sol_halo, begin, end
):
    phi_above, phi_below, phi_sides = phi_halo
    sol_above, sol_below, sol_sides = sol_halo

    def spread(field, z, halo, weights):
        above, below, sides = halo
        f = field[z]
        one = pl.ds(z, 1)
        up, down, left, right = beside(f, above[one, :], below[one, :], sides[z])
        before = jnp.where(z > 0, field[jnp.maximum(z - 1, 0)], 0.0)
        after = jnp.where(z < PZ - 1, field[jnp.minimum(z + 1, PZ - 1)], 0.0)
        wz, wx, wy = weights
        total = (wz * ((before - f) + (after - f)) + wx * ((up - f) + (down - f))) + wy * (
            (left - f) + (right - f)
        )
        return f, total

    def plane(z, carry):
        p, spread_p = spread(phi, z, phi_halo, PHASE_WEIGHTS)
        s, spread_s = spread(sol, z, sol_halo, SOLUTE_WEIGHTS)
        drive = 0.45 * jnp.tanh(
            response[z] * (liquefying_threshold - warmth[z] - freezing_line_gradient * s)
        )
        p_new = p + phase_dt * (spread_p + 4.0 * p * (1.0 - p) * (p - 0.5 + drive))
        new_phi[z] = p_new
        new_sol[z] = s + phase_dt * spread_s - solute_reject * (p_new - p) * s
        return carry

    lax.fori_loop(begin, end, plane, 0, unroll=4)


def first_kernel(
    ids,
    deposit,
    owners,
    sources,
    inbox,
    near,
    side_a,
    side_b,
    heat,
    coeff,
    order,
    joined,
    warmth,
    near_out,
    far_out,
    side_a_out,
    side_b_out,
    above_a,
    below_a,
    sides_a,
    above_b,
    below_b,
    sides_b,
):
    grp, slab = ids[0], ids[1]
    parity = slab & 1
    far_top = parity == 0

    def arrived(pair):
        blocks = [(side, 2 * slot + pair) for side in (0, 1) for slot in (0, 1)]
        return jnp.concatenate([inbox[1 - grp, :, side, at, :] for side, at in blocks], axis=0)

    lane = iota((CY, CY), 1)

    @pl.when(grp == 0)
    def _():
        table = plate_table(owners, sources, slab)
        for pair in (0, 1):
            units = pick_left(table, arrived(pair), ((0,), (0,)))
            left, right = units[:CY], units[CY:]
            even = jnp.where(lane < HALF, left, pltpu.roll(right, HALF, 1))
            odd = jnp.where(lane < HALF, pltpu.roll(left, HALF, 1), right)
            for i, layer in ((2 * pair, even), (2 * pair + 1, odd)):
                layer = layer.reshape(PZ // ZQ, CX, CY)
                for q in range(PZ // ZQ):
                    joined[0, ZQ * q + i] = layer[q]

        def source(z):
            return joined[0, z] + jnp.where(z == 0, deposit[...], 0.0)

        near_above = parity == 1
        for part, (above, below, side) in enumerate(
            ((above_a, below_a, sides_a), (above_b, below_b, sides_b))
        ):
            row = near[1 - parity, part]
            above[...] = jnp.where(near_above, row, 0.0)
            below[...] = jnp.where(near_above, 0.0, row)
            side[...] = receive_sides(ids, side_a, side_b, part).reshape(PZ, CX, CY)
        halo_a = (above_a, below_a, sides_a)
        halo_b = (above_b, below_b, sides_b)
        first = joined.at[1]
        heat_planes(heat, coeff, order, source, first, halo_a, halo_b)
        near_out[0] = edge_row(first, near_above)
        scale = heat_dt / edge_row(order.at[0], far_top)
        for part, x in enumerate((heat, coeff, first)):
            far_out[part * PZ : (part + 1) * PZ] = edge_row(x, far_top)
        far_out[3 * PZ : 4 * PZ] = scale
        at = iota((PZ * CX, CY), 0) == iota((PZ * CX, CY), 1) * CX + jnp.where(far_top, 0, CX - 1)
        lines = lines_of(ids, side_a, side_b, 0) + lines_of(ids, side_a, side_b, 1)
        rows = iota((8, PZ * CX), 0)
        corners = jnp.zeros((8, PZ * CX), F32)
        for n, line in enumerate(lines):
            corners = jnp.where(rows == n, jnp.broadcast_to(line, corners.shape), corners)
        far_out[4 * PZ :] = pick_right(corners, ones_where(at))
        send_columns(ids, first[...].reshape(PZ * CX, CY), side_a_out, side_b_out, 0)
        send_columns(ids, scale, side_a_out, side_b_out, 1)

    @pl.when(grp == 1)
    def _():
        table = window_table(owners, slab)
        row = iota((CY, 2 * CY), 0)
        col = iota((CY, 2 * CY), 1)
        target = col & (CY - 1)
        parent = target >> 1
        next_to = jnp.clip(parent - 1 + 2 * (target & 1), 0, HALF - 1)
        at = row - (col >> 7) * HALF
        fine = (jnp.where(at == parent, 0.75, 0.0) + jnp.where(at == next_to, 0.25, 0.0)).astype(
            BF16
        )
        for pair in (0, 1):
            refined = pick_right(arrived(pair), fine)
            placed = pick_left(table, refined, ((0,), (0,)))
            for i in (0, 1):
                layer = placed[:, i * CY : (i + 1) * CY].reshape(PZ // ZQ, CX, CY)
                for q in range(PZ // ZQ):
                    warmth[ZQ * q + 2 * pair + i] = layer[q]
        for part in (0, 1):
            far_out[part * PZ : (part + 1) * PZ] = edge_row(order.at[part], far_top)


def second_kernel(
    ids,
    deposit,
    near_k,
    side_a_k,
    side_b_k,
    near,
    far,
    side_a,
    side_b,
    heat,
    coeff,
    order,
    joined,
    warmth,
    result_out,
    joined_out,
    above_a,
    below_a,
    sides_a,
    above_b,
    below_b,
    sides_b,
    result,
    both,
    sems,
):
    grp, parity = ids[0], ids[1] & 1
    even = parity == 0
    parts = RESULT_PARTS
    size = PZ // parts
    halo_a = (above_a, below_a, sides_a)
    halo_b = (above_b, below_b, sides_b)

    def place(above, below, near_values, far_values):
        above[...] = jnp.where(even, far_values, near_values)
        below[...] = jnp.where(even, near_values, far_values)

    def write(source, target, n):
        copy = pltpu.make_async_copy(source, target, sems.at[n])
        copy.start()
        return copy

    @pl.when(grp == 0)
    def _():
        copies = [write(joined.at[0], joined_out.at[0, 0], 0)]
        t_far, k_far, partial, scale_far = [far[n * PZ : (n + 1) * PZ] for n in range(4)]
        t_here, k_here = edge_row(heat, even), edge_row(coeff, even)
        scale = heat_dt / edge_row(order.at[0], even)
        crossing = harmonic(k_here, k_far) * (t_far - t_here)
        first = both.at[0]
        first[...] = joined[1]
        for top, row in ((True, 0), (False, CX - 1)):
            add = jnp.where(even == top, scale * crossing, 0.0)
            first[:, row, :] = first[:, row, :] + add
        copies.append(write(first, joined_out.at[0, 1], 1))
        place(above_a, below_a, near[1 - parity, 0], partial - scale_far * crossing)
        place(above_b, below_b, near_k[1 - parity, 1], k_far)
        sides_a[...] = receive_sides(ids, side_a, side_b, 0).reshape(PZ, CX, CY)
        sides_b[...] = receive_sides(ids, side_a_k, side_b_k, 1).reshape(PZ, CX, CY)
        row = jnp.where(even, 0, CX - 1)
        lane = iota((PZ, CY), 1)
        add = jnp.zeros((PZ, CY), F32)
        temps, conds = lines_of(ids, side_a_k, side_b_k, 0), lines_of(ids, side_a_k, side_b_k, 1)
        scales = lines_of(ids, side_a, side_b, 1)
        for n, end in enumerate((0, CY - 1)):
            t, k = down(temps[n], row, CX), down(conds[n], row, CX)
            corner = 4 * PZ + n
            t_next, k_next = down(far[corner : corner + 1]), down(far[corner + 2 : corner + 3])
            shared = 2.0 * k * k_next / jnp.maximum(k + k_next, 1e-6)
            change = down(scales[n][:, :CY]) * shared * (t_next - t)
            add = add + jnp.where(lane == end, change, 0.0)
        for top, row in ((True, 0), (False, CX - 1)):
            sides_a[:, row, :] = sides_a[:, row, :] + jnp.where(even == top, add, 0.0)

        def source(z):
            return joined[0, z] + jnp.where(z == 0, deposit[...], 0.0)

        for n in range(parts):
            begin, end = n * size, (n + 1) * size
            heat_planes(first, coeff, order, source, result, halo_a, halo_b, begin, end)
            planes = pl.ds(begin, size)
            copies.append(write(result.at[planes], result_out.at[0, planes], 2 + n))
        for copy in copies:
            copy.wait()

    @pl.when(grp == 1)
    def _():
        copies = [write(warmth, result_out.at[0], 0)]
        for part, (above, below, side) in enumerate((halo_a, halo_b)):
            far_values = far[part * PZ : (part + 1) * PZ]
            place(above, below, near_k[1 - parity, part], far_values)
            side[...] = receive_sides(ids, side_a_k, side_b_k, part).reshape(PZ, CX, CY)
        for n in range(parts):
            begin, end = n * size, (n + 1) * size
            phase_planes(
                order.at[0],
                order.at[1],
                coeff,
                warmth,
                both.at[0],
                both.at[1],
                halo_a,
                halo_b,
                begin,
                end,
            )
            planes = pl.ds(begin, size)
            copies.append(write(both.at[:, planes], joined_out.at[0, :, planes], 2 + n))
        for copy in copies:
            copy.wait()


RESULT_PARTS = 4
HBM = pl.BlockSpec(memory_space=pltpu.HBM)
SMEM = pl.BlockSpec(memory_space=pltpu.SMEM)
VMEM = pl.BlockSpec(memory_space=pltpu.VMEM)


def located(kernel, slabs, cols):
    def body(number, *refs):
        n = number[0]
        ids = lax.div(n, slabs * cols), lax.rem(lax.div(n, cols), slabs), lax.rem(n, cols)
        kernel(ids, *refs)

    return body


def call(kernel, specs, outs, scratch=(), out_space=VMEM, limit=24 << 20):
    shapes = [jax.ShapeDtypeStruct(shape, F32) for shape in outs]
    single = len(shapes) == 1
    return pl.pallas_call(
        kernel,
        out_shape=shapes[0] if single else shapes,
        in_specs=list(specs),
        out_specs=out_space if single else [out_space] * len(shapes),
        scratch_shapes=list(scratch),
        compiler_params=pltpu.CompilerParams(vmem_limit_bytes=limit),
    )


def halo_scratch():
    one = [
        pltpu.VMEM((PZ, CY), F32),
        pltpu.VMEM((PZ, CY), F32),
        pltpu.VMEM((PZ, CX, CY), F32),
    ]
    return one + one


def swaps(starts):
    return [pair for i in starts for pair in ((i, i + 1), (i + 1, i))]


def per_device(heat_field, coeff, order, block_owner, block_source, laser_cells):
    slabs, cols = lax.axis_size("slab"), lax.axis_size("col")
    chips = slabs // 2
    grp = lax.axis_index("grp")
    number = lax.axis_index(("grp", "slab", "col")).reshape(1)

    def place(kernel, *specs, **options):
        return call(located(kernel, slabs, cols), *specs, **options)

    near_pairs = [[2 * i, 2 * i + 1] for i in range(chips)]
    far_swap = swaps(range(1, slabs - 1, 2))
    side_a_swap, side_b_swap = swaps(range(0, cols - 1, 2)), swaps(range(1, cols - 1, 2))
    heat, conduct, orders = heat_field[0], coeff[0], order[0]
    owners, sources, laser = block_owner[0, :, :, 0], block_source[0], laser_cells[0]

    slab_table = pltpu.VMEM(owners.shape, jnp.int32)
    outbox, deposit = place(
        pack_kernel,
        [SMEM] + [HBM] * 4,
        [(2, chips, 2, 4, CY), (CX, CY)],
        [
            slab_table,
            slab_table,
            pltpu.VMEM((PZ // ZQ, ZQ, CX, CY), F32),
            pltpu.VMEM(laser.shape, jnp.int32),
            pltpu.SemaphoreType.DMA((4,)),
        ],
        limit=60 << 20,
    )(number, owners, sources, heat.reshape(PZ // ZQ, ZQ, CX, CY), laser)
    inbox = lax.all_to_all(
        outbox.reshape(-1, 4, CY), ("grp", "slab"), split_axis=0, concat_axis=0, tiled=True
    ).reshape(outbox.shape)
    rows, column, field = (2, PZ, CY), (2, PZ * CX), (PZ, CX, CY)
    near, side_a, side_b = place(edges_kernel, [SMEM] + [VMEM] * 3, [rows, column, column])(
        number, heat, conduct, orders
    )
    side_a = lax.ppermute(side_a, "col", side_a_swap)
    side_b = lax.ppermute(side_b, "col", side_b_swap)
    near = lax.all_gather(near, "slab", axis_index_groups=near_pairs)
    joined, warmth, near_1, far_1, side_a_1, side_b_1 = place(
        first_kernel,
        [SMEM] + [VMEM] * 10,
        [(2,) + field, field, (1, PZ, CY), (4 * PZ + 8, CY), column, column],
        halo_scratch(),
    )(number, deposit, owners, sources, inbox, near, side_a, side_b, heat, conduct, orders)
    far_1 = lax.ppermute(far_1, "slab", far_swap)
    side_a_1 = lax.ppermute(side_a_1, "col", side_a_swap)
    side_b_1 = lax.ppermute(side_b_1, "col", side_b_swap)
    near_1 = lax.all_gather(near_1, "slab", axis_index_groups=near_pairs)
    return place(
        second_kernel,
        [SMEM] + [VMEM] * 13,
        [(1,) + field, (1, 2) + field],
        halo_scratch()
        + [
            pltpu.VMEM(field, F32),
            pltpu.VMEM((2,) + field, F32),
            pltpu.SemaphoreType.DMA((2 + RESULT_PARTS,)),
        ],
        HBM,
    )(
        number,
        deposit,
        near,
        side_a,
        side_b,
        near_1,
        far_1,
        side_a_1,
        side_b_1,
        heat,
        conduct,
        orders,
        joined,
        warmth,
    )


def solution(mesh):
    placed = (
        P("grp", None, "slab", "col"),
        P("grp", None, "slab", "col"),
        P("grp", None, None, "slab", "col"),
        P("col", None, None, None),
        P("col", None, None),
        P("slab", "col", None),
    )
    return jax.shard_map(
        per_device,
        mesh=mesh,
        in_specs=placed,
        out_specs=(P("grp", None, "slab", "col"), P("grp", None, None, "slab", "col")),
        check_vma=False,
    )
```

```python
import jax
import jax.numpy as jnp
from jax import lax
from jax.experimental import pallas as pl
from jax.experimental.pallas import tpu as pltpu
from jax.sharding import PartitionSpec as P

PZ = 32
ZQ = 4
CX = 16
CY = 128
HALF = CY // 2

heat_dt = 0.07
phase_dt = 0.1
laser_power = 3.0
liquefying_threshold = 0.3
freezing_line_gradient = 0.5
solute_reject = 0.5
PHASE_WEIGHTS = (1.0, 1.3, 0.7)
SOLUTE_WEIGHTS = (0.8, 0.8, 0.8)

F32 = jnp.float32
BF16 = jnp.bfloat16
BIG = 1 << 20


def iota(shape, dim):
    return lax.broadcasted_iota(jnp.int32, shape, dim)


def ones_where(mask):
    return jnp.where(mask, 1.0, 0.0).astype(BF16)


def two_parts(x):
    high = x.astype(BF16)
    return high, (x - high.astype(F32)).astype(BF16)


def dot(a, b, dims=((1,), (0,))):
    return lax.dot_general(a, b, (dims, ((), ())), preferred_element_type=F32)


def pick_left(table, x, dims=((1,), (0,))):
    width = x.shape[1]
    both = dot(table, jnp.concatenate(two_parts(x), axis=1), dims)
    return both[:, :width] + both[:, width:]


def pick_right(x, table, dims=((1,), (0,))):
    high, low = two_parts(x)
    return dot(high, table, dims) + dot(low, table, dims)


def plate_table(owners, sources, slab):
    count = owners.shape[0] // 2
    rows = []
    for parity in (0, 1):
        own = owners[pl.ds(parity, count, stride=2), :]
        src = sources[pl.ds(parity, count, stride=2), :]
        key = iota(own.shape, 1) * 256 + src
        mine = own == slab
        first = jnp.min(jnp.where(mine, key, BIG).astype(F32), axis=1, keepdims=True)
        last = jnp.max(jnp.where(mine, key, -1).astype(F32), axis=1, keepdims=True)
        first, last = first.astype(jnp.int32), last.astype(jnp.int32)
        for value, valid in ((first, first < BIG), (last, last > first)):
            unit = value & 255
            place = jnp.where(valid, (unit & 1) * 128 + (unit >> 1), -1)
            rows.append(ones_where(iota((count, 256), 1) == place))
    return jnp.concatenate(rows, axis=0)


def window_table(owners, slab):
    count = owners.shape[0] // 2
    own = owners[pl.ds(slab, 1), :]
    units = own.shape[1]
    unit = iota((count, units), 1)
    rows = []
    for parity in (0, 1):
        mine = jnp.broadcast_to(own, (count, units)) == iota((count, units), 0) * 2 + parity
        first = jnp.min(jnp.where(mine, unit, BIG).astype(F32), axis=1, keepdims=True)
        last = jnp.max(jnp.where(mine, unit, -1).astype(F32), axis=1, keepdims=True)
        first, last = first.astype(jnp.int32), last.astype(jnp.int32)
        rows.append(ones_where(unit == first))
        rows.append(ones_where((unit == last) & (last > first)))
    spread = ones_where((iota((units, 2 * units), 1) >> 1) == iota((units, 2 * units), 0))
    return dot(jnp.concatenate(rows, axis=0), spread).astype(BF16)


def laser_heat(cells):
    count = cells.shape[1]
    rows = ones_where(iota((CX, count), 0) == jnp.broadcast_to(cells >> 7, (CX, count)))
    lanes = ones_where(iota((CY, count), 0) == jnp.broadcast_to(cells & 127, (CY, count)))
    return laser_power * dot(rows, lanes, ((1,), (1,)))


def pack_kernel(
    ids,
    owners_in,
    sources_in,
    heat_in,
    laser_in,
    out,
    deposit,
    owners,
    sources,
    heat,
    laser,
    sems,
):
    copies = [
        pltpu.make_async_copy(source, target, sems.at[n])
        for n, (source, target) in enumerate(
            (
                (owners_in, owners),
                (sources_in, sources),
                (heat_in, heat),
                (laser_in, laser),
            )
        )
    ]
    for copy in copies:
        copy.start()
    grp, slab = ids[0], ids[1]
    count = owners.shape[0] // 2
    lane = iota((CY, CY), 1)

    def store(result, pair):
        for block in range(4):
            at = (block & 1) * 2 + pair
            out[1 - grp, :, block >> 1, at, :] = result[block * count : (block + 1) * count]

    for n in (0, 1, 3):
        copies[n].wait()

    @pl.when(grp == 0)
    def _():
        table = plate_table(owners, sources, slab)
        deposit[...] = laser_heat(laser[...])
        copies[2].wait()
        for pair in (0, 1):
            even = heat[:, 2 * pair].reshape(CY, CY)
            odd = heat[:, 2 * pair + 1].reshape(CY, CY)
            left = jnp.where(lane < HALF, even, pltpu.roll(odd, HALF, 1))
            right = jnp.where(lane < HALF, pltpu.roll(even, HALF, 1), odd)
            store(pick_left(table, jnp.concatenate([left, right], axis=0)), pair)

    @pl.when(grp == 1)
    def _():
        table = window_table(owners, slab)
        copies[2].wait()
        row = iota((2 * CY, CY), 0)
        col = iota((2 * CY, CY), 1)
        mean = jnp.where((row >> 1) == col, 0.25, 0.0).astype(BF16)
        for pair in (0, 1):
            even = heat[:, 2 * pair].reshape(CY, CY)
            odd = heat[:, 2 * pair + 1].reshape(CY, CY)
            means = pick_right(jnp.concatenate([even, odd], axis=1), mean)
            store(pick_left(table, means), pair)


def edge_columns(x, right):
    side = jnp.where(right, iota((8, CY), 0), 1 - iota((8, CY), 0))
    lane = iota((8, CY), 1)
    pick = ones_where(((side == 0) & (lane == CY - 1)) | ((side == 1) & (lane == 0)))
    high, low = two_parts(x)
    dims = ((1,), (1,))
    return (dot(pick, high, dims) + dot(pick, low, dims))[:2]


def send_columns(ids, x, side_a, side_b, part):
    columns = edge_columns(x, ids[2] & 1 == 0)
    side_a[part : part + 1, : x.shape[0]] = columns[:1]
    side_b[part : part + 1, : x.shape[0]] = columns[1:]


def edge_row(x, top):
    return jnp.where(top, x[:, 0, :], x[:, CX - 1, :])


def edges_kernel(ids, heat, coeff, order, near, side_a, side_b):
    grp, top = ids[0], ids[1] & 1 == 1

    def send(fields):
        for part, x in enumerate(fields):
            near[part] = edge_row(x, top)
            send_columns(ids, x[...].reshape(PZ * CX, CY), side_a, side_b, part)

    @pl.when(grp == 0)
    def _():
        send((heat, coeff))

    @pl.when(grp == 1)
    def _():
        send((order.at[0], order.at[1]))


def lines_of(ids, side_a, side_b, part):
    even = ids[2] & 1 == 0
    in_a, in_b = side_a[part : part + 1], side_b[part : part + 1]
    return jnp.where(even, in_b, in_a), jnp.where(even, in_a, in_b)


def down(line, start=0, step=1):
    shape = (PZ, line.shape[1])
    at = iota(shape, 1) == iota(shape, 0) * step + start
    return jnp.sum(jnp.where(at, jnp.broadcast_to(line, shape), 0.0), axis=1, keepdims=True)


def receive_sides(ids, side_a, side_b, part):
    left, right = lines_of(ids, side_a, side_b, part)
    size = left.shape[1]
    row = iota((8, size), 0)
    left = jnp.broadcast_to(left, (8, size))
    right = jnp.broadcast_to(right, (8, size))
    both = jnp.where(row == 0, left, jnp.where(row == 1, right, 0.0))
    row, lane = iota((8, CY), 0), iota((8, CY), 1)
    place = ones_where(((row == 0) & (lane == 0)) | ((row == 1) & (lane == CY - 1)))
    return pick_right(both, place, ((0,), (0,)))


def beside(v, above, below, sides):
    row, lane = iota((CX, CY), 0), iota((CX, CY), 1)
    up = jnp.where(row == 0, jnp.broadcast_to(above, (CX, CY)), pltpu.roll(v, 1, 0))
    down = jnp.where(row == CX - 1, jnp.broadcast_to(below, (CX, CY)), pltpu.roll(v, CX - 1, 0))
    left = jnp.where(lane == 0, sides, pltpu.roll(v, 1, 1))
    right = jnp.where(lane == CY - 1, sides, pltpu.roll(v, CY - 1, 1))
    return up, down, left, right


def harmonic(center, beside_it):
    return 2.0 * center * beside_it / (center + beside_it)


def heat_planes(
    temp, cond, order, source, result, temp_halo, cond_halo, begin=0, end=PZ, scales=None
):
    temp_above, temp_below, temp_sides = temp_halo
    cond_above, cond_below, cond_sides = cond_halo

    def plane(z, from_above):
        v, k = temp[z], cond[z]
        one = pl.ds(z, 1)
        vs = beside(v, temp_above[one, :], temp_below[one, :], temp_sides[z])
        ks = beside(k, cond_above[one, :], cond_below[one, :], cond_sides[z])
        later = jnp.minimum(z + 1, PZ - 1)
        to_below = harmonic(k, cond[later]) * (temp[later] - v)
        total = to_below - from_above
        for v_next, k_next in zip(vs, ks):
            total = total + harmonic(k, k_next) * (v_next - v)
        result[z] = v + heat_dt * ((total + source(z)) / order[0, z] - order[1, z] * v)
        if scales is not None:
            scales[z] = heat_dt / order[0, z]
        return to_below

    if begin == 0:
        carry = jnp.zeros((CX, CY), F32)
    else:
        before = begin - 1
        carry = harmonic(cond[before], cond[begin]) * (temp[begin] - temp[before])
    lax.fori_loop(begin, end, plane, carry, unroll=4)


def phase_planes(
    phi, sol, response, warmth, new_phi, new_sol, phi_halo, sol_halo, begin, end
):
    phi_above, phi_below, phi_sides = phi_halo
    sol_above, sol_below, sol_sides = sol_halo

    def spread(field, z, halo, weights):
        above, below, sides = halo
        f = field[z]
        one = pl.ds(z, 1)
        up, down, left, right = beside(f, above[one, :], below[one, :], sides[z])
        before = jnp.where(z > 0, field[jnp.maximum(z - 1, 0)], 0.0)
        after = jnp.where(z < PZ - 1, field[jnp.minimum(z + 1, PZ - 1)], 0.0)
        wz, wx, wy = weights
        total = (wz * ((before - f) + (after - f)) + wx * ((up - f) + (down - f))) + wy * (
            (left - f) + (right - f)
        )
        return f, total

    def plane(z, carry):
        p, spread_p = spread(phi, z, phi_halo, PHASE_WEIGHTS)
        s, spread_s = spread(sol, z, sol_halo, SOLUTE_WEIGHTS)
        drive = 0.45 * jnp.tanh(
            response[z] * (liquefying_threshold - warmth[z] - freezing_line_gradient * s)
        )
        p_new = p + phase_dt * (spread_p + 4.0 * p * (1.0 - p) * (p - 0.5 + drive))
        new_phi[z] = p_new
        new_sol[z] = s + phase_dt * spread_s - solute_reject * (p_new - p) * s
        return carry

    lax.fori_loop(begin, end, plane, 0, unroll=4)


def base_kernel(
    ids,
    deposit,
    owners,
    sources,
    near,
    side_a,
    side_b,
    heat,
    coeff,
    order,
    table,
    base,
    scales,
    above_a,
    below_a,
    sides_a,
    above_b,
    below_b,
    sides_b,
):
    grp, slab = ids[0], ids[1]
    near_above = slab & 1 == 1

    @pl.when(grp == 0)
    def _():
        table[...] = plate_table(owners, sources, slab).astype(F32)
        for part, (above, below, side) in enumerate(
            ((above_a, below_a, sides_a), (above_b, below_b, sides_b))
        ):
            row = near[1 - (slab & 1), part]
            above[...] = jnp.where(near_above, row, 0.0)
            below[...] = jnp.where(near_above, 0.0, row)
            side[...] = receive_sides(ids, side_a, side_b, part).reshape(PZ, CX, CY)

        def source(z):
            return jnp.where(z == 0, deposit[...], 0.0)

        halo_a = (above_a, below_a, sides_a)
        halo_b = (above_b, below_b, sides_b)
        heat_planes(heat, coeff, order, source, base, halo_a, halo_b, scales=scales)

    @pl.when(grp == 1)
    def _():
        table[:, :CY] = window_table(owners, slab).astype(F32)


def first_kernel(
    ids,
    inbox,
    table,
    base,
    scales,
    side_a,
    side_b,
    heat,
    coeff,
    order,
    joined,
    warmth,
    near_out,
    far_out,
    side_a_out,
    side_b_out,
):
    grp, parity = ids[0], ids[1] & 1
    far_top = parity == 0

    def arrived(pair):
        blocks = [(side, 2 * slot + pair) for side in (0, 1) for slot in (0, 1)]
        return jnp.concatenate([inbox[1 - grp, :, side, at, :] for side, at in blocks], axis=0)

    lane = iota((CY, CY), 1)

    @pl.when(grp == 0)
    def _():
        picks = table[...].astype(BF16)
        first = joined.at[1]
        for pair in (0, 1):
            units = pick_left(picks, arrived(pair), ((0,), (0,)))
            left, right = units[:CY], units[CY:]
            even = jnp.where(lane < HALF, left, pltpu.roll(right, HALF, 1))
            odd = jnp.where(lane < HALF, pltpu.roll(left, HALF, 1), right)
            for i, layer in ((2 * pair, even), (2 * pair + 1, odd)):
                layer = layer.reshape(PZ // ZQ, CX, CY)
                for q in range(PZ // ZQ):
                    z = ZQ * q + i
                    joined[0, z] = layer[q]
                    first[z] = base[z] + scales[z] * layer[q]
        near_out[0] = edge_row(first, jnp.logical_not(far_top))
        scale = edge_row(scales, far_top)
        for part, x in enumerate((heat, coeff, first)):
            far_out[part * PZ : (part + 1) * PZ] = edge_row(x, far_top)
        far_out[3 * PZ : 4 * PZ] = scale
        at = iota((PZ * CX, CY), 0) == iota((PZ * CX, CY), 1) * CX + jnp.where(far_top, 0, CX - 1)
        lines = lines_of(ids, side_a, side_b, 0) + lines_of(ids, side_a, side_b, 1)
        rows = iota((8, PZ * CX), 0)
        corners = jnp.zeros((8, PZ * CX), F32)
        for n, line in enumerate(lines):
            corners = jnp.where(rows == n, jnp.broadcast_to(line, corners.shape), corners)
        far_out[4 * PZ :] = pick_right(corners, ones_where(at))
        send_columns(ids, first[...].reshape(PZ * CX, CY), side_a_out, side_b_out, 0)
        send_columns(ids, scale, side_a_out, side_b_out, 1)

    @pl.when(grp == 1)
    def _():
        picks = table[:, :CY].astype(BF16)
        row = iota((CY, 2 * CY), 0)
        col = iota((CY, 2 * CY), 1)
        target = col & (CY - 1)
        parent = target >> 1
        next_to = jnp.clip(parent - 1 + 2 * (target & 1), 0, HALF - 1)
        at = row - (col >> 7) * HALF
        fine = (jnp.where(at == parent, 0.75, 0.0) + jnp.where(at == next_to, 0.25, 0.0)).astype(
            BF16
        )
        for pair in (0, 1):
            refined = pick_right(arrived(pair), fine)
            placed = pick_left(picks, refined, ((0,), (0,)))
            for i in (0, 1):
                layer = placed[:, i * CY : (i + 1) * CY].reshape(PZ // ZQ, CX, CY)
                for q in range(PZ // ZQ):
                    warmth[ZQ * q + 2 * pair + i] = layer[q]
        for part in (0, 1):
            far_out[part * PZ : (part + 1) * PZ] = edge_row(order.at[part], far_top)


def second_kernel(
    ids,
    deposit,
    near_k,
    side_a_k,
    side_b_k,
    near,
    far,
    side_a,
    side_b,
    heat,
    coeff,
    order,
    joined,
    warmth,
    result_out,
    joined_out,
    above_a,
    below_a,
    sides_a,
    above_b,
    below_b,
    sides_b,
    result,
    both,
    sems,
):
    grp, parity = ids[0], ids[1] & 1
    even = parity == 0
    parts = RESULT_PARTS
    size = PZ // parts
    halo_a = (above_a, below_a, sides_a)
    halo_b = (above_b, below_b, sides_b)

    def place(above, below, near_values, far_values):
        above[...] = jnp.where(even, far_values, near_values)
        below[...] = jnp.where(even, near_values, far_values)

    def write(source, target, n):
        copy = pltpu.make_async_copy(source, target, sems.at[n])
        copy.start()
        return copy

    @pl.when(grp == 0)
    def _():
        copies = [write(joined.at[0], joined_out.at[0, 0], 0)]
        t_far, k_far, partial, scale_far = [far[n * PZ : (n + 1) * PZ] for n in range(4)]
        t_here, k_here = edge_row(heat, even), edge_row(coeff, even)
        scale = heat_dt / edge_row(order.at[0], even)
        crossing = harmonic(k_here, k_far) * (t_far - t_here)
        first = both.at[0]
        first[...] = joined[1]
        for top, row in ((True, 0), (False, CX - 1)):
            add = jnp.where(even == top, scale * crossing, 0.0)
            first[:, row, :] = first[:, row, :] + add
        copies.append(write(first, joined_out.at[0, 1], 1))
        place(above_a, below_a, near[1 - parity, 0], partial - scale_far * crossing)
        place(above_b, below_b, near_k[1 - parity, 1], k_far)
        sides_a[...] = receive_sides(ids, side_a, side_b, 0).reshape(PZ, CX, CY)
        sides_b[...] = receive_sides(ids, side_a_k, side_b_k, 1).reshape(PZ, CX, CY)
        row = jnp.where(even, 0, CX - 1)
        lane = iota((PZ, CY), 1)
        add = jnp.zeros((PZ, CY), F32)
        temps, conds = lines_of(ids, side_a_k, side_b_k, 0), lines_of(ids, side_a_k, side_b_k, 1)
        scales = lines_of(ids, side_a, side_b, 1)
        for n, end in enumerate((0, CY - 1)):
            t, k = down(temps[n], row, CX), down(conds[n], row, CX)
            corner = 4 * PZ + n
            t_next, k_next = down(far[corner : corner + 1]), down(far[corner + 2 : corner + 3])
            shared = 2.0 * k * k_next / jnp.maximum(k + k_next, 1e-6)
            change = down(scales[n][:, :CY]) * shared * (t_next - t)
            add = add + jnp.where(lane == end, change, 0.0)
        for top, row in ((True, 0), (False, CX - 1)):
            sides_a[:, row, :] = sides_a[:, row, :] + jnp.where(even == top, add, 0.0)

        def source(z):
            return joined[0, z] + jnp.where(z == 0, deposit[...], 0.0)

        for n in range(parts):
            begin, end = n * size, (n + 1) * size
            heat_planes(first, coeff, order, source, result, halo_a, halo_b, begin, end)
            planes = pl.ds(begin, size)
            copies.append(write(result.at[planes], result_out.at[0, planes], 2 + n))
        for copy in copies:
            copy.wait()

    @pl.when(grp == 1)
    def _():
        copies = [write(warmth, result_out.at[0], 0)]
        for part, (above, below, side) in enumerate((halo_a, halo_b)):
            far_values = far[part * PZ : (part + 1) * PZ]
            place(above, below, near_k[1 - parity, part], far_values)
            side[...] = receive_sides(ids, side_a_k, side_b_k, part).reshape(PZ, CX, CY)
        for n in range(parts):
            begin, end = n * size, (n + 1) * size
            phase_planes(
                order.at[0],
                order.at[1],
                coeff,
                warmth,
                both.at[0],
                both.at[1],
                halo_a,
                halo_b,
                begin,
                end,
            )
            planes = pl.ds(begin, size)
            copies.append(write(both.at[:, planes], joined_out.at[0, :, planes], 2 + n))
        for copy in copies:
            copy.wait()


RESULT_PARTS = 4
HBM = pl.BlockSpec(memory_space=pltpu.HBM)
SMEM = pl.BlockSpec(memory_space=pltpu.SMEM)
VMEM = pl.BlockSpec(memory_space=pltpu.VMEM)


def located(kernel, slabs, cols):
    def body(number, *refs):
        n = number[0]
        ids = lax.div(n, slabs * cols), lax.rem(lax.div(n, cols), slabs), lax.rem(n, cols)
        kernel(ids, *refs)

    return body


def call(kernel, specs, outs, scratch=(), out_space=VMEM, limit=24 << 20):
    shapes = [jax.ShapeDtypeStruct(shape, F32) for shape in outs]
    single = len(shapes) == 1
    return pl.pallas_call(
        kernel,
        out_shape=shapes[0] if single else shapes,
        in_specs=list(specs),
        out_specs=out_space if single else [out_space] * len(shapes),
        scratch_shapes=list(scratch),
        compiler_params=pltpu.CompilerParams(vmem_limit_bytes=limit),
    )


def halo_scratch():
    one = [
        pltpu.VMEM((PZ, CY), F32),
        pltpu.VMEM((PZ, CY), F32),
        pltpu.VMEM((PZ, CX, CY), F32),
    ]
    return one + one


def swaps(starts):
    return [pair for i in starts for pair in ((i, i + 1), (i + 1, i))]


def per_device(heat_field, coeff, order, block_owner, block_source, laser_cells):
    slabs, cols = lax.axis_size("slab"), lax.axis_size("col")
    chips = slabs // 2
    grp = lax.axis_index("grp")
    number = lax.axis_index(("grp", "slab", "col")).reshape(1)

    def place(kernel, *specs, **options):
        return call(located(kernel, slabs, cols), *specs, **options)

    near_pairs = [[2 * i, 2 * i + 1] for i in range(chips)]
    far_swap = swaps(range(1, slabs - 1, 2))
    side_a_swap, side_b_swap = swaps(range(0, cols - 1, 2)), swaps(range(1, cols - 1, 2))
    heat, conduct, orders = heat_field[0], coeff[0], order[0]
    owners, sources, laser = block_owner[0, :, :, 0], block_source[0], laser_cells[0]

    slab_table = pltpu.VMEM(owners.shape, jnp.int32)
    outbox, deposit = place(
        pack_kernel,
        [SMEM] + [HBM] * 4,
        [(2, chips, 2, 4, CY), (CX, CY)],
        [
            slab_table,
            slab_table,
            pltpu.VMEM((PZ // ZQ, ZQ, CX, CY), F32),
            pltpu.VMEM(laser.shape, jnp.int32),
            pltpu.SemaphoreType.DMA((4,)),
        ],
        limit=60 << 20,
    )(number, owners, sources, heat.reshape(PZ // ZQ, ZQ, CX, CY), laser)
    inbox = lax.all_to_all(
        outbox.reshape(-1, 4, CY), ("grp", "slab"), split_axis=0, concat_axis=0, tiled=True
    ).reshape(outbox.shape)
    rows, column, field = (2, PZ, CY), (2, PZ * CX), (PZ, CX, CY)
    near, side_a, side_b = place(edges_kernel, [SMEM] + [VMEM] * 3, [rows, column, column])(
        number, heat, conduct, orders
    )
    side_a = lax.ppermute(side_a, "col", side_a_swap)
    side_b = lax.ppermute(side_b, "col", side_b_swap)
    near = lax.all_gather(near, "slab", axis_index_groups=near_pairs)
    table, base, scales = place(
        base_kernel, [SMEM] + [VMEM] * 9, [(2 * slabs, 256), field, field], halo_scratch()
    )(number, deposit, owners, sources, near, side_a, side_b, heat, conduct, orders)
    joined, warmth, near_1, far_1, side_a_1, side_b_1 = place(
        first_kernel,
        [SMEM] + [VMEM] * 9,
        [(2,) + field, field, (1, PZ, CY), (4 * PZ + 8, CY), column, column],
    )(number, inbox, table, base, scales, side_a, side_b, heat, conduct, orders)
    far_1 = lax.ppermute(far_1, "slab", far_swap)
    side_a_1 = lax.ppermute(side_a_1, "col", side_a_swap)
    side_b_1 = lax.ppermute(side_b_1, "col", side_b_swap)
    near_1 = lax.all_gather(near_1, "slab", axis_index_groups=near_pairs)
    return place(
        second_kernel,
        [SMEM] + [VMEM] * 13,
        [(1,) + field, (1, 2) + field],
        halo_scratch()
        + [
            pltpu.VMEM(field, F32),
            pltpu.VMEM((2,) + field, F32),
            pltpu.SemaphoreType.DMA((2 + RESULT_PARTS,)),
        ],
        HBM,
    )(
        number,
        deposit,
        near,
        side_a,
        side_b,
        near_1,
        far_1,
        side_a_1,
        side_b_1,
        heat,
        conduct,
        orders,
        joined,
        warmth,
    )


def solution(mesh):
    placed = (
        P("grp", None, "slab", "col"),
        P("grp", None, "slab", "col"),
        P("grp", None, None, "slab", "col"),
        P("col", None, None, None),
        P("col", None, None),
        P("slab", "col", None),
    )
    return jax.shard_map(
        per_device,
        mesh=mesh,
        in_specs=placed,
        out_specs=(P("grp", None, "slab", "col"), P("grp", None, None, "slab", "col")),
        check_vma=False,
    )
```

```python
import jax
import jax.numpy as jnp
from jax import lax
from jax.experimental import pallas as pl
from jax.experimental.pallas import tpu as pltpu
from jax.sharding import PartitionSpec as P

PZ = 32
ZQ = 4
CX = 16
CY = 128
HALF = CY // 2

heat_dt = 0.07
phase_dt = 0.1
laser_power = 3.0
liquefying_threshold = 0.3
freezing_line_gradient = 0.5
solute_reject = 0.5
PHASE_WEIGHTS = (1.0, 1.3, 0.7)
SOLUTE_WEIGHTS = (0.8, 0.8, 0.8)

F32 = jnp.float32
BF16 = jnp.bfloat16
BIG = 1 << 20


def iota(shape, dim):
    return lax.broadcasted_iota(jnp.int32, shape, dim)


def ones_where(mask):
    return jnp.where(mask, 1.0, 0.0).astype(BF16)


def two_parts(x):
    high = x.astype(BF16)
    return high, (x - high.astype(F32)).astype(BF16)


def dot(a, b, dims=((1,), (0,))):
    return lax.dot_general(a, b, (dims, ((), ())), preferred_element_type=F32)


def pick_left(table, x, dims=((1,), (0,))):
    width = x.shape[1]
    both = dot(table, jnp.concatenate(two_parts(x), axis=1), dims)
    return both[:, :width] + both[:, width:]


def pick_right(x, table, dims=((1,), (0,))):
    high, low = two_parts(x)
    return dot(high, table, dims) + dot(low, table, dims)


def plate_table(owners, sources, slab):
    count = owners.shape[0] // 2
    rows = []
    for parity in (0, 1):
        own = owners[pl.ds(parity, count, stride=2), :]
        src = sources[pl.ds(parity, count, stride=2), :]
        key = iota(own.shape, 1) * 256 + src
        mine = own == slab
        first = jnp.min(jnp.where(mine, key, BIG).astype(F32), axis=1, keepdims=True)
        last = jnp.max(jnp.where(mine, key, -1).astype(F32), axis=1, keepdims=True)
        first, last = first.astype(jnp.int32), last.astype(jnp.int32)
        for value, valid in ((first, first < BIG), (last, last > first)):
            unit = value & 255
            place = jnp.where(valid, (unit & 1) * 128 + (unit >> 1), -1)
            rows.append(ones_where(iota((count, 256), 1) == place))
    return jnp.concatenate(rows, axis=0)


def window_table(owners, slab):
    count = owners.shape[0] // 2
    own = owners[pl.ds(slab, 1), :]
    units = own.shape[1]
    unit = iota((count, units), 1)
    rows = []
    for parity in (0, 1):
        mine = jnp.broadcast_to(own, (count, units)) == iota((count, units), 0) * 2 + parity
        first = jnp.min(jnp.where(mine, unit, BIG).astype(F32), axis=1, keepdims=True)
        last = jnp.max(jnp.where(mine, unit, -1).astype(F32), axis=1, keepdims=True)
        first, last = first.astype(jnp.int32), last.astype(jnp.int32)
        rows.append(ones_where(unit == first))
        rows.append(ones_where((unit == last) & (last > first)))
    spread = ones_where((iota((units, 2 * units), 1) >> 1) == iota((units, 2 * units), 0))
    return dot(jnp.concatenate(rows, axis=0), spread).astype(BF16)


def laser_heat(cells):
    count = cells.shape[1]
    rows = ones_where(iota((CX, count), 0) == jnp.broadcast_to(cells >> 7, (CX, count)))
    lanes = ones_where(iota((CY, count), 0) == jnp.broadcast_to(cells & 127, (CY, count)))
    return laser_power * dot(rows, lanes, ((1,), (1,)))


def pack_kernel(
    ids,
    owners_in,
    sources_in,
    heat_in,
    laser_in,
    out,
    deposit,
    owners,
    sources,
    heat,
    laser,
    sems,
):
    copies = [
        pltpu.make_async_copy(source, target, sems.at[n])
        for n, (source, target) in enumerate(
            (
                (owners_in, owners),
                (sources_in, sources),
                (heat_in, heat),
                (laser_in, laser),
            )
        )
    ]
    for copy in copies:
        copy.start()
    grp, slab = ids[0], ids[1]
    count = owners.shape[0] // 2
    lane = iota((CY, CY), 1)

    def store(result, pair):
        for block in range(4):
            at = (block & 1) * 2 + pair
            out[1 - grp, :, block >> 1, at, :] = result[block * count : (block + 1) * count]

    for n in (0, 1, 3):
        copies[n].wait()

    @pl.when(grp == 0)
    def _():
        table = plate_table(owners, sources, slab)
        deposit[...] = laser_heat(laser[...])
        copies[2].wait()
        for pair in (0, 1):
            even = heat[:, 2 * pair].reshape(CY, CY)
            odd = heat[:, 2 * pair + 1].reshape(CY, CY)
            left = jnp.where(lane < HALF, even, pltpu.roll(odd, HALF, 1))
            right = jnp.where(lane < HALF, pltpu.roll(even, HALF, 1), odd)
            store(pick_left(table, jnp.concatenate([left, right], axis=0)), pair)

    @pl.when(grp == 1)
    def _():
        table = window_table(owners, slab)
        copies[2].wait()
        row = iota((2 * CY, CY), 0)
        col = iota((2 * CY, CY), 1)
        mean = jnp.where((row >> 1) == col, 0.25, 0.0).astype(BF16)
        for pair in (0, 1):
            even = heat[:, 2 * pair].reshape(CY, CY)
            odd = heat[:, 2 * pair + 1].reshape(CY, CY)
            means = pick_right(jnp.concatenate([even, odd], axis=1), mean)
            store(pick_left(table, means), pair)


def edge_columns(x, right):
    side = jnp.where(right, iota((8, CY), 0), 1 - iota((8, CY), 0))
    lane = iota((8, CY), 1)
    pick = ones_where(((side == 0) & (lane == CY - 1)) | ((side == 1) & (lane == 0)))
    high, low = two_parts(x)
    dims = ((1,), (1,))
    return (dot(pick, high, dims) + dot(pick, low, dims))[:2]


def send_columns(ids, x, side_a, side_b, part):
    columns = edge_columns(x, ids[2] & 1 == 0)
    side_a[part : part + 1, : x.shape[0]] = columns[:1]
    side_b[part : part + 1, : x.shape[0]] = columns[1:]


def edge_row(x, top):
    return jnp.where(top, x[:, 0, :], x[:, CX - 1, :])


def edges_kernel(ids, heat, coeff, order, near, side_a, side_b):
    grp, top = ids[0], ids[1] & 1 == 1

    def send(fields):
        for part, x in enumerate(fields):
            near[part] = edge_row(x, top)
            send_columns(ids, x[...].reshape(PZ * CX, CY), side_a, side_b, part)

    @pl.when(grp == 0)
    def _():
        send((heat, coeff))

    @pl.when(grp == 1)
    def _():
        send((order.at[0], order.at[1]))


def lines_of(ids, side_a, side_b, part):
    even = ids[2] & 1 == 0
    in_a, in_b = side_a[part : part + 1], side_b[part : part + 1]
    return jnp.where(even, in_b, in_a), jnp.where(even, in_a, in_b)


def down(line, start=0, step=1):
    shape = (PZ, line.shape[1])
    at = iota(shape, 1) == iota(shape, 0) * step + start
    return jnp.sum(jnp.where(at, jnp.broadcast_to(line, shape), 0.0), axis=1, keepdims=True)


def receive_sides(ids, side_a, side_b, part):
    left, right = lines_of(ids, side_a, side_b, part)
    size = left.shape[1]
    row = iota((8, size), 0)
    left = jnp.broadcast_to(left, (8, size))
    right = jnp.broadcast_to(right, (8, size))
    both = jnp.where(row == 0, left, jnp.where(row == 1, right, 0.0))
    row, lane = iota((8, CY), 0), iota((8, CY), 1)
    place = ones_where(((row == 0) & (lane == 0)) | ((row == 1) & (lane == CY - 1)))
    return pick_right(both, place, ((0,), (0,)))


def beside(v, above, below, sides):
    row, lane = iota((CX, CY), 0), iota((CX, CY), 1)
    up = jnp.where(row == 0, jnp.broadcast_to(above, (CX, CY)), pltpu.roll(v, 1, 0))
    down = jnp.where(row == CX - 1, jnp.broadcast_to(below, (CX, CY)), pltpu.roll(v, CX - 1, 0))
    left = jnp.where(lane == 0, sides, pltpu.roll(v, 1, 1))
    right = jnp.where(lane == CY - 1, sides, pltpu.roll(v, CY - 1, 1))
    return up, down, left, right


def harmonic(center, beside_it):
    return 2.0 * center * beside_it / (center + beside_it)


def base_planes(temp, cond, order, deposit, base, scales, shares, top, temp_halo, cond_halo):
    temp_above, temp_below, temp_sides = temp_halo
    cond_above, cond_below, cond_sides = cond_halo

    def plane(z, from_above):
        v, k = temp[z], cond[z]
        one = pl.ds(z, 1)
        vs = beside(v, temp_above[one, :], temp_below[one, :], temp_sides[z])
        ks = beside(k, cond_above[one, :], cond_below[one, :], cond_sides[z])
        later = jnp.minimum(z + 1, PZ - 1)
        shared = harmonic(k, cond[later])
        shares[0, z] = shared
        to_below = shared * (temp[later] - v)
        total = to_below - from_above
        for n, (v_next, k_next) in enumerate(zip(vs, ks)):
            shared = harmonic(k, k_next)
            if n == 0:
                top[one, :] = shared[:1]
            else:
                shares[n, z] = shared
            total = total + shared * (v_next - v)
        total = total + jnp.where(z == 0, deposit[...], 0.0)
        base[z] = v + heat_dt * (total / order[0, z] - order[1, z] * v)
        scales[z] = heat_dt / order[0, z]
        return to_below

    lax.fori_loop(0, PZ, plane, jnp.zeros((CX, CY), F32), unroll=4)


def second_planes(
    v, order, latent, deposit, shares, top, halo, far_row, far_flux, result, begin, end
):
    above, below, sides = halo
    row = iota((CX, CY), 0)

    def spread(line):
        return jnp.broadcast_to(line, (CX, CY))

    def plane(z, from_above):
        center = v[z]
        one = pl.ds(z, 1)
        vs = beside(center, above[one, :], below[one, :], sides[z])
        down = shares[1, z]
        up = jnp.where(row == 0, spread(top[one, :]), pltpu.roll(down, 1, 0))
        to_below = shares[0, z] * (v[jnp.minimum(z + 1, PZ - 1)] - center)
        total = to_below - from_above
        for shared, v_next in zip((up, down, shares[2, z], shares[3, z]), vs):
            total = total + shared * (v_next - center)
        total = total + jnp.where(row == far_row, spread(far_flux[one, :]), 0.0)
        source = latent[z] + jnp.where(z == 0, deposit[...], 0.0)
        result[z] = center + heat_dt * ((total + source) / order[0, z] - order[1, z] * center)
        return to_below

    if begin == 0:
        carry = jnp.zeros((CX, CY), F32)
    else:
        carry = shares[0, begin - 1] * (v[begin] - v[begin - 1])
    lax.fori_loop(begin, end, plane, carry, unroll=4)


def phase_planes(
    phi, sol, response, warmth, new_phi, new_sol, phi_halo, sol_halo, begin, end
):
    phi_above, phi_below, phi_sides = phi_halo
    sol_above, sol_below, sol_sides = sol_halo

    def spread(field, z, halo, weights):
        above, below, sides = halo
        f = field[z]
        one = pl.ds(z, 1)
        up, down, left, right = beside(f, above[one, :], below[one, :], sides[z])
        before = jnp.where(z > 0, field[jnp.maximum(z - 1, 0)], 0.0)
        after = jnp.where(z < PZ - 1, field[jnp.minimum(z + 1, PZ - 1)], 0.0)
        wz, wx, wy = weights
        total = (wz * ((before - f) + (after - f)) + wx * ((up - f) + (down - f))) + wy * (
            (left - f) + (right - f)
        )
        return f, total

    def plane(z, carry):
        p, spread_p = spread(phi, z, phi_halo, PHASE_WEIGHTS)
        s, spread_s = spread(sol, z, sol_halo, SOLUTE_WEIGHTS)
        drive = 0.45 * jnp.tanh(
            response[z] * (liquefying_threshold - warmth[z] - freezing_line_gradient * s)
        )
        p_new = p + phase_dt * (spread_p + 4.0 * p * (1.0 - p) * (p - 0.5 + drive))
        new_phi[z] = p_new
        new_sol[z] = s + phase_dt * spread_s - solute_reject * (p_new - p) * s
        return carry

    lax.fori_loop(begin, end, plane, 0, unroll=4)


def base_kernel(
    ids,
    deposit,
    owners,
    sources,
    near,
    side_a,
    side_b,
    heat,
    coeff,
    order,
    table,
    base,
    scales,
    shares,
    top,
    above_a,
    below_a,
    sides_a,
    above_b,
    below_b,
    sides_b,
):
    grp, slab = ids[0], ids[1]
    near_above = slab & 1 == 1

    @pl.when(grp == 0)
    def _():
        table[...] = plate_table(owners, sources, slab).astype(F32)
        for part, (above, below, side) in enumerate(
            ((above_a, below_a, sides_a), (above_b, below_b, sides_b))
        ):
            row = near[1 - (slab & 1), part]
            above[...] = jnp.where(near_above, row, 0.0)
            below[...] = jnp.where(near_above, 0.0, row)
            side[...] = receive_sides(ids, side_a, side_b, part).reshape(PZ, CX, CY)

        halo_a = (above_a, below_a, sides_a)
        halo_b = (above_b, below_b, sides_b)
        base_planes(
            heat, coeff, order, deposit, base, scales, shares, top, halo_a, halo_b
        )

    @pl.when(grp == 1)
    def _():
        table[:, :CY] = window_table(owners, slab).astype(F32)


def first_kernel(
    ids,
    inbox,
    table,
    base,
    scales,
    side_a,
    side_b,
    heat,
    coeff,
    order,
    joined,
    warmth,
    near_out,
    far_out,
    side_a_out,
    side_b_out,
):
    grp, parity = ids[0], ids[1] & 1
    far_top = parity == 0

    def arrived(pair):
        blocks = [(side, 2 * slot + pair) for side in (0, 1) for slot in (0, 1)]
        return jnp.concatenate([inbox[1 - grp, :, side, at, :] for side, at in blocks], axis=0)

    lane = iota((CY, CY), 1)

    @pl.when(grp == 0)
    def _():
        picks = table[...].astype(BF16)
        first = joined.at[1]
        for pair in (0, 1):
            units = pick_left(picks, arrived(pair), ((0,), (0,)))
            left, right = units[:CY], units[CY:]
            even = jnp.where(lane < HALF, left, pltpu.roll(right, HALF, 1))
            odd = jnp.where(lane < HALF, pltpu.roll(left, HALF, 1), right)
            for i, layer in ((2 * pair, even), (2 * pair + 1, odd)):
                layer = layer.reshape(PZ // ZQ, CX, CY)
                for q in range(PZ // ZQ):
                    z = ZQ * q + i
                    joined[0, z] = layer[q]
                    first[z] = base[z] + scales[z] * layer[q]
        near_out[0] = edge_row(first, jnp.logical_not(far_top))
        scale = edge_row(scales, far_top)
        for part, x in enumerate((heat, coeff, first)):
            far_out[part * PZ : (part + 1) * PZ] = edge_row(x, far_top)
        far_out[3 * PZ : 4 * PZ] = scale
        at = iota((PZ * CX, CY), 0) == iota((PZ * CX, CY), 1) * CX + jnp.where(far_top, 0, CX - 1)
        lines = lines_of(ids, side_a, side_b, 0) + lines_of(ids, side_a, side_b, 1)
        rows = iota((8, PZ * CX), 0)
        corners = jnp.zeros((8, PZ * CX), F32)
        for n, line in enumerate(lines):
            corners = jnp.where(rows == n, jnp.broadcast_to(line, corners.shape), corners)
        far_out[4 * PZ :] = pick_right(corners, ones_where(at))
        send_columns(ids, first[...].reshape(PZ * CX, CY), side_a_out, side_b_out, 0)
        send_columns(ids, scale, side_a_out, side_b_out, 1)

    @pl.when(grp == 1)
    def _():
        picks = table[:, :CY].astype(BF16)
        row = iota((CY, 2 * CY), 0)
        col = iota((CY, 2 * CY), 1)
        target = col & (CY - 1)
        parent = target >> 1
        next_to = jnp.clip(parent - 1 + 2 * (target & 1), 0, HALF - 1)
        at = row - (col >> 7) * HALF
        fine = (jnp.where(at == parent, 0.75, 0.0) + jnp.where(at == next_to, 0.25, 0.0)).astype(
            BF16
        )
        for pair in (0, 1):
            refined = pick_right(arrived(pair), fine)
            placed = pick_left(picks, refined, ((0,), (0,)))
            for i in (0, 1):
                layer = placed[:, i * CY : (i + 1) * CY].reshape(PZ // ZQ, CX, CY)
                for q in range(PZ // ZQ):
                    warmth[ZQ * q + 2 * pair + i] = layer[q]
        for part in (0, 1):
            far_out[part * PZ : (part + 1) * PZ] = edge_row(order.at[part], far_top)


def second_kernel(
    ids,
    deposit,
    near_k,
    side_a_k,
    side_b_k,
    near,
    far,
    side_a,
    side_b,
    far_sent,
    shares,
    top,
    coeff,
    order,
    joined,
    warmth,
    result_out,
    joined_out,
    above_a,
    below_a,
    sides_a,
    above_b,
    below_b,
    sides_b,
    result,
    both,
    far_flux,
    sems,
):
    grp, parity = ids[0], ids[1] & 1
    even = parity == 0
    parts = RESULT_PARTS
    size = PZ // parts
    halo_a = (above_a, below_a, sides_a)
    halo_b = (above_b, below_b, sides_b)

    def place(above, below, near_values, far_values):
        above[...] = jnp.where(even, far_values, near_values)
        below[...] = jnp.where(even, near_values, far_values)

    def write(source, target, n):
        copy = pltpu.make_async_copy(source, target, sems.at[n])
        copy.start()
        return copy

    @pl.when(grp == 0)
    def _():
        copies = [write(joined.at[0], joined_out.at[0, 0], 0)]
        t_far, k_far, partial, scale_far = [far[n * PZ : (n + 1) * PZ] for n in range(4)]
        t_here, k_here = far_sent[:PZ], far_sent[PZ : 2 * PZ]
        scale = far_sent[3 * PZ : 4 * PZ]
        shared_far = harmonic(k_here, k_far)
        crossing = shared_far * (t_far - t_here)
        first = both.at[0]
        first[...] = joined[1]
        for at_top, row in ((True, 0), (False, CX - 1)):
            add = jnp.where(even == at_top, scale * crossing, 0.0)
            first[:, row, :] = first[:, row, :] + add
        copies.append(write(first, joined_out.at[0, 1], 1))
        far_first = partial - scale_far * crossing
        far_flux[...] = shared_far * (far_first - edge_row(first, even))
        place(above_a, below_a, near[1 - parity, 0], far_first)
        sides_a[...] = receive_sides(ids, side_a, side_b, 0).reshape(PZ, CX, CY)
        row = jnp.where(even, 0, CX - 1)
        lane = iota((PZ, CY), 1)
        add = jnp.zeros((PZ, CY), F32)
        temps, conds = lines_of(ids, side_a_k, side_b_k, 0), lines_of(ids, side_a_k, side_b_k, 1)
        scales = lines_of(ids, side_a, side_b, 1)
        for n, end in enumerate((0, CY - 1)):
            t, k = down(temps[n], row, CX), down(conds[n], row, CX)
            corner = 4 * PZ + n
            t_next, k_next = down(far[corner : corner + 1]), down(far[corner + 2 : corner + 3])
            shared = 2.0 * k * k_next / jnp.maximum(k + k_next, 1e-6)
            change = down(scales[n][:, :CY]) * shared * (t_next - t)
            add = add + jnp.where(lane == end, change, 0.0)
        for at_top, edge in ((True, 0), (False, CX - 1)):
            sides_a[:, edge, :] = sides_a[:, edge, :] + jnp.where(even == at_top, add, 0.0)
        for n in range(parts):
            begin, end = n * size, (n + 1) * size
            second_planes(
                first,
                order,
                joined.at[0],
                deposit,
                shares,
                top,
                halo_a,
                row,
                far_flux,
                result,
                begin,
                end,
            )
            planes = pl.ds(begin, size)
            copies.append(write(result.at[planes], result_out.at[0, planes], 2 + n))
        for copy in copies:
            copy.wait()

    @pl.when(grp == 1)
    def _():
        copies = [write(warmth, result_out.at[0], 0)]
        for part, (above, below, side) in enumerate((halo_a, halo_b)):
            far_values = far[part * PZ : (part + 1) * PZ]
            place(above, below, near_k[1 - parity, part], far_values)
            side[...] = receive_sides(ids, side_a_k, side_b_k, part).reshape(PZ, CX, CY)
        for n in range(parts):
            begin, end = n * size, (n + 1) * size
            phase_planes(
                order.at[0],
                order.at[1],
                coeff,
                warmth,
                both.at[0],
                both.at[1],
                halo_a,
                halo_b,
                begin,
                end,
            )
            planes = pl.ds(begin, size)
            copies.append(write(both.at[:, planes], joined_out.at[0, :, planes], 2 + n))
        for copy in copies:
            copy.wait()


RESULT_PARTS = 4
HBM = pl.BlockSpec(memory_space=pltpu.HBM)
SMEM = pl.BlockSpec(memory_space=pltpu.SMEM)
VMEM = pl.BlockSpec(memory_space=pltpu.VMEM)


def located(kernel, slabs, cols):
    def body(number, *refs):
        n = number[0]
        ids = lax.div(n, slabs * cols), lax.rem(lax.div(n, cols), slabs), lax.rem(n, cols)
        kernel(ids, *refs)

    return body


def call(kernel, specs, outs, scratch=(), out_space=VMEM, limit=24 << 20):
    shapes = [jax.ShapeDtypeStruct(shape, F32) for shape in outs]
    single = len(shapes) == 1
    return pl.pallas_call(
        kernel,
        out_shape=shapes[0] if single else shapes,
        in_specs=list(specs),
        out_specs=out_space if single else [out_space] * len(shapes),
        scratch_shapes=list(scratch),
        compiler_params=pltpu.CompilerParams(vmem_limit_bytes=limit),
    )


def halo_scratch():
    one = [
        pltpu.VMEM((PZ, CY), F32),
        pltpu.VMEM((PZ, CY), F32),
        pltpu.VMEM((PZ, CX, CY), F32),
    ]
    return one + one


def swaps(starts):
    return [pair for i in starts for pair in ((i, i + 1), (i + 1, i))]


def per_device(heat_field, coeff, order, block_owner, block_source, laser_cells):
    slabs, cols = lax.axis_size("slab"), lax.axis_size("col")
    chips = slabs // 2
    grp = lax.axis_index("grp")
    number = lax.axis_index(("grp", "slab", "col")).reshape(1)

    def place(kernel, *specs, **options):
        return call(located(kernel, slabs, cols), *specs, **options)

    near_pairs = [[2 * i, 2 * i + 1] for i in range(chips)]
    far_swap = swaps(range(1, slabs - 1, 2))
    side_a_swap, side_b_swap = swaps(range(0, cols - 1, 2)), swaps(range(1, cols - 1, 2))
    heat, conduct, orders = heat_field[0], coeff[0], order[0]
    owners, sources, laser = block_owner[0, :, :, 0], block_source[0], laser_cells[0]

    slab_table = pltpu.VMEM(owners.shape, jnp.int32)
    outbox, deposit = place(
        pack_kernel,
        [SMEM] + [HBM] * 4,
        [(2, chips, 2, 4, CY), (CX, CY)],
        [
            slab_table,
            slab_table,
            pltpu.VMEM((PZ // ZQ, ZQ, CX, CY), F32),
            pltpu.VMEM(laser.shape, jnp.int32),
            pltpu.SemaphoreType.DMA((4,)),
        ],
        limit=60 << 20,
    )(number, owners, sources, heat.reshape(PZ // ZQ, ZQ, CX, CY), laser)
    inbox = lax.all_to_all(
        outbox.reshape(-1, 4, CY), ("grp", "slab"), split_axis=0, concat_axis=0, tiled=True
    ).reshape(outbox.shape)
    rows, column, field = (2, PZ, CY), (2, PZ * CX), (PZ, CX, CY)
    near, side_a, side_b = place(edges_kernel, [SMEM] + [VMEM] * 3, [rows, column, column])(
        number, heat, conduct, orders
    )
    side_a = lax.ppermute(side_a, "col", side_a_swap)
    side_b = lax.ppermute(side_b, "col", side_b_swap)
    near = lax.all_gather(near, "slab", axis_index_groups=near_pairs)
    table, base, scales, shares, top = place(
        base_kernel,
        [SMEM] + [VMEM] * 9,
        [(2 * slabs, 256), field, field, (4,) + field, (PZ, CY)],
        halo_scratch(),
    )(number, deposit, owners, sources, near, side_a, side_b, heat, conduct, orders)
    joined, warmth, near_1, far_1, side_a_1, side_b_1 = place(
        first_kernel,
        [SMEM] + [VMEM] * 9,
        [(2,) + field, field, (1, PZ, CY), (4 * PZ + 8, CY), column, column],
    )(number, inbox, table, base, scales, side_a, side_b, heat, conduct, orders)
    far_sent = far_1
    far_1 = lax.ppermute(far_1, "slab", far_swap)
    side_a_1 = lax.ppermute(side_a_1, "col", side_a_swap)
    side_b_1 = lax.ppermute(side_b_1, "col", side_b_swap)
    near_1 = lax.all_gather(near_1, "slab", axis_index_groups=near_pairs)
    return place(
        second_kernel,
        [SMEM] + [VMEM] * 15,
        [(1,) + field, (1, 2) + field],
        halo_scratch()
        + [
            pltpu.VMEM(field, F32),
            pltpu.VMEM((2,) + field, F32),
            pltpu.VMEM((PZ, CY), F32),
            pltpu.SemaphoreType.DMA((2 + RESULT_PARTS,)),
        ],
        HBM,
    )(
        number,
        deposit,
        near,
        side_a,
        side_b,
        near_1,
        far_1,
        side_a_1,
        side_b_1,
        far_sent,
        shares,
        top,
        conduct,
        orders,
        joined,
        warmth,
    )


def solution(mesh):
    placed = (
        P("grp", None, "slab", "col"),
        P("grp", None, "slab", "col"),
        P("grp", None, None, "slab", "col"),
        P("col", None, None, None),
        P("col", None, None),
        P("slab", "col", None),
    )
    return jax.shard_map(
        per_device,
        mesh=mesh,
        in_specs=placed,
        out_specs=(P("grp", None, "slab", "col"), P("grp", None, None, "slab", "col")),
        check_vma=False,
    )
```

```python
import jax
import jax.numpy as jnp
from jax import lax
from jax.experimental import pallas as pl
from jax.experimental.pallas import tpu as pltpu
from jax.sharding import PartitionSpec as P

PZ = 32
ZQ = 4
CX = 16
CY = 128
HALF = CY // 2

heat_dt = 0.07
phase_dt = 0.1
laser_power = 3.0
liquefying_threshold = 0.3
freezing_line_gradient = 0.5
solute_reject = 0.5
PHASE_WEIGHTS = (1.0, 1.3, 0.7)
SOLUTE_WEIGHTS = (0.8, 0.8, 0.8)

F32 = jnp.float32
BF16 = jnp.bfloat16
BIG = 1 << 20


def iota(shape, dim):
    return lax.broadcasted_iota(jnp.int32, shape, dim)


def ones_where(mask):
    return jnp.where(mask, 1.0, 0.0).astype(BF16)


def two_parts(x):
    high = x.astype(BF16)
    return high, (x - high.astype(F32)).astype(BF16)


def dot(a, b, dims=((1,), (0,))):
    return lax.dot_general(a, b, (dims, ((), ())), preferred_element_type=F32)


def pick_left(table, x, dims=((1,), (0,))):
    width = x.shape[1]
    both = dot(table, jnp.concatenate(two_parts(x), axis=1), dims)
    return both[:, :width] + both[:, width:]


def pick_right(x, table, dims=((1,), (0,))):
    high, low = two_parts(x)
    return dot(high, table, dims) + dot(low, table, dims)


def plate_table(owners, sources, slab):
    count = owners.shape[0] // 2
    rows = []
    for parity in (0, 1):
        own = owners[pl.ds(parity, count, stride=2), :]
        src = sources[pl.ds(parity, count, stride=2), :]
        key = iota(own.shape, 1) * 256 + src
        mine = own == slab
        first = jnp.min(jnp.where(mine, key, BIG).astype(F32), axis=1, keepdims=True)
        last = jnp.max(jnp.where(mine, key, -1).astype(F32), axis=1, keepdims=True)
        first, last = first.astype(jnp.int32), last.astype(jnp.int32)
        for value, valid in ((first, first < BIG), (last, last > first)):
            unit = value & 255
            place = jnp.where(valid, (unit & 1) * 128 + (unit >> 1), -1)
            rows.append(ones_where(iota((count, 256), 1) == place))
    return jnp.concatenate(rows, axis=0)


def window_table(owners, slab):
    count = owners.shape[0] // 2
    own = owners[pl.ds(slab, 1), :]
    units = own.shape[1]
    unit = iota((count, units), 1)
    rows = []
    for parity in (0, 1):
        mine = jnp.broadcast_to(own, (count, units)) == iota((count, units), 0) * 2 + parity
        first = jnp.min(jnp.where(mine, unit, BIG).astype(F32), axis=1, keepdims=True)
        last = jnp.max(jnp.where(mine, unit, -1).astype(F32), axis=1, keepdims=True)
        first, last = first.astype(jnp.int32), last.astype(jnp.int32)
        rows.append(ones_where(unit == first))
        rows.append(ones_where((unit == last) & (last > first)))
    spread = ones_where((iota((units, 2 * units), 1) >> 1) == iota((units, 2 * units), 0))
    return dot(jnp.concatenate(rows, axis=0), spread).astype(BF16)


def laser_heat(cells):
    count = cells.shape[1]
    rows = ones_where(iota((CX, count), 0) == jnp.broadcast_to(cells >> 7, (CX, count)))
    lanes = ones_where(iota((CY, count), 0) == jnp.broadcast_to(cells & 127, (CY, count)))
    return laser_power * dot(rows, lanes, ((1,), (1,)))


def pack_kernel(
    ids,
    owners_in,
    sources_in,
    heat_in,
    laser_in,
    out,
    deposit,
    owners,
    sources,
    heat,
    laser,
    sems,
):
    copies = [
        pltpu.make_async_copy(source, target, sems.at[n])
        for n, (source, target) in enumerate(
            (
                (owners_in, owners),
                (sources_in, sources),
                (heat_in, heat),
                (laser_in, laser),
            )
        )
    ]
    for copy in copies:
        copy.start()
    grp, slab = ids[0], ids[1]
    count = owners.shape[0] // 2
    lane = iota((CY, CY), 1)

    def store(result, pair):
        for block in range(4):
            at = (block & 1) * 2 + pair
            out[1 - grp, :, block >> 1, at, :] = result[block * count : (block + 1) * count]

    for n in (0, 1, 3):
        copies[n].wait()

    @pl.when(grp == 0)
    def _():
        table = plate_table(owners, sources, slab)
        deposit[...] = laser_heat(laser[...])
        copies[2].wait()
        for pair in (0, 1):
            even = heat[:, 2 * pair].reshape(CY, CY)
            odd = heat[:, 2 * pair + 1].reshape(CY, CY)
            left = jnp.where(lane < HALF, even, pltpu.roll(odd, HALF, 1))
            right = jnp.where(lane < HALF, pltpu.roll(even, HALF, 1), odd)
            store(pick_left(table, jnp.concatenate([left, right], axis=0)), pair)

    @pl.when(grp == 1)
    def _():
        table = window_table(owners, slab)
        copies[2].wait()
        row = iota((2 * CY, CY), 0)
        col = iota((2 * CY, CY), 1)
        mean = jnp.where((row >> 1) == col, 0.25, 0.0).astype(BF16)
        for pair in (0, 1):
            even = heat[:, 2 * pair].reshape(CY, CY)
            odd = heat[:, 2 * pair + 1].reshape(CY, CY)
            means = pick_right(jnp.concatenate([even, odd], axis=1), mean)
            store(pick_left(table, means), pair)


def edge_columns(x, right):
    side = jnp.where(right, iota((8, CY), 0), 1 - iota((8, CY), 0))
    lane = iota((8, CY), 1)
    pick = ones_where(((side == 0) & (lane == CY - 1)) | ((side == 1) & (lane == 0)))
    high, low = two_parts(x)
    dims = ((1,), (1,))
    return (dot(pick, high, dims) + dot(pick, low, dims))[:2]


def send_columns(ids, x, side_a, side_b, part):
    columns = edge_columns(x, ids[2] & 1 == 0)
    side_a[part : part + 1, : x.shape[0]] = columns[:1]
    side_b[part : part + 1, : x.shape[0]] = columns[1:]


def edge_row(x, top):
    return jnp.where(top, x[:, 0, :], x[:, CX - 1, :])


def edges_kernel(ids, heat, coeff, order, near, side_a, side_b):
    grp, top = ids[0], ids[1] & 1 == 1

    def send(fields):
        for part, x in enumerate(fields):
            near[part] = edge_row(x, top)
            send_columns(ids, x[...].reshape(PZ * CX, CY), side_a, side_b, part)

    @pl.when(grp == 0)
    def _():
        send((heat, coeff))

    @pl.when(grp == 1)
    def _():
        send((order.at[0], order.at[1]))


def lines_of(ids, side_a, side_b, part):
    even = ids[2] & 1 == 0
    in_a, in_b = side_a[part : part + 1], side_b[part : part + 1]
    return jnp.where(even, in_b, in_a), jnp.where(even, in_a, in_b)


def down(line, start=0, step=1):
    shape = (PZ, line.shape[1])
    at = iota(shape, 1) == iota(shape, 0) * step + start
    return jnp.sum(jnp.where(at, jnp.broadcast_to(line, shape), 0.0), axis=1, keepdims=True)


def receive_sides(ids, side_a, side_b, part):
    left, right = lines_of(ids, side_a, side_b, part)
    size = left.shape[1]
    row = iota((8, size), 0)
    left = jnp.broadcast_to(left, (8, size))
    right = jnp.broadcast_to(right, (8, size))
    both = jnp.where(row == 0, left, jnp.where(row == 1, right, 0.0))
    row, lane = iota((8, CY), 0), iota((8, CY), 1)
    place = ones_where(((row == 0) & (lane == 0)) | ((row == 1) & (lane == CY - 1)))
    return pick_right(both, place, ((0,), (0,)))


def beside(v, above, below, sides):
    row, lane = iota((CX, CY), 0), iota((CX, CY), 1)
    up = jnp.where(row == 0, jnp.broadcast_to(above, (CX, CY)), pltpu.roll(v, 1, 0))
    down = jnp.where(row == CX - 1, jnp.broadcast_to(below, (CX, CY)), pltpu.roll(v, CX - 1, 0))
    left = jnp.where(lane == 0, sides, pltpu.roll(v, 1, 1))
    right = jnp.where(lane == CY - 1, sides, pltpu.roll(v, CY - 1, 1))
    return up, down, left, right


def harmonic(center, beside_it):
    return 2.0 * center * beside_it / (center + beside_it)


def base_planes(temp, cond, order, deposit, base, scales, shares, top, temp_halo, cond_halo):
    temp_above, temp_below, temp_sides = temp_halo
    cond_above, cond_below, cond_sides = cond_halo

    def plane(z, from_above):
        v, k = temp[z], cond[z]
        one = pl.ds(z, 1)
        vs = beside(v, temp_above[one, :], temp_below[one, :], temp_sides[z])
        ks = beside(k, cond_above[one, :], cond_below[one, :], cond_sides[z])
        later = jnp.minimum(z + 1, PZ - 1)
        shared = harmonic(k, cond[later])
        shares[0, z] = shared
        to_below = shared * (temp[later] - v)
        total = to_below - from_above
        for n, (v_next, k_next) in enumerate(zip(vs, ks)):
            shared = harmonic(k, k_next)
            if n == 0:
                top[one, :] = shared[:1]
            else:
                shares[n, z] = shared
            total = total + shared * (v_next - v)
        total = total + jnp.where(z == 0, deposit[...], 0.0)
        base[z] = v + heat_dt * (total / order[0, z] - order[1, z] * v)
        scales[z] = heat_dt / order[0, z]
        return to_below

    lax.fori_loop(0, PZ, plane, jnp.zeros((CX, CY), F32), unroll=8)


def second_planes(
    v, order, latent, deposit, shares, top, halo, far_row, far_flux, result, begin, end
):
    above, below, sides = halo
    row = iota((CX, CY), 0)

    def spread(line):
        return jnp.broadcast_to(line, (CX, CY))

    def plane(z, from_above):
        center = v[z]
        one = pl.ds(z, 1)
        vs = beside(center, above[one, :], below[one, :], sides[z])
        down = shares[1, z]
        up = jnp.where(row == 0, spread(top[one, :]), pltpu.roll(down, 1, 0))
        to_below = shares[0, z] * (v[jnp.minimum(z + 1, PZ - 1)] - center)
        total = to_below - from_above
        for shared, v_next in zip((up, down, shares[2, z], shares[3, z]), vs):
            total = total + shared * (v_next - center)
        total = total + jnp.where(row == far_row, spread(far_flux[one, :]), 0.0)
        source = latent[z] + jnp.where(z == 0, deposit[...], 0.0)
        result[z] = center + heat_dt * ((total + source) / order[0, z] - order[1, z] * center)
        return to_below

    if begin == 0:
        carry = jnp.zeros((CX, CY), F32)
    else:
        carry = shares[0, begin - 1] * (v[begin] - v[begin - 1])
    lax.fori_loop(begin, end, plane, carry, unroll=8)


def phase_planes(
    phi, sol, response, warmth, new_phi, new_sol, phi_halo, sol_halo, begin, end
):
    phi_above, phi_below, phi_sides = phi_halo
    sol_above, sol_below, sol_sides = sol_halo

    def spread(field, z, halo, weights):
        above, below, sides = halo
        f = field[z]
        one = pl.ds(z, 1)
        up, down, left, right = beside(f, above[one, :], below[one, :], sides[z])
        before = jnp.where(z > 0, field[jnp.maximum(z - 1, 0)], 0.0)
        after = jnp.where(z < PZ - 1, field[jnp.minimum(z + 1, PZ - 1)], 0.0)
        wz, wx, wy = weights
        total = (wz * ((before - f) + (after - f)) + wx * ((up - f) + (down - f))) + wy * (
            (left - f) + (right - f)
        )
        return f, total

    def plane(z, carry):
        p, spread_p = spread(phi, z, phi_halo, PHASE_WEIGHTS)
        s, spread_s = spread(sol, z, sol_halo, SOLUTE_WEIGHTS)
        drive = 0.45 * jnp.tanh(
            response[z] * (liquefying_threshold - warmth[z] - freezing_line_gradient * s)
        )
        p_new = p + phase_dt * (spread_p + 4.0 * p * (1.0 - p) * (p - 0.5 + drive))
        new_phi[z] = p_new
        new_sol[z] = s + phase_dt * spread_s - solute_reject * (p_new - p) * s
        return carry

    lax.fori_loop(begin, end, plane, 0, unroll=8)


def base_kernel(
    ids,
    deposit,
    owners,
    sources,
    near,
    side_a,
    side_b,
    heat,
    coeff,
    order,
    table,
    base,
    scales,
    shares,
    top,
    above_a,
    below_a,
    sides_a,
    above_b,
    below_b,
    sides_b,
):
    grp, slab = ids[0], ids[1]
    near_above = slab & 1 == 1

    @pl.when(grp == 0)
    def _():
        table[...] = plate_table(owners, sources, slab).astype(F32)
        for part, (above, below, side) in enumerate(
            ((above_a, below_a, sides_a), (above_b, below_b, sides_b))
        ):
            row = near[1 - (slab & 1), part]
            above[...] = jnp.where(near_above, row, 0.0)
            below[...] = jnp.where(near_above, 0.0, row)
            side[...] = receive_sides(ids, side_a, side_b, part).reshape(PZ, CX, CY)

        halo_a = (above_a, below_a, sides_a)
        halo_b = (above_b, below_b, sides_b)
        base_planes(
            heat, coeff, order, deposit, base, scales, shares, top, halo_a, halo_b
        )

    @pl.when(grp == 1)
    def _():
        table[:, :CY] = window_table(owners, slab).astype(F32)


def first_kernel(
    ids,
    inbox,
    table,
    base,
    scales,
    side_a,
    side_b,
    heat,
    coeff,
    order,
    joined,
    warmth,
    near_out,
    far_out,
    side_a_out,
    side_b_out,
):
    grp, parity = ids[0], ids[1] & 1
    far_top = parity == 0

    def arrived(pair):
        blocks = [(side, 2 * slot + pair) for side in (0, 1) for slot in (0, 1)]
        return jnp.concatenate([inbox[1 - grp, :, side, at, :] for side, at in blocks], axis=0)

    lane = iota((CY, CY), 1)

    @pl.when(grp == 0)
    def _():
        picks = table[...].astype(BF16)
        first = joined.at[1]
        for pair in (0, 1):
            units = pick_left(picks, arrived(pair), ((0,), (0,)))
            left, right = units[:CY], units[CY:]
            even = jnp.where(lane < HALF, left, pltpu.roll(right, HALF, 1))
            odd = jnp.where(lane < HALF, pltpu.roll(left, HALF, 1), right)
            for i, layer in ((2 * pair, even), (2 * pair + 1, odd)):
                layer = layer.reshape(PZ // ZQ, CX, CY)
                for q in range(PZ // ZQ):
                    z = ZQ * q + i
                    joined[0, z] = layer[q]
                    first[z] = base[z] + scales[z] * layer[q]
        near_out[0] = edge_row(first, jnp.logical_not(far_top))
        scale = edge_row(scales, far_top)
        for part, x in enumerate((heat, coeff, first)):
            far_out[part * PZ : (part + 1) * PZ] = edge_row(x, far_top)
        far_out[3 * PZ : 4 * PZ] = scale
        at = iota((PZ * CX, CY), 0) == iota((PZ * CX, CY), 1) * CX + jnp.where(far_top, 0, CX - 1)
        lines = lines_of(ids, side_a, side_b, 0) + lines_of(ids, side_a, side_b, 1)
        rows = iota((8, PZ * CX), 0)
        corners = jnp.zeros((8, PZ * CX), F32)
        for n, line in enumerate(lines):
            corners = jnp.where(rows == n, jnp.broadcast_to(line, corners.shape), corners)
        far_out[4 * PZ :] = pick_right(corners, ones_where(at))
        send_columns(ids, first[...].reshape(PZ * CX, CY), side_a_out, side_b_out, 0)
        send_columns(ids, scale, side_a_out, side_b_out, 1)

    @pl.when(grp == 1)
    def _():
        picks = table[:, :CY].astype(BF16)
        row = iota((CY, 2 * CY), 0)
        col = iota((CY, 2 * CY), 1)
        target = col & (CY - 1)
        parent = target >> 1
        next_to = jnp.clip(parent - 1 + 2 * (target & 1), 0, HALF - 1)
        at = row - (col >> 7) * HALF
        fine = (jnp.where(at == parent, 0.75, 0.0) + jnp.where(at == next_to, 0.25, 0.0)).astype(
            BF16
        )
        for pair in (0, 1):
            refined = pick_right(arrived(pair), fine)
            placed = pick_left(picks, refined, ((0,), (0,)))
            for i in (0, 1):
                layer = placed[:, i * CY : (i + 1) * CY].reshape(PZ // ZQ, CX, CY)
                for q in range(PZ // ZQ):
                    warmth[ZQ * q + 2 * pair + i] = layer[q]
        for part in (0, 1):
            far_out[part * PZ : (part + 1) * PZ] = edge_row(order.at[part], far_top)


def second_kernel(
    ids,
    deposit,
    near_k,
    side_a_k,
    side_b_k,
    near,
    far,
    side_a,
    side_b,
    far_sent,
    shares,
    top,
    coeff,
    order,
    joined,
    warmth,
    result_out,
    joined_out,
    above_a,
    below_a,
    sides_a,
    above_b,
    below_b,
    sides_b,
    result,
    both,
    far_flux,
    sems,
):
    grp, parity = ids[0], ids[1] & 1
    even = parity == 0
    parts = RESULT_PARTS
    size = PZ // parts
    halo_a = (above_a, below_a, sides_a)
    halo_b = (above_b, below_b, sides_b)

    def place(above, below, near_values, far_values):
        above[...] = jnp.where(even, far_values, near_values)
        below[...] = jnp.where(even, near_values, far_values)

    def write(source, target, n):
        copy = pltpu.make_async_copy(source, target, sems.at[n])
        copy.start()
        return copy

    @pl.when(grp == 0)
    def _():
        copies = [write(joined.at[0], joined_out.at[0, 0], 0)]
        t_far, k_far, partial, scale_far = [far[n * PZ : (n + 1) * PZ] for n in range(4)]
        t_here, k_here = far_sent[:PZ], far_sent[PZ : 2 * PZ]
        scale = far_sent[3 * PZ : 4 * PZ]
        shared_far = harmonic(k_here, k_far)
        crossing = shared_far * (t_far - t_here)
        first = both.at[0]
        first[...] = joined[1]
        for at_top, row in ((True, 0), (False, CX - 1)):
            add = jnp.where(even == at_top, scale * crossing, 0.0)
            first[:, row, :] = first[:, row, :] + add
        copies.append(write(first, joined_out.at[0, 1], 1))
        far_first = partial - scale_far * crossing
        far_flux[...] = shared_far * (far_first - edge_row(first, even))
        place(above_a, below_a, near[1 - parity, 0], far_first)
        sides_a[...] = receive_sides(ids, side_a, side_b, 0).reshape(PZ, CX, CY)
        row = jnp.where(even, 0, CX - 1)
        lane = iota((PZ, CY), 1)
        add = jnp.zeros((PZ, CY), F32)
        temps, conds = lines_of(ids, side_a_k, side_b_k, 0), lines_of(ids, side_a_k, side_b_k, 1)
        scales = lines_of(ids, side_a, side_b, 1)
        for n, end in enumerate((0, CY - 1)):
            t, k = down(temps[n], row, CX), down(conds[n], row, CX)
            corner = 4 * PZ + n
            t_next, k_next = down(far[corner : corner + 1]), down(far[corner + 2 : corner + 3])
            shared = 2.0 * k * k_next / jnp.maximum(k + k_next, 1e-6)
            change = down(scales[n][:, :CY]) * shared * (t_next - t)
            add = add + jnp.where(lane == end, change, 0.0)
        for at_top, edge in ((True, 0), (False, CX - 1)):
            sides_a[:, edge, :] = sides_a[:, edge, :] + jnp.where(even == at_top, add, 0.0)
        for n in range(parts):
            begin, end = n * size, (n + 1) * size
            second_planes(
                first,
                order,
                joined.at[0],
                deposit,
                shares,
                top,
                halo_a,
                row,
                far_flux,
                result,
                begin,
                end,
            )
            planes = pl.ds(begin, size)
            copies.append(write(result.at[planes], result_out.at[0, planes], 2 + n))
        for copy in copies:
            copy.wait()

    @pl.when(grp == 1)
    def _():
        copies = [write(warmth, result_out.at[0], 0)]
        for part, (above, below, side) in enumerate((halo_a, halo_b)):
            far_values = far[part * PZ : (part + 1) * PZ]
            place(above, below, near_k[1 - parity, part], far_values)
            side[...] = receive_sides(ids, side_a_k, side_b_k, part).reshape(PZ, CX, CY)
        for n in range(parts):
            begin, end = n * size, (n + 1) * size
            phase_planes(
                order.at[0],
                order.at[1],
                coeff,
                warmth,
                both.at[0],
                both.at[1],
                halo_a,
                halo_b,
                begin,
                end,
            )
            planes = pl.ds(begin, size)
            copies.append(write(both.at[:, planes], joined_out.at[0, :, planes], 2 + n))
        for copy in copies:
            copy.wait()


RESULT_PARTS = 4
HBM = pl.BlockSpec(memory_space=pltpu.HBM)
SMEM = pl.BlockSpec(memory_space=pltpu.SMEM)
VMEM = pl.BlockSpec(memory_space=pltpu.VMEM)


def located(kernel, slabs, cols):
    def body(number, *refs):
        n = number[0]
        ids = lax.div(n, slabs * cols), lax.rem(lax.div(n, cols), slabs), lax.rem(n, cols)
        kernel(ids, *refs)

    return body


def call(kernel, specs, outs, scratch=(), out_space=VMEM, limit=24 << 20):
    shapes = [jax.ShapeDtypeStruct(shape, F32) for shape in outs]
    single = len(shapes) == 1
    return pl.pallas_call(
        kernel,
        out_shape=shapes[0] if single else shapes,
        in_specs=list(specs),
        out_specs=out_space if single else [out_space] * len(shapes),
        scratch_shapes=list(scratch),
        compiler_params=pltpu.CompilerParams(vmem_limit_bytes=limit),
    )


def halo_scratch():
    one = [
        pltpu.VMEM((PZ, CY), F32),
        pltpu.VMEM((PZ, CY), F32),
        pltpu.VMEM((PZ, CX, CY), F32),
    ]
    return one + one


def swaps(starts):
    return [pair for i in starts for pair in ((i, i + 1), (i + 1, i))]


def per_device(heat_field, coeff, order, block_owner, block_source, laser_cells):
    slabs, cols = lax.axis_size("slab"), lax.axis_size("col")
    chips = slabs // 2
    grp = lax.axis_index("grp")
    number = lax.axis_index(("grp", "slab", "col")).reshape(1)

    def place(kernel, *specs, **options):
        return call(located(kernel, slabs, cols), *specs, **options)

    near_pairs = [[2 * i, 2 * i + 1] for i in range(chips)]
    far_swap = swaps(range(1, slabs - 1, 2))
    side_a_swap, side_b_swap = swaps(range(0, cols - 1, 2)), swaps(range(1, cols - 1, 2))
    heat, conduct, orders = heat_field[0], coeff[0], order[0]
    owners, sources, laser = block_owner[0, :, :, 0], block_source[0], laser_cells[0]

    slab_table = pltpu.VMEM(owners.shape, jnp.int32)
    outbox, deposit = place(
        pack_kernel,
        [SMEM] + [HBM] * 4,
        [(2, chips, 2, 4, CY), (CX, CY)],
        [
            slab_table,
            slab_table,
            pltpu.VMEM((PZ // ZQ, ZQ, CX, CY), F32),
            pltpu.VMEM(laser.shape, jnp.int32),
            pltpu.SemaphoreType.DMA((4,)),
        ],
        limit=60 << 20,
    )(number, owners, sources, heat.reshape(PZ // ZQ, ZQ, CX, CY), laser)
    inbox = lax.all_to_all(
        outbox.reshape(-1, 4, CY), ("grp", "slab"), split_axis=0, concat_axis=0, tiled=True
    ).reshape(outbox.shape)
    rows, column, field = (2, PZ, CY), (2, PZ * CX), (PZ, CX, CY)
    near, side_a, side_b = place(edges_kernel, [SMEM] + [VMEM] * 3, [rows, column, column])(
        number, heat, conduct, orders
    )
    side_a = lax.ppermute(side_a, "col", side_a_swap)
    side_b = lax.ppermute(side_b, "col", side_b_swap)
    near = lax.all_gather(near, "slab", axis_index_groups=near_pairs)
    table, base, scales, shares, top = place(
        base_kernel,
        [SMEM] + [VMEM] * 9,
        [(2 * slabs, 256), field, field, (4,) + field, (PZ, CY)],
        halo_scratch(),
    )(number, deposit, owners, sources, near, side_a, side_b, heat, conduct, orders)
    joined, warmth, near_1, far_1, side_a_1, side_b_1 = place(
        first_kernel,
        [SMEM] + [VMEM] * 9,
        [(2,) + field, field, (1, PZ, CY), (4 * PZ + 8, CY), column, column],
    )(number, inbox, table, base, scales, side_a, side_b, heat, conduct, orders)
    far_sent = far_1
    far_1 = lax.ppermute(far_1, "slab", far_swap)
    side_a_1 = lax.ppermute(side_a_1, "col", side_a_swap)
    side_b_1 = lax.ppermute(side_b_1, "col", side_b_swap)
    near_1 = lax.all_gather(near_1, "slab", axis_index_groups=near_pairs)
    return place(
        second_kernel,
        [SMEM] + [VMEM] * 15,
        [(1,) + field, (1, 2) + field],
        halo_scratch()
        + [
            pltpu.VMEM(field, F32),
            pltpu.VMEM((2,) + field, F32),
            pltpu.VMEM((PZ, CY), F32),
            pltpu.SemaphoreType.DMA((2 + RESULT_PARTS,)),
        ],
        HBM,
    )(
        number,
        deposit,
        near,
        side_a,
        side_b,
        near_1,
        far_1,
        side_a_1,
        side_b_1,
        far_sent,
        shares,
        top,
        conduct,
        orders,
        joined,
        warmth,
    )


def solution(mesh):
    placed = (
        P("grp", None, "slab", "col"),
        P("grp", None, "slab", "col"),
        P("grp", None, None, "slab", "col"),
        P("col", None, None, None),
        P("col", None, None),
        P("slab", "col", None),
    )
    return jax.shard_map(
        per_device,
        mesh=mesh,
        in_specs=placed,
        out_specs=(P("grp", None, "slab", "col"), P("grp", None, None, "slab", "col")),
        check_vma=False,
    )
```
